32 devices in a mesh: dp: 4 (over x, core), ctx: 8 (over z, y).
Axes of the slice: x: 2, y: 2, z: 4, core: 2. Of those that a mesh axis runs over, the one named last changes fastest.
Arguments:
- tokens: bfloat16 [8, 512, 2048], P('dp', 'ctx'), may hold values from -43 to 43
- cotangent: bfloat16 [8, 512, 2048], P('dp', 'ctx'), may hold values from -6 to 6
- attn_gain: bfloat16 [2048], P(('dp', 'ctx')), may hold values from 0.5 to 1.5
- query_weight: bfloat16 [2048, 2048], P(('dp', 'ctx')), may hold values from -0.1875 to 0.1875
- key_weight: bfloat16 [2048, 256], P(('dp', 'ctx')), may hold values from -0.1875 to 0.1875
- value_weight: bfloat16 [2048, 256], P(('dp', 'ctx')), may hold values from -0.125 to 0.125
- output_weight: bfloat16 [2048, 2048], P(('dp', 'ctx')), may hold values from -0.75 to 0.75
- mlp_gain: bfloat16 [2048], P(('dp', 'ctx')), may hold values from 0.5 to 1.5
- gate_weight: bfloat16 [2048, 5632], P(('dp', 'ctx')), may hold values from -0.125 to 0.125
- up_weight: bfloat16 [2048, 5632], P(('dp', 'ctx')), may hold values from -0.125 to 0.125
- down_weight: bfloat16 [5632, 2048], P(None, ('dp', 'ctx')), may hold values from -0.078125 to 0.078125
Outputs:
- block_out: bfloat16 [8, 512, 2048], P('dp', 'ctx')
- tokens_grad: float32 [8, 512, 2048], P('dp', 'ctx')
- attn_gain_grad: float32 [2048], P(('dp', 'ctx'))
- query_grad: float32 [2048, 2048], P(('dp', 'ctx'))
- key_grad: float32 [2048, 256], P(('dp', 'ctx'))
- value_grad: float32 [2048, 256], P(('dp', 'ctx'))
- output_grad: float32 [2048, 2048], P(('dp', 'ctx'))
- mlp_gain_grad: float32 [2048], P(('dp', 'ctx'))
- gate_grad: float32 [2048, 5632], P(('dp', 'ctx'))
- up_grad: float32 [2048, 5632], P(('dp', 'ctx'))
- down_grad: float32 [5632, 2048], P(None, ('dp', 'ctx'))
The draws below stay inside these ranges and needn't reach their ends.
All inputs are finite; a program needn't handle non-finite values.
Results may differ from the reference program's by a relative error of at most 0.023.
Values may be sent and summed in bfloat16 or wider, within the bound.
No kernel may reach another device: no remote copies, remote signals or barrier semaphores. Data moves between devices by JAX's collectives and lax.ppermute only.
A program may use at most 384 MiB of HBM per device.

```python
import math
import jax
import jax.numpy as jnp
from jax import lax

D = 2048
FF = 5632
HEADS = 32
KV_HEADS = 4
HEAD_DIM = 64
LENGTH = 512
BATCH = 8


def draw_tokens(key, part):
    split_keys = jax.random.split(key, 3)
    row_scale = jnp.exp(jax.random.uniform(split_keys[1], (BATCH, LENGTH, 1), jnp.float32, math.log(0.25), math.log(2.5)))
    col_scale = jnp.exp(jax.random.uniform(split_keys[2], (D,), jnp.float32, math.log(0.35), math.log(3.5)))
    base_values = jnp.clip(jax.random.normal(split_keys[0], (BATCH, LENGTH, D), jnp.float32), -4.0, 4.0)
    return (base_values * row_scale * col_scale).astype(jnp.bfloat16)


def steps_of(rng, extent, shards, low, top_value):
    def one(dim, parts):
        steps = jax.random.uniform(jax.random.fold_in(jax.random.fold_in(rng, 6), dim), (parts,), jnp.float32, low / len(shards), top_value / len(shards))
        return jnp.repeat(jnp.exp(steps), extent[dim] // parts).reshape((-1,) + (1,) * (len(extent) - dim - 1))

    gain = one(*shards[0])
    for cut in shards[1:]:
        gain = gain * one(*cut)
    return gain


def gaussian(own_key, shape, deviation, reach, cuts=(), kind=jnp.bfloat16):
    array = deviation * jax.random.normal(own_key, shape, jnp.float32)
    if cuts:
        array = array * steps_of(own_key, shape, cuts, -0.22, 0.18)
    return jnp.clip(array, -reach, reach).astype(kind)


def setup_inputs(seed: int = 0) -> dict:
    splits = jax.random.split(jax.random.key(seed), 12)
    return {
        "tokens": draw_tokens(jax.random.fold_in(splits[11], 71), 0),
        "cotangent": gaussian(splits[1], (BATCH, LENGTH, D), 1.0, 6.0, ((0, 4), (1, 8))),
        "attn_gain": jnp.clip(1.0 + 0.1 * jax.random.normal(splits[2], (D,), jnp.float32), 0.5, 1.5).astype(jnp.bfloat16),
        "query_weight": gaussian(splits[3], (D, HEADS * HEAD_DIM), (D // 2) ** -0.5, 0.1875, ((0, 32),)),
        "key_weight": gaussian(splits[4], (D, KV_HEADS * HEAD_DIM), (D // 2) ** -0.5, 0.1875, ((0, 32),)),
        "value_weight": gaussian(splits[5], (D, KV_HEADS * HEAD_DIM), D ** -0.5, 0.125, ((0, 32),)),
        "output_weight": gaussian(splits[6], (HEADS * HEAD_DIM, D), HEAD_DIM ** -0.5, 0.75, ((0, 32),)),
        "mlp_gain": jnp.clip(1.0 + 0.1 * jax.random.normal(splits[7], (D,), jnp.float32), 0.5, 1.5).astype(jnp.bfloat16),
        "gate_weight": gaussian(splits[8], (D, FF), D ** -0.5, 0.125, ((0, 32),)),
        "up_weight": gaussian(splits[9], (D, FF), D ** -0.5, 0.125, ((0, 32),)),
        "down_weight": gaussian(splits[10], (FF, D), FF ** -0.5, 0.078125, ((1, 32),)),
    }


norm_eps = 1e-05
rope_base = 10000.0

@jax.custom_vjp
def low(v):
    return lax.optimization_barrier(v.astype(jnp.bfloat16)).astype(jnp.float32)

@jax.custom_vjp
def low_back(v):
    return v

def low_keep(v):
    return (low(v), None)

def low_pass(kept, grad):
    return (grad,)

def back_keep(v):
    return (v, None)

def back_low(kept, grad):
    return (low(grad),)
low.defvjp(low_keep, low_pass)
low_back.defvjp(back_keep, back_low)

def matmul(left, right):
    return jnp.dot(left, right, precision=lax.Precision.HIGHEST, preferred_element_type=jnp.float32)

def rope_tables(positions):
    half = HEAD_DIM // 2
    freqs = rope_base ** (-(jnp.arange(half, dtype=jnp.float32) * 2.0) / HEAD_DIM)
    angles = positions.astype(jnp.float32)[:, None] * freqs[None, :]
    cosine = jnp.cos(angles)
    sine = jnp.sin(angles)
    return (jnp.concatenate([cosine, cosine], -1), jnp.concatenate([sine, sine], -1))

def rotate(values, cosine, sine):
    half = values.shape[-1] // 2
    turned = jnp.concatenate([-values[..., half:], values[..., :half]], -1)
    return values * cosine[:, None, :] + turned * sine[:, None, :]

def layer(stream, attn_gain, query_weight, key_weight, value_weight, output_weight, mlp_gain, gate_weight, up_weight, down_weight):
    length = stream.shape[0]
    groups = HEADS // KV_HEADS
    factor = 1.0 / math.sqrt(HEAD_DIM)
    inverse_one = lax.rsqrt(lax.optimization_barrier(jnp.mean(stream * stream, -1, keepdims=True)) + norm_eps)
    inputs_one = low(stream * inverse_one * attn_gain)
    queries = low_back(matmul(inputs_one, query_weight))
    keys_raw = low_back(matmul(inputs_one, key_weight))
    values = low(low_back(matmul(inputs_one, value_weight)))
    cosine, sine = rope_tables(jnp.arange(length))
    queries = low(rotate(queries.reshape(length, HEADS, HEAD_DIM), cosine, sine))
    keys_all = low(rotate(keys_raw.reshape(length, KV_HEADS, HEAD_DIM), cosine, sine))
    values = values.reshape(length, KV_HEADS, HEAD_DIM)
    block = math.gcd(length, 512)
    grouped = queries.reshape(length // block, block, KV_HEADS, groups, HEAD_DIM)
    starts = jnp.arange(length // block) * block
    key_positions = jnp.arange(length)

    def attend(block_items):
        query_block, first = block_items
        scores = jnp.einsum('bgjd,lgd->gjbl', query_block, keys_all, precision=lax.Precision.HIGHEST) * factor
        scores = low_back(scores)
        visible = (first + jnp.arange(block))[:, None] >= key_positions[None, :]
        weights = jnp.where(visible, jnp.exp(scores), 0.0)
        totals = lax.optimization_barrier(jnp.sum(weights, -1))
        mixed = low_back(jnp.einsum('gjbl,lgd->bgjd', low(weights), values, precision=lax.Precision.HIGHEST))
        return mixed / jnp.transpose(totals, (2, 0, 1))[..., None]
    attended = lax.map(jax.checkpoint(attend), (grouped, starts))
    heads_low = low(attended.reshape(length, HEADS * HEAD_DIM))
    middle = stream + low_back(matmul(heads_low, output_weight))
    inverse_two = lax.rsqrt(lax.optimization_barrier(jnp.mean(middle * middle, -1, keepdims=True)) + norm_eps)
    inputs_two = low(middle * inverse_two * mlp_gain)
    gate_values = low_back(matmul(inputs_two, gate_weight))
    up_values = low_back(matmul(inputs_two, up_weight))
    hidden_low = low(jax.nn.silu(gate_values) * up_values)
    return middle + low_back(matmul(hidden_low, down_weight))

def reference(tokens, cotangent, attn_gain, query_weight, key_weight, value_weight, output_weight, mlp_gain, gate_weight, up_weight, down_weight):
    weight_list = tuple((weight.astype(jnp.float32) for weight in (attn_gain, query_weight, key_weight, value_weight, output_weight, mlp_gain, gate_weight, up_weight, down_weight)))

    def sequence_step(carried, pair_items):
        sequence, tangent = pair_items
        result, pullback = jax.vjp(layer, sequence, *weight_list)
        grads = pullback(tangent)
        summed = tuple((total + grad for total, grad in zip(carried, grads[1:])))
        return (summed, (result.astype(jnp.bfloat16), grads[0]))
    initial = tuple((jnp.zeros_like(weight) for weight in weight_list))
    totals, (outputs, input_grads) = lax.scan(sequence_step, initial, (tokens.astype(jnp.float32), cotangent.astype(jnp.float32)))
    return (outputs, input_grads, totals[0], totals[1], totals[2], totals[3], totals[4], totals[5], totals[6], totals[7], totals[8])
```

```python
import math

import jax
import jax.numpy as jnp
from jax import lax
from jax.sharding import PartitionSpec as P

HEADS = 32
KV_HEADS = 4
HEAD_DIM = 64
GROUPS = HEADS // KV_HEADS

norm_eps = 1e-05
rope_base = 10000.0

BF = jnp.bfloat16
F32 = jnp.float32


def dot(left, right):
    return jnp.dot(left, right, preferred_element_type=F32)


def dot_nt(left, right):
    return lax.dot_general(left, right, (((1,), (1,)), ((), ())), preferred_element_type=F32)


def dot_tn(left, right):
    return lax.dot_general(left, right, (((0,), (0,)), ((), ())), preferred_element_type=F32)


class Bit:
    def __init__(self, axis, bit, size):
        self.axis, self.bit = axis, bit
        self.pairs = [(i, i ^ (1 << bit)) for i in range(size)]

    def mine(self):
        return (lax.axis_index(self.axis) >> self.bit) & 1

    def swap(self, value):
        return lax.ppermute(value, self.axis, self.pairs)


def rope_tables(positions):
    half = HEAD_DIM // 2
    freqs = rope_base ** (-(jnp.arange(half, dtype=F32) * 2.0) / HEAD_DIM)
    angles = positions.astype(F32)[:, None] * freqs[None, :]
    cosine = jnp.cos(angles)
    sine = jnp.sin(angles)
    return (jnp.concatenate([cosine, cosine], -1), jnp.concatenate([sine, sine], -1))


def turn(values):
    half = values.shape[-1] // 2
    return jnp.concatenate([-values[..., half:], values[..., :half]], -1)


def rotate(values, cosine, sine):
    return values * cosine[:, None, :] + turn(values) * sine[:, None, :]


def rotate_back(grads, cosine, sine):
    return grads * cosine[:, None, :] - turn(grads * sine[:, None, :])


def norm_back(grad_normed, normed, inverse, gain):
    scaled = grad_normed * gain
    return inverse * (scaled - normed * jnp.mean(scaled * normed, -1, keepdims=True))


def gather_bits(value, bits):
    acc = value[None]
    for bit in bits:
        acc = jnp.concatenate([acc, bit.swap(acc)], 0)
    return acc


def reduce_bits(blocks, bits):
    acc = blocks
    for bit in reversed(bits):
        half = acc.shape[0] // 2
        got = bit.swap(acc[half:].astype(BF))
        acc = acc[:half].astype(F32) + got.astype(F32)
    return acc[0]


def trade(value, dim, bit):
    mine = bit.mine()
    got = bit.swap(lax.dynamic_index_in_dim(value, 1 - mine, dim, True))
    keep = lax.dynamic_index_in_dim(value, mine, dim, True)
    low = jnp.where(mine == 0, keep, got)
    high = jnp.where(mine == 0, got, keep)
    return jnp.concatenate([low, high], dim)


def absolute(blocks, index, bits):
    def one(j):
        other = index ^ j
        slot = sum(((other >> b.bit) & 1) << i for i, b in enumerate(bits))
        return lax.dynamic_index_in_dim(blocks, slot, 0, False)

    return [one(j) for j in range(blocks.shape[0])]


def relative(blocks, index, bits):
    def one(r):
        code = sum(((r >> i) & 1) << b.bit for i, b in enumerate(bits))
        return lax.dynamic_index_in_dim(blocks, index ^ code, 0, False)

    return jnp.stack([one(r) for r in range(blocks.shape[0])])


def shards(
    dp,
    ctx,
    tokens,
    cotangent,
    attn_gain,
    query_weight,
    key_weight,
    value_weight,
    output_weight,
    mlp_gain,
    gate_weight,
    up_weight,
    down_weight,
):
    seqs, seq_dev, width = tokens.shape
    rows = seqs * seq_dev
    depth = query_weight.shape[0]
    ff = gate_weight.shape[1]
    factor = 1.0 / math.sqrt(HEAD_DIM)
    head_cols = GROUPS * HEAD_DIM

    bit_x, bit_core = Bit("dp", 1, dp), Bit("dp", 0, dp)
    ctx_bits = [Bit("ctx", b, ctx) for b in reversed(range(ctx.bit_length() - 1))]
    near = ctx_bits[-2]
    far = [b for b in ctx_bits if b is not near]
    team = [bit_x, near, bit_core]
    dp_bits = [bit_x, bit_core]
    d_index = lax.axis_index("dp")
    c_index = lax.axis_index("ctx")

    levels = len(ctx_bits)
    split_shape = (2, 2) + (2,) * levels + (depth,)
    near_dim = 2 + levels - 2
    far_dims = [2 + k for k in range(levels) if ctx_bits[k] is not near]
    order = far_dims + [0, near_dim, 1, 2 + levels]
    back_order = [order.index(k) for k in range(len(order))]
    pieces = 1 << len(far)
    piece = width // pieces

    def to_pieces(array):
        count = array.shape[0]
        out = array.reshape((count,) + split_shape)
        for k, bit in zip(far_dims, far):
            out = jnp.where(bit.mine() == 1, jnp.flip(out, k + 1), out)
        return out.transpose([0] + [k + 1 for k in order]).reshape(count, width)

    def from_pieces(array):
        count = array.shape[0]
        out = array.reshape([count] + [split_shape[k] for k in order])
        out = out.transpose([0] + [k + 1 for k in back_order])
        for k, bit in zip(far_dims, far):
            out = jnp.where(bit.mine() == 1, jnp.flip(out, k + 1), out)
        return out.reshape(count, width)

    gains = jnp.stack([attn_gain, mlp_gain])
    gains = jnp.stack(absolute(gather_bits(gains, dp_bits), d_index, dp_bits))
    gains = jnp.stack(absolute(gather_bits(gains, ctx_bits), c_index, ctx_bits))
    gains = gains.transpose(2, 1, 0, 3).reshape(2, width).astype(F32)
    gain_one, gain_two = gains[0], gains[1]

    own_qkv = jnp.concatenate(
        [
            query_weight.reshape(depth, dp, head_cols),
            key_weight.reshape(depth, dp, HEAD_DIM),
            value_weight.reshape(depth, dp, HEAD_DIM),
        ],
        -1,
    ).transpose(1, 0, 2)
    qkv_cols = own_qkv.shape[-1]
    own_qkv = own_qkv.reshape(2, 2, depth, qkv_cols)
    own_qkv = trade(trade(own_qkv, 0, bit_x), 1, bit_core).reshape(dp, depth, qkv_cols)
    qkv_rel = gather_bits(own_qkv, ctx_bits)
    qkv = jnp.stack(absolute(qkv_rel, c_index, ctx_bits), 1).reshape(width, qkv_cols)
    out_rel = gather_bits(output_weight, ctx_bits)
    out_full = jnp.concatenate(absolute(out_rel, c_index, ctx_bits), 0)

    def mlp_slices(weight):
        own = weight.reshape(depth, 2, 2, 2, ff // 8).transpose(1, 2, 3, 0, 4)
        own = trade(own, 2, bit_core)
        own = trade(own, 0, bit_x)
        own = trade(own, 1, near)
        own = own.reshape(piece, ff // 8)
        parts = [own]
        for bit in far:
            parts = parts + [bit.swap(p) for p in parts]
        return parts

    gate_parts = mlp_slices(gate_weight)
    up_parts = mlp_slices(up_weight)
    down_parts = mlp_slices(down_weight.T)
    digit = [sum(((k >> i) & 1) << (len(far) - 1 - i) for i in range(len(far))) for k in range(pieces)]

    def part_cols(array, k):
        return array[:, digit[k] * piece : (digit[k] + 1) * piece]

    positions = c_index * seq_dev + jnp.arange(seq_dev, dtype=jnp.int32)
    cosine, sine = rope_tables(positions)
    stream = tokens.astype(F32).reshape(rows, width)
    inverse_one = lax.rsqrt(jnp.mean(stream * stream, -1, keepdims=True) + norm_eps)
    normed_one = stream * inverse_one
    inputs_one = (normed_one * gain_one).astype(BF)
    a1 = gather_bits(inputs_one, dp_bits).reshape(dp * rows, width)
    all_seqs = dp * seqs
    raw = dot(a1, qkv)
    queries = rotate(
        raw[:, :head_cols].reshape(all_seqs, seq_dev, GROUPS, HEAD_DIM), cosine, sine
    ).astype(BF)
    keys_own = rotate(
        raw[:, head_cols : head_cols + HEAD_DIM].reshape(all_seqs, seq_dev, 1, HEAD_DIM), cosine, sine
    ).astype(BF)
    values_own = raw[:, head_cols + HEAD_DIM :].astype(BF).reshape(all_seqs, seq_dev, HEAD_DIM)
    kv_own = jnp.concatenate([keys_own[:, :, 0, :], values_own], -1)
    kv = gather_bits(kv_own, ctx_bits)
    rel = jnp.arange(ctx, dtype=jnp.int32)
    rel_abs = sum(((rel >> i) & 1) << b.bit for i, b in enumerate(ctx_bits)) ^ c_index
    key_positions = (rel_abs[:, None] * seq_dev + jnp.arange(seq_dev, dtype=jnp.int32)[None]).reshape(-1)
    kv = kv.transpose(1, 0, 2, 3).reshape(all_seqs, ctx * seq_dev, 2 * HEAD_DIM)
    keys, values = kv[..., :HEAD_DIM], kv[..., HEAD_DIM:]
    scores = jnp.einsum("sqjd,skd->sjqk", queries, keys, preferred_element_type=F32) * factor
    visible = positions[:, None] >= key_positions[None, :]
    weights = jnp.where(visible, jnp.exp(scores), 0.0)
    weights_low = weights.astype(BF)
    totals = jnp.sum(weights, -1)
    mixed = jnp.einsum("sjqk,skd->sjqd", weights_low, values, preferred_element_type=F32)
    attended = mixed / totals[..., None]
    heads_low = attended.transpose(0, 2, 1, 3).reshape(dp * rows, head_cols).astype(BF)
    branch = dot(heads_low, out_full)
    middle = stream + reduce_bits(branch.reshape(dp, rows, width), dp_bits)

    inverse_two = lax.rsqrt(jnp.mean(middle * middle, -1, keepdims=True) + norm_eps)
    normed_two = middle * inverse_two
    inputs_two = to_pieces((normed_two * gain_two).astype(BF))
    grad_low = to_pieces(cotangent.reshape(rows, width))
    crowd = 8 * rows
    a2 = gather_bits(inputs_two, team).reshape(crowd, width)
    gb = gather_bits(grad_low, team).reshape(crowd, width)

    def through(array, parts):
        total = None
        for k in range(pieces):
            term = dot(part_cols(array, k), parts[k])
            total = term if total is None else total + term
        return total

    gate_values = through(a2, gate_parts)
    up_values = through(a2, up_parts)
    sigmoid_gate = jax.nn.sigmoid(gate_values)
    activated = gate_values * sigmoid_gate
    hidden = (activated * up_values).astype(BF)
    by_digit = sorted(range(pieces), key=lambda k: digit[k])
    down_out = jnp.concatenate([dot_nt(hidden, down_parts[k]) for k in by_digit], -1)
    result = middle + from_pieces(reduce_bits(down_out.reshape(8, rows, width), team))

    grad_hidden = through(gb, down_parts)
    grad_gate = (
        grad_hidden * up_values * sigmoid_gate * (1.0 + gate_values * (1.0 - sigmoid_gate))
    ).astype(BF)
    grad_up = (grad_hidden * activated).astype(BF)
    grad_a2 = jnp.concatenate(
        [dot_nt(grad_gate, gate_parts[k]) + dot_nt(grad_up, up_parts[k]) for k in by_digit], -1
    )
    grad_inputs_two = from_pieces(reduce_bits(grad_a2.reshape(8, rows, width), team))

    def mlp_return(left, right):
        terms = [dot_tn(part_cols(left, k), right) for k in range(pieces)]
        for bit in reversed(far):
            half = len(terms) // 2
            got = [bit.swap(t.astype(BF)) for t in terms[half:]]
            terms = [t + g.astype(F32) for t, g in zip(terms[:half], got)]
        own = terms[0].astype(BF).reshape(2, 2, 2, depth, ff // 8)
        own = trade(own, 1, near)
        own = trade(own, 0, bit_x)
        own = trade(own, 2, bit_core)
        return own.transpose(3, 0, 1, 2, 4).reshape(depth, ff).astype(F32)

    gate_grad = mlp_return(a2, grad_gate)
    up_grad = mlp_return(a2, grad_up)
    down_grad = mlp_return(gb, hidden).T

    grad_out = cotangent.astype(F32).reshape(rows, width)
    gain_two_total = jnp.sum(grad_inputs_two * normed_two, 0)
    grad_middle = grad_out + norm_back(grad_inputs_two, normed_two, inverse_two, gain_two)

    grad_branch = gather_bits(grad_middle.astype(BF), dp_bits).reshape(dp * rows, width)
    output_total = dot_tn(heads_low, grad_branch)
    grad_heads = dot_nt(grad_branch, out_full)
    grad_attended = grad_heads.reshape(all_seqs, seq_dev, GROUPS, HEAD_DIM).transpose(0, 2, 1, 3)
    deltas = jnp.sum(grad_attended * attended, -1) / totals
    grad_mixed = (grad_attended / totals[..., None]).astype(BF)
    through_values = jnp.einsum("sjqd,skd->sjqk", grad_mixed, values, preferred_element_type=F32)
    grad_scores = (weights * (through_values - deltas[..., None])).astype(BF)
    grad_queries = jnp.einsum("sjqk,skd->sqjd", grad_scores, keys, preferred_element_type=F32) * factor
    grad_keys = jnp.einsum("sjqk,sqjd->skd", grad_scores, queries, preferred_element_type=F32) * factor
    grad_values = jnp.einsum("sjqk,sjqd->skd", weights_low, grad_mixed, preferred_element_type=F32)
    grad_kv = jnp.concatenate([grad_keys, grad_values], -1)
    grad_kv = grad_kv.reshape(all_seqs, ctx, seq_dev, 2 * HEAD_DIM).transpose(1, 0, 2, 3)
    grad_kv = reduce_bits(grad_kv, ctx_bits)
    grad_query_low = rotate_back(grad_queries, cosine, sine).astype(BF).reshape(dp * rows, head_cols)
    grad_key_low = rotate_back(grad_kv[:, :, None, :HEAD_DIM], cosine, sine).astype(BF)
    grad_key_low = grad_key_low.reshape(dp * rows, HEAD_DIM)
    grad_value_low = grad_kv[..., HEAD_DIM:].astype(BF).reshape(dp * rows, HEAD_DIM)
    grad_raw = jnp.concatenate([grad_query_low, grad_key_low, grad_value_low], -1)
    qkv_total = dot_tn(a1, grad_raw)
    grad_a1 = dot_nt(grad_raw, qkv)
    grad_inputs_one = reduce_bits(grad_a1.reshape(dp, rows, width), dp_bits)
    gain_one_total = jnp.sum(grad_inputs_one * normed_one, 0)
    grad_tokens = grad_middle + norm_back(grad_inputs_one, normed_one, inverse_one, gain_one)

    qkv_blocks = qkv_total.reshape(dp, ctx, depth, qkv_cols).transpose(1, 0, 2, 3)
    qkv_own = reduce_bits(relative(qkv_blocks, c_index, ctx_bits), ctx_bits).astype(BF).reshape(2, 2, depth, qkv_cols)
    qkv_own = trade(trade(qkv_own, 1, bit_core), 0, bit_x).reshape(dp, depth, qkv_cols).astype(F32)
    query_grad = qkv_own[..., :head_cols].transpose(1, 0, 2).reshape(depth, dp * head_cols)
    key_grad = qkv_own[..., head_cols : head_cols + HEAD_DIM].transpose(1, 0, 2).reshape(depth, dp * HEAD_DIM)
    value_grad = qkv_own[..., head_cols + HEAD_DIM :].transpose(1, 0, 2).reshape(depth, dp * HEAD_DIM)
    out_blocks = output_total.reshape(ctx, depth, width)
    output_grad = reduce_bits(relative(out_blocks, c_index, ctx_bits), ctx_bits)

    gain_totals = lax.psum_scatter(
        jnp.stack([gain_one_total, gain_two_total]), ("dp", "ctx"), scatter_dimension=1, tiled=True
    )
    return (
        result.astype(BF).reshape(seqs, seq_dev, width),
        grad_tokens.reshape(seqs, seq_dev, width),
        gain_totals[0],
        query_grad,
        key_grad,
        value_grad,
        output_grad,
        gain_totals[1],
        gate_grad,
        up_grad,
        down_grad,
    )


def solution(mesh):
    dp, ctx = mesh.shape["dp"], mesh.shape["ctx"]

    def local(*args):
        return shards(dp, ctx, *args)

    weight = P(("dp", "ctx"), None)
    flat = P(("dp", "ctx"))
    acts = P("dp", "ctx", None)
    down = P(None, ("dp", "ctx"))
    return jax.shard_map(
        local,
        mesh=mesh,
        in_specs=(acts, acts, flat, weight, weight, weight, weight, flat, weight, weight, down),
        out_specs=(acts, acts, flat, weight, weight, weight, weight, flat, weight, weight, down),
        check_vma=False,
    )
```

```python
import functools
import math

import jax
import jax.numpy as jnp
from jax import lax
from jax.experimental import pallas as pl
from jax.experimental.pallas import tpu as pltpu
from jax.sharding import PartitionSpec as P

HEADS = 32
KV_HEADS = 4
HEAD_DIM = 64
GROUPS = HEADS // KV_HEADS
HEAD_COLS = GROUPS * HEAD_DIM
FACTOR = 1.0 / math.sqrt(HEAD_DIM)

norm_eps = 1e-05
rope_base = 10000.0

BF = jnp.bfloat16
F32 = jnp.float32
MIB = 1 << 20


def dot(left, right):
    return jnp.dot(left, right, preferred_element_type=F32)


def dot_nt(left, right):
    return lax.dot_general(left, right, (((1,), (1,)), ((), ())), preferred_element_type=F32)


def dot_tn(left, right):
    return lax.dot_general(left, right, (((0,), (0,)), ((), ())), preferred_element_type=F32)


def shape_of(shape, kind):
    return jax.ShapeDtypeStruct(shape, kind)


def run(kernel, ins, outs, specs=None, out_specs=None, grid=None, vmem=32, scratch=(), flops=0):
    whole = pl.BlockSpec(memory_space=pltpu.VMEM)
    moved = sum(math.prod(a.shape) * a.dtype.itemsize for a in list(ins) + list(outs))
    extra = {} if grid is None else {"grid": grid}
    name = kernel.func.__name__ if isinstance(kernel, functools.partial) else kernel.__name__
    return pl.pallas_call(
        kernel,
        name=name,
        out_shape=list(outs),
        in_specs=specs or [whole] * len(ins),
        out_specs=out_specs or [whole] * len(outs),
        scratch_shapes=list(scratch),
        compiler_params=pltpu.CompilerParams(vmem_limit_bytes=vmem * MIB),
        cost_estimate=pl.CostEstimate(flops=0, bytes_accessed=0, transcendentals=0),
        **extra,
    )(*ins)


SMEM = pl.BlockSpec(memory_space=pltpu.SMEM)


class Bit:
    def __init__(self, axis, bit, size):
        self.axis, self.bit = axis, bit
        self.pairs = [(i, i ^ (1 << bit)) for i in range(size)]

    def mine(self):
        return (lax.axis_index(self.axis) >> self.bit) & 1

    def swap(self, value, what="rows"):
        with jax.named_scope(f"{what}_{self.axis}{self.bit}"):
            return lax.ppermute(value, self.axis, self.pairs)


def after(value, *others):
    return lax.optimization_barrier((value,) + others)[0]


class Order:
    def __init__(self, names, gathered, rest, depth):
        self.names, self.gathered, self.rest, self.depth = names, gathered, rest, depth
        self.rel = gathered + rest
        self.fast = depth == 64 and len(names) == 5 and names[-1] in gathered and rest[-1] is not names[-1]
        self.mine = jnp.stack(
            [b.mine() if b in gathered else jnp.zeros((), jnp.int32) for b in names]
        ).astype(jnp.int32)

    def to_tiles(self, read, write, mine):
        lanes = lax.broadcasted_iota(jnp.int32, (1, 128), 1)
        head = self.rel[:-1]
        last = self.rel[-1]
        for q in range(16):
            value = {b: (q >> (3 - i)) & 1 for i, b in enumerate(head)}

            def source(low):
                index = 0
                for i, b in enumerate(self.names[:-1]):
                    v = low if b is last else value[b]
                    if b in self.gathered:
                        v = v ^ mine[i]
                    index = index * 2 + v
                return read(index)

            a, b = source(0), source(1)
            side = value[self.names[-1]] ^ mine[4]
            first = jnp.where(lanes < 64, a, pltpu.roll(b, 64, 1))
            second = jnp.where(lanes < 64, pltpu.roll(a, 64, 1), b)
            write(q, jnp.where(side == 0, first, second))

    def from_tiles(self, read, write, mine):
        lanes = lax.broadcasted_iota(jnp.int32, (1, 128), 1)
        for t in range(16):
            value = {b: (t >> (3 - i)) & 1 for i, b in enumerate(self.names[:-1])}

            def source(y):
                index = 0
                for b in self.rel[:-1]:
                    v = y if b is self.names[-1] else value[b]
                    if b in self.gathered:
                        v = v ^ mine[self.names.index(b)]
                    index = index * 2 + v
                return read(index)

            low, high = source(0), source(1)
            if value[self.rel[-1]] == 0:
                write(t, jnp.where(lanes < 64, low, pltpu.roll(high, 64, 1)))
            else:
                write(t, jnp.where(lanes < 64, pltpu.roll(low, 64, 1), high))

    def to_rel(self, array):
        count, width = array.shape
        out = array.reshape((count,) + (2,) * len(self.names) + (self.depth,))
        for b in self.gathered:
            k = self.names.index(b) + 1
            out = jnp.where(b.mine() == 1, jnp.flip(out, k), out)
        axes = [self.names.index(b) + 1 for b in self.rel]
        return out.transpose([0] + axes + [len(self.names) + 1]).reshape(count, width)

    def from_rel(self, array):
        count, width = array.shape
        out = array.reshape((count,) + (2,) * len(self.names) + (self.depth,))
        axes = [self.rel.index(b) + 1 for b in self.names]
        out = out.transpose([0] + axes + [len(self.names) + 1])
        for b in self.gathered:
            k = self.names.index(b) + 1
            out = jnp.where(b.mine() == 1, jnp.flip(out, k), out)
        return out.reshape(count, width)


def tile(index):
    start = index * 128
    return pl.ds(start if isinstance(start, int) else pl.multiple_of(start, 128), 128)


def row_specs(count, rows, width, steps):
    return [pl.BlockSpec((rows // steps, width), lambda i: (i, 0))] * count


def inverse_of(x):
    return lax.rsqrt(jnp.mean(x * x, -1, keepdims=True) + norm_eps)


def norm_kernel(order, mine_ref, x_ref, gain_ref, out_ref):
    mine = [mine_ref[i] for i in range(5)]
    inverse = inverse_of(x_ref[...].astype(F32))

    def write(q, value):
        out_ref[:, tile(q)] = value.astype(BF)

    def read(i):
        return x_ref[:, tile(i)].astype(F32) * inverse * gain_ref[:, tile(i)]

    order.to_tiles(read, write, mine)


def norm_to(order, x, gain):
    if not order.fast:
        x = x.astype(F32)
        return order.to_rel((x * inverse_of(x) * gain).astype(BF))
    rows, width = x.shape
    specs = row_specs(2, rows, width, 2)
    return run(
        functools.partial(norm_kernel, order),
        [order.mine, x, gain],
        [shape_of((rows, width), BF)],
        [SMEM, specs[0], pl.BlockSpec((1, width), lambda i: (0, 0))],
        [specs[1]],
        (2,),
    )[0]


def order_kernel(order, mine_ref, x_ref, out_ref):
    mine = [mine_ref[i] for i in range(5)]

    def write(q, value):
        out_ref[:, tile(q)] = value.astype(out_ref.dtype)

    order.to_tiles(lambda i: x_ref[:, tile(i)].astype(F32), write, mine)


def order_to(order, x):
    if not order.fast:
        return order.to_rel(x)
    rows, width = x.shape
    specs = row_specs(2, rows, width, 2)
    return run(
        functools.partial(order_kernel, order),
        [order.mine, x],
        [shape_of((rows, width), x.dtype)],
        [SMEM, specs[0]],
        [specs[1]],
        (2,),
    )[0]


def middle_kernel(order, mine_ref, x_ref, a_ref, b_ref, mid_ref, out_ref):
    mine = [mine_ref[i] for i in range(5)]
    mid = x_ref[...].astype(F32) + a_ref[...].astype(F32) + b_ref[...].astype(F32)
    mid_ref[...] = mid
    inverse = inverse_of(mid)

    def write(q, value):
        out_ref[:, tile(q)] = value.astype(BF)

    order.to_tiles(lambda i: mid_ref[:, tile(i)] * inverse, write, mine)


def middle_to(order, x, a, b):
    rows, width = x.shape
    if not order.fast:
        mid = x.astype(F32) + a.astype(F32) + b.astype(F32)
        return mid, order.to_rel((mid * inverse_of(mid)).astype(BF))
    specs = row_specs(5, rows, width, 2)
    return run(
        functools.partial(middle_kernel, order),
        [order.mine, x, a, b],
        [shape_of((rows, width), F32), shape_of((rows, width), BF)],
        [SMEM] + specs[:3],
        specs[:2],
        (2,),
    )


def back_kernel(order, scaled, mine_ref, x_ref, g_ref, a_ref, b_ref, *outs):
    mine = [mine_ref[i] for i in range(5)]
    scratch = outs[-1]
    if scaled:
        gain_ref, outs = outs[0], outs[1:]
    inverse = inverse_of(x_ref[...].astype(F32))

    def write(t, value):
        scratch[:, tile(t)] = value * gain_ref[:, tile(t)] if scaled else value

    def read(i):
        return a_ref[:, tile(i)].astype(F32) + b_ref[:, tile(i)].astype(F32)

    order.from_tiles(read, write, mine)
    normed = x_ref[...].astype(F32) * inverse
    scaled = scratch[...]
    shared = jnp.mean(scaled * normed, -1, keepdims=True)
    total = g_ref[...].astype(F32) + inverse * (scaled - normed * shared)
    outs[0][...] = total
    if len(outs) == 3:
        outs[1][...] = total.astype(BF)


def norm_back(order, x, g, a, b, gain=None, low=False):
    rows, width = x.shape
    scaled = gain is not None
    if not order.fast:
        x = x.astype(F32)
        inverse = inverse_of(x)
        normed = x * inverse
        grad = a.astype(F32) + b.astype(F32)
        grad = order.from_rel(grad)
        grad = grad * gain if scaled else grad
        shared = jnp.mean(grad * normed, -1, keepdims=True)
        total = g.astype(F32) + inverse * (grad - normed * shared)
        return (total, total.astype(BF)) if low else (total,)
    specs = row_specs(6, rows, width, 2)
    outs = [shape_of((rows, width), F32)] + ([shape_of((rows, width), BF)] if low else [])
    return run(
        functools.partial(back_kernel, order, scaled),
        [order.mine, x, g, a, b] + ([gain] if scaled else []),
        outs,
        [SMEM] + specs[:4] + [pl.BlockSpec((1, width), lambda i: (0, 0))] * scaled,
        specs[: len(outs)],
        (2,),
        scratch=[pltpu.VMEM((rows // 2, width), F32)],
    )


def result_kernel(order, mine_ref, mid_ref, a_ref, b_ref, out_ref):
    mine = [mine_ref[i] for i in range(5)]

    def write(t, value):
        out_ref[:, tile(t)] = (mid_ref[:, tile(t)] + value).astype(BF)

    order.from_tiles(
        lambda i: a_ref[:, tile(i)].astype(F32) + b_ref[:, tile(i)].astype(F32), write, mine
    )


def result_of(order, mid, a, b):
    rows, width = mid.shape
    if not order.fast:
        return (mid + order.from_rel(a.astype(F32) + b.astype(F32))).astype(BF)
    specs = row_specs(4, rows, width, 2)
    return run(
        functools.partial(result_kernel, order),
        [order.mine, mid, a, b],
        [shape_of((rows, width), BF)],
        [SMEM] + specs[:3],
        specs[:1],
        (2,),
    )[0]


def pack_kernel(count, kinds, *refs):
    out_ref = refs[-1]
    cols = out_ref.shape[-1]
    depth = refs[0].shape[0]
    for m in range(kinds):
        value = refs[m][...].astype(F32)
        if len(refs) > kinds + 1:
            value = value * refs[kinds][...]
        for t in range(count):
            out_ref[t, m * depth : (m + 1) * depth] = value[:, t * cols : (t + 1) * cols].astype(BF)


def pack(weights, gain, count):
    depth, width = weights[0].shape
    return run(
        functools.partial(pack_kernel, count, len(weights)),
        weights + ([] if gain is None else [gain]),
        [shape_of((count, len(weights) * depth, width // count), BF)],
    )[0]


def unpack_kernel(count, kinds, scaled, *refs):
    p_ref = refs[0]
    cols = p_ref.shape[-1]
    depth = p_ref.shape[1] // kinds
    outs = refs[-kinds - 1 : -1] if scaled else refs[-kinds:]
    total = jnp.zeros((depth, 1), F32)
    for m in range(kinds):
        for t in range(count):
            part = p_ref[t, m * depth : (m + 1) * depth].astype(F32)
            lanes = slice(t * cols, (t + 1) * cols)
            if scaled:
                total = total + jnp.sum(part * refs[1 + m][:, lanes].astype(F32), -1, keepdims=True)
                part = part * refs[1 + kinds][...]
            outs[m][:, lanes] = part
    if scaled:
        refs[-1][...] = total


def unpack(parts, weights, gain):
    count, depth, cols = parts.shape
    if gain is None:
        outs = [shape_of((depth, count * cols), F32)]
        return run(functools.partial(unpack_kernel, count, 1, False), [parts], outs)
    kinds = len(weights)
    outs = [shape_of((depth // kinds, count * cols), F32)] * kinds + [shape_of((depth // kinds, 1), F32)]
    return run(functools.partial(unpack_kernel, count, kinds, True), [parts] + weights + [gain], outs)


def pack_qkv_kernel(count, q_ref, k_ref, v_ref, out_ref):
    for t in range(count):
        out_ref[t, :, :HEAD_COLS] = q_ref[:, t * HEAD_COLS : (t + 1) * HEAD_COLS]
        lanes = slice(t * HEAD_DIM, (t + 1) * HEAD_DIM)
        both = jnp.concatenate([k_ref[:, lanes].astype(F32), v_ref[:, lanes].astype(F32)], -1)
        out_ref[t, :, HEAD_COLS:] = both.astype(BF)


def unpack_qkv_kernel(count, q_ref, k_ref, v_ref, g_ref, p_ref, qo_ref, ko_ref, vo_ref, sum_ref):
    gain = g_ref[...]
    total = jnp.zeros_like(gain)
    for t in range(count):
        part = p_ref[t].astype(F32)
        lanes = slice(t * HEAD_COLS, (t + 1) * HEAD_COLS)
        thin = slice(t * HEAD_DIM, (t + 1) * HEAD_DIM)
        gq = part[:, :HEAD_COLS]
        gk = part[:, HEAD_COLS : HEAD_COLS + HEAD_DIM]
        gv = part[:, HEAD_COLS + HEAD_DIM :]
        total = total + jnp.sum(gq * q_ref[:, lanes].astype(F32), -1, keepdims=True)
        total = total + jnp.sum(gk * k_ref[:, thin].astype(F32), -1, keepdims=True)
        total = total + jnp.sum(gv * v_ref[:, thin].astype(F32), -1, keepdims=True)
        qo_ref[:, lanes] = gq
        ko_ref[:, thin] = gk
        vo_ref[:, thin] = gv
    sum_ref[...] = total / gain


def swap_halves(values):
    width = values.shape[-1]
    lanes = lax.broadcasted_iota(jnp.int32, (1, width), 1)
    return jnp.where(
        lanes % HEAD_DIM < HEAD_DIM // 2,
        pltpu.roll(values, width - HEAD_DIM // 2, 1),
        pltpu.roll(values, HEAD_DIM // 2, 1),
    )


def project_kernel(repeat, count, *refs):
    a_ref, cos_ref, sin_ref = refs[:3]
    w_refs, q_ref, kv_ref = refs[3 : 3 + count], refs[-2], refs[-1]
    piece = w_refs[0].shape[0]
    raw = None
    for k in range(count):
        term = dot(a_ref[:, k * piece : (k + 1) * piece], w_refs[k][...])
        raw = term if raw is None else raw + term
    cosine = jnp.concatenate([cos_ref[...]] * repeat, 0)
    sine = jnp.concatenate([sin_ref[...]] * repeat, 0)
    out = (raw * cosine + swap_halves(raw) * sine).astype(BF)
    q_ref[...] = out[:, :HEAD_COLS]
    kv_ref[...] = out[:, HEAD_COLS:]


def project(a1, cosine, sine, parts):
    rows, width = a1.shape
    seq_dev, cols = cosine.shape
    block = min(2 * seq_dev, rows)
    fixed = lambda i: (0, 0)
    moving = lambda i: (i, 0)
    return run(
        functools.partial(project_kernel, block // seq_dev, len(parts)),
        [a1, cosine, sine] + parts,
        [shape_of((rows, HEAD_COLS), BF), shape_of((rows, 2 * HEAD_DIM), BF)],
        [pl.BlockSpec((block, width), moving)]
        + [pl.BlockSpec((seq_dev, cols), fixed)] * 2
        + [pl.BlockSpec(p.shape, fixed) for p in parts],
        [pl.BlockSpec((block, HEAD_COLS), moving), pl.BlockSpec((block, 2 * HEAD_DIM), moving)],
        (rows // block,),
        flops=2 * rows * width * cols,
    )


def stack_heads(values):
    return jnp.concatenate(
        [values[:, j * HEAD_DIM : (j + 1) * HEAD_DIM] for j in range(GROUPS)], 0
    )


def soft_weights(queries, keys, key_ref, seq_dev):
    scores = dot_nt(queries, keys) * FACTOR
    place = lax.broadcasted_iota(jnp.int32, (queries.shape[0], 1), 0) % seq_dev
    return jnp.where(place >= key_ref[...], jnp.exp(scores), 0.0)


def attend_kernel(q_ref, kv_ref, key_ref, o_ref):
    seq_dev = q_ref.shape[0]
    both = kv_ref[...].reshape(-1, 2 * HEAD_DIM)
    keys, values = both[:, :HEAD_DIM], both[:, HEAD_DIM:]
    weights = soft_weights(stack_heads(q_ref[...]), keys, key_ref, seq_dev)
    totals = jnp.sum(weights, -1, keepdims=True)
    attended = dot(weights.astype(BF), values) / totals
    for j in range(GROUPS):
        rows = attended[j * seq_dev : (j + 1) * seq_dev]
        o_ref[:, j * HEAD_DIM : (j + 1) * HEAD_DIM] = rows.astype(BF)


def attend(queries, kv, key_places, seq_dev):
    rows = queries.shape[0]
    count, seqs = kv.shape[:2]
    return run(
        attend_kernel,
        [queries, kv, key_places],
        [shape_of((rows, HEAD_COLS), BF)],
        [
            pl.BlockSpec((seq_dev, HEAD_COLS), lambda s: (s, 0)),
            pl.BlockSpec((count, 1, seq_dev, 2 * HEAD_DIM), lambda s: (0, s, 0, 0)),
            pl.BlockSpec((1, count * seq_dev), lambda s: (0, 0)),
        ],
        [pl.BlockSpec((seq_dev, HEAD_COLS), lambda s: (s, 0))],
        (seqs,),
        flops=4 * rows * GROUPS * HEAD_DIM * count * seq_dev,
    )[0]


def attend_back_kernel(q_ref, kv_ref, key_ref, do_ref, cos_ref, sin_ref, dq_ref, dkv_ref, mid_ref):
    seq_dev = q_ref.shape[0]
    both = kv_ref[...].reshape(-1, 2 * HEAD_DIM)
    keys, values = both[:, :HEAD_DIM], both[:, HEAD_DIM:]
    queries = stack_heads(q_ref[...])
    weights = soft_weights(queries, keys, key_ref, seq_dev)
    totals = jnp.sum(weights, -1, keepdims=True)
    low = weights.astype(BF)
    attended = dot(low, values) / totals
    grads = stack_heads(do_ref[...])
    deltas = jnp.sum(grads * attended, -1, keepdims=True) / totals
    mixed = (grads / totals).astype(BF)
    scores = (weights * (dot_nt(mixed, values) - deltas)).astype(BF)
    turned = dot(scores, keys) * FACTOR
    for j in range(GROUPS):
        mid_ref[:, j * HEAD_DIM : (j + 1) * HEAD_DIM] = turned[j * seq_dev : (j + 1) * seq_dev]
    whole = mid_ref[...]
    dq_ref[...] = (whole * cos_ref[...] - swap_halves(whole) * sin_ref[...]).astype(BF)
    grad_keys = dot_tn(scores, queries) * FACTOR
    grad_values = dot_tn(low, mixed)
    joined = jnp.concatenate([grad_keys, grad_values], -1)
    dkv_ref[...] = joined.astype(BF).reshape(dkv_ref.shape)


def attend_back(queries, kv, key_places, grads, cosine, sine, seq_dev):
    rows = queries.shape[0]
    count, seqs = kv.shape[:2]
    own = pl.BlockSpec((seq_dev, HEAD_COLS), lambda s: (s, 0))
    table = pl.BlockSpec((seq_dev, HEAD_COLS), lambda s: (0, 0))
    blocks = pl.BlockSpec((count, 1, seq_dev, 2 * HEAD_DIM), lambda s: (0, s, 0, 0))
    return run(
        attend_back_kernel,
        [queries, kv, key_places, grads, cosine, sine],
        [shape_of((rows, HEAD_COLS), BF), shape_of(kv.shape, BF)],
        [own, blocks, pl.BlockSpec((1, count * seq_dev), lambda s: (0, 0)), own, table, table],
        [own, blocks],
        (seqs,),
        scratch=[pltpu.VMEM((seq_dev, HEAD_COLS), F32)],
        flops=14 * rows * GROUPS * HEAD_DIM * count * seq_dev,
    )


def turn_back_kernel(repeat, a_ref, b_ref, cos_ref, sin_ref, out_ref):
    total = a_ref[...].astype(F32) + b_ref[...].astype(F32)
    cosine = jnp.concatenate([cos_ref[...]] * repeat, 0)
    sine = jnp.concatenate([sin_ref[...]] * repeat, 0)
    out_ref[...] = (total * cosine - swap_halves(total) * sine).astype(BF)


def wide_kernel(product, left_ref, *refs):
    rights, out_ref = refs[:-1], refs[-1]
    cols = out_ref.shape[1] // len(rights)
    for k, right in enumerate(rights):
        out_ref[:, k * cols : (k + 1) * cols] = product(left_ref[...], right[...]).astype(BF)


def wide(product, left, rights, width, block):
    rows, depth = left.shape
    return run(
        functools.partial(wide_kernel, product),
        [left] + rights,
        [shape_of((rows, width), BF)],
        [pl.BlockSpec((block, depth), lambda i: (i, 0))]
        + [pl.BlockSpec(r.shape, lambda i: (0, 0)) for r in rights],
        [pl.BlockSpec((block, width), lambda i: (i, 0))],
        (rows // block,),
        vmem=48,
        flops=2 * rows * depth * width,
    )[0]


def gate_kernel(pieces, a_ref, *refs):
    both = refs[:pieces]
    hid_ref, one_ref, two_ref = refs[pieces:]
    units, cols = hid_ref.shape[1], both[0].shape[1]
    gate = up = None
    for k in range(pieces):
        part = a_ref[:, k * cols : (k + 1) * cols]
        g, u = dot_nt(part, both[k][:units]), dot_nt(part, both[k][units:])
        gate = g if gate is None else gate + g
        up = u if up is None else up + u
    sigmoid = jax.nn.sigmoid(gate)
    active = gate * sigmoid
    hid_ref[...] = (active * up).astype(BF)
    one_ref[...] = up * sigmoid * (1.0 + gate * (1.0 - sigmoid))
    two_ref[...] = active


def gate_up(a2, both, block):
    rows, width = a2.shape
    cols = both[0].shape[0] // 2
    moving = lambda i: (i, 0)
    out = pl.BlockSpec((block, cols), moving)
    return run(
        functools.partial(gate_kernel, len(both)),
        [a2] + both,
        [shape_of((rows, cols), BF), shape_of((rows, cols), F32), shape_of((rows, cols), F32)],
        [pl.BlockSpec((block, width), moving)]
        + [pl.BlockSpec(w.shape, lambda i: (0, 0)) for w in both],
        [out, out, out],
        (rows // block,),
        vmem=48,
        flops=4 * rows * width * cols,
    )


def hidden_kernel(pieces, g_ref, one_ref, two_ref, *refs):
    downs, both = refs[:pieces], refs[pieces : 2 * pieces]
    dboth_ref, out_ref = refs[2 * pieces :]
    units, cols = downs[0].shape
    total = None
    for k in range(pieces):
        term = dot_nt(g_ref[:, k * cols : (k + 1) * cols], downs[k][...])
        total = term if total is None else total + term
    dgate = (total * one_ref[...]).astype(BF)
    dup = (total * two_ref[...]).astype(BF)
    dboth_ref[:, :units] = dgate
    dboth_ref[:, units:] = dup
    for k in range(pieces):
        part = dot(dgate, both[k][:units]) + dot(dup, both[k][units:])
        out_ref[:, k * cols : (k + 1) * cols] = part.astype(BF)


def hidden_back(gb, one, two, downs, both, block):
    rows, width = gb.shape
    cols = downs[0].shape[0]
    moving = lambda i: (i, 0)
    thin = pl.BlockSpec((block, cols), moving)
    full = pl.BlockSpec((block, width), moving)
    return run(
        functools.partial(hidden_kernel, len(downs)),
        [gb, one, two] + downs + both,
        [shape_of((rows, 2 * cols), BF), shape_of((rows, width), BF)],
        [full, thin, thin] + [pl.BlockSpec(w.shape, lambda i: (0, 0)) for w in downs + both],
        [pl.BlockSpec((block, 2 * cols), moving), full],
        (rows // block,),
        vmem=56,
        flops=6 * rows * width * cols,
    )


def gather_rows(value, bits, what):
    acc = value
    for bit in bits:
        acc = jnp.concatenate([acc, bit.swap(acc, what)], 0)
    return acc


def reduce_rows(acc, bits, what):
    for bit in list(reversed(bits))[:-1]:
        half = acc.shape[0] // 2
        got = bit.swap(acc[half:], what)
        acc = (acc[:half].astype(F32) + got.astype(F32)).astype(BF)
    half = acc.shape[0] // 2
    return acc[:half], bits[0].swap(acc[half:], what)


def gather_team(value, bit_x, near, bit_core, what):
    half = value.shape[0] // 2
    by_x, by_near = bit_x.swap(value, what), near.swap(value, what)
    diagonal = [bit_x.swap(by_near[:half], what), near.swap(by_x[half:], what)]
    four = jnp.concatenate([value, by_x, by_near] + diagonal, 0)
    return jnp.concatenate([four, bit_core.swap(four, what)], 0)


def add_low(a, b):
    return (a.astype(F32) + b.astype(F32)).astype(BF)


def reduce_team(acc, bit_x, near, bit_core, what):
    half = acc.shape[0] // 2
    return reduce_four(acc[:half], bit_core.swap(acc[half:], what), bit_x, near, what)


def reduce_four(acc, got, bit_x, near, what):
    half = acc.shape[0]
    acc = add_low(acc, got)
    rows = half // 4
    own, by_x, by_near = acc[:rows], acc[rows : 2 * rows], acc[2 * rows : 3 * rows]
    first, second = acc[3 * rows : 3 * rows + rows // 2], acc[3 * rows + rows // 2 :]
    got_near = bit_x.swap(first, what)
    got_x = near.swap(second, what)
    by_near = jnp.concatenate([add_low(by_near[: rows // 2], got_near), by_near[rows // 2 :]], 0)
    by_x = jnp.concatenate([by_x[: rows // 2], add_low(by_x[rows // 2 :], got_x)], 0)
    return add_low(own, bit_x.swap(by_x, what)), near.swap(by_near, what)


def absolute(blocks, index, bits):
    def one(j):
        other = index ^ j
        slot = sum(((other >> b.bit) & 1) << i for i, b in enumerate(bits))
        return lax.dynamic_index_in_dim(blocks, slot, 0, False)

    return jnp.stack([one(j) for j in range(blocks.shape[0])])


def relative(blocks, index, bits):
    def one(r):
        code = sum(((r >> i) & 1) << b.bit for i, b in enumerate(bits))
        return lax.dynamic_index_in_dim(blocks, index ^ code, 0, False)

    return jnp.stack([one(r) for r in range(blocks.shape[0])])


def shards(
    dp,
    ctx,
    tokens,
    cotangent,
    attn_gain,
    query_weight,
    key_weight,
    value_weight,
    output_weight,
    mlp_gain,
    gate_weight,
    up_weight,
    down_weight,
):
    seqs, seq_dev, width = tokens.shape
    rows = seqs * seq_dev
    depth = query_weight.shape[0]
    c_index = lax.axis_index("ctx")

    bit_x, bit_core = Bit("dp", 1, dp), Bit("dp", 0, dp)
    ctx_bits = [Bit("ctx", b, ctx) for b in reversed(range(ctx.bit_length() - 1))]
    near = ctx_bits[-2]
    far = [b for b in ctx_bits if b is not near]
    dp_bits = [bit_x, bit_core]
    names = dp_bits + ctx_bits
    attn_order = Order(names, list(reversed(ctx_bits)), dp_bits, depth)
    mlp_order = Order(names, far, dp_bits + [near], depth)
    x = tokens.reshape(rows, width)
    cot = cotangent.reshape(rows, width)
    gain_one = attn_gain.astype(F32)[:, None]
    gain_two = mlp_gain.astype(F32)[:, None]

    team_groups = []
    for c in range(ctx):
        if not (c >> near.bit) & 1:
            team_groups.append([d * ctx + (c | (n << near.bit)) for d in range(dp) for n in range(2)])
    team = 2 * dp

    def mlp_trade(parts):
        return lax.all_to_all(
            parts, ("dp", "ctx"), 0, 0, axis_index_groups=team_groups, tiled=True
        )

    def mlp_slices(weights, gain):
        kinds = len(weights)
        parts = mlp_trade(pack(weights, gain, team)).reshape(team, kinds, depth, -1)
        return parts.transpose(1, 3, 0, 2).reshape(-1, team * depth)

    def mlp_rows(sums, kinds):
        parts = sums.reshape(kinds, -1, team, depth).transpose(2, 0, 3, 1)
        return mlp_trade(parts.reshape(team, kinds * depth, -1))

    digits = [sum(((k >> i) & 1) << (len(far) - 1 - i) for i in range(len(far))) for k in range(1 << len(far))]

    qkv_cols = HEAD_COLS + 2 * HEAD_DIM
    own = run(
        functools.partial(pack_qkv_kernel, dp),
        [query_weight, key_weight, value_weight],
        [shape_of((dp, depth, qkv_cols), BF)],
    )[0]
    own = lax.all_to_all(own, "dp", 0, 0, tiled=True).reshape(dp * depth, qkv_cols)
    both_own = mlp_slices([after(gate_weight, own), up_weight], gain_two)
    gain_all = jnp.broadcast_to(after(attn_gain, both_own)[None], (dp * ctx, depth))
    gain_all = lax.all_to_all(gain_all, ("dp", "ctx"), 0, 0, tiled=True)
    gain_all = gain_all.reshape(1, width).astype(F32)
    down_own = mlp_slices([after(down_weight.T, gain_all)], None)
    half = own
    for bit in ctx_bits[:-1]:
        half = jnp.concatenate([half, bit.swap(half, "qkv")], 0)
    qkv = [half, ctx_bits[-1].swap(half, "qkv")]
    out_bits = ctx_bits[:-2] + [ctx_bits[-1], near]
    out_rel = output_weight
    for i, bit in enumerate(out_bits):
        if bit is near:
            out_rel = after(out_rel, down_own)
        out_rel = jnp.concatenate([out_rel, bit.swap(out_rel, "out")], 0)
    out_full = absolute(out_rel.reshape(ctx, depth, width), c_index, out_bits)
    out_full = out_full.reshape(ctx * depth, width)

    def mlp_parts(own, marks, what):
        parts = [own]
        for i, bit in enumerate(far):
            sent = []
            for k, p in enumerate(parts):
                mark = marks.get((min(i, 1), min(k, 1)))
                sent.append(p if mark is None else after(p, mark))
            parts = parts + [bit.swap(p, what) for p in sent]
        return parts

    both = mlp_parts(both_own, {}, "both")
    downs = mlp_parts(down_own, {(0, 0): both[1]}, "down")
    pieces = len(both)
    piece = width // pieces

    def by_digit(parts):
        return [parts[digits.index(k)] for k in range(pieces)]

    places = jnp.arange(seq_dev, dtype=jnp.int32)
    half_dim = HEAD_DIM // 2
    freqs = rope_base ** (-(jnp.arange(half_dim, dtype=F32) * 2.0) / HEAD_DIM)
    angles = (c_index * seq_dev + places).astype(F32)[:, None] * freqs[None, :]
    cosine, sine = jnp.cos(angles), jnp.sin(angles)
    cosine = jnp.concatenate([cosine, cosine] * (GROUPS + 1) + [jnp.ones((seq_dev, HEAD_DIM), F32)], -1)
    sine = jnp.concatenate([-sine, sine] * (GROUPS + 1) + [jnp.zeros((seq_dev, HEAD_DIM), F32)], -1)
    rel = jnp.arange(ctx, dtype=jnp.int32)
    others = sum(((rel >> i) & 1) << b.bit for i, b in enumerate(ctx_bits)) ^ c_index
    key_places = (((others - c_index) * seq_dev)[:, None] + places[None, :]).reshape(1, -1)

    a1 = gather_rows(norm_to(attn_order, x, gain_all), dp_bits, "a1")
    queries, kv_own = project(after(a1, down_own), cosine, sine, qkv)
    all_seqs = dp * seqs
    kv = kv_own
    for bit in ctx_bits:
        kv = jnp.concatenate([kv, bit.swap(kv, "kv")], 0)
    gb = order_to(mlp_order, after(cot, kv))
    gb = gather_team(gb, bit_x, near, bit_core, "gb")
    kv = kv.reshape(ctx, all_seqs, seq_dev, 2 * HEAD_DIM)
    heads = attend(queries, kv, key_places, seq_dev)
    branch = dot(after(heads, both[1]), out_full).astype(BF)
    branch = reduce_rows(branch, dp_bits, "branch")
    middle, a2 = middle_to(mlp_order, after(x, both[2]), *branch)

    a2 = gather_team(a2, bit_x, near, bit_core, "a2")
    block = min(256, a2.shape[0])
    both, downs = by_digit(both), by_digit(downs)
    hidden, one, two = gate_up(a2, both, block)
    dboth, da2 = hidden_back(gb, one, two, downs, both, block)
    half = da2.shape[0] // 2
    da2_got = bit_core.swap(da2[half:], "da2")
    da2_two = reduce_four(da2[:half], da2_got, bit_x, near, "da2")
    grad_middle, db = norm_back(mlp_order, middle, cot, *da2_two, low=True)
    grad_branch = gather_rows(db, dp_bits, "db")
    down_out = wide(dot, after(hidden, grad_branch), downs, width, block)
    result = reduce_team(down_out, bit_x, near, bit_core, "result")
    result = result_of(mlp_order, middle, *result)

    grad_heads = dot_nt(grad_branch, out_full)
    dq, dkv = attend_back(
        queries, kv, key_places, grad_heads, cosine[:, :HEAD_COLS], sine[:, :HEAD_COLS], seq_dev
    )

    def mlp_return(left, right, kinds, what):
        terms = []
        for k in range(pieces):
            one = left if k == pieces - 1 else after(left, da2_got)
            terms.append(dot_tn(right, one[:, k * piece : (k + 1) * piece]).astype(BF))
        terms = [terms[digits[k]] for k in range(pieces)]
        for bit in reversed(far):
            half = len(terms) // 2
            got = [bit.swap(s, what) for s in terms[half:]]
            terms = [add_low(after(t, dq) if k == 0 else t, got[k]) for k, t in enumerate(terms[:half])]
        return mlp_rows(terms[0], kinds)

    both_back = mlp_return(a2, dboth, 2, "dboth")
    down_back = mlp_return(gb, hidden, 1, "ddown")
    dkv_two = reduce_rows(dkv.reshape(-1, 2 * HEAD_DIM), ctx_bits, "dkv")
    dkv_low = run(
        functools.partial(turn_back_kernel, all_seqs),
        list(dkv_two) + [cosine[:, HEAD_COLS:], sine[:, HEAD_COLS:]],
        [shape_of((dp * rows, 2 * HEAD_DIM), BF)],
    )[0]
    draw = jnp.concatenate([dq, dkv_low], -1)
    da1 = wide(dot_nt, draw, qkv, width, min(256, dp * rows))
    (grad_tokens,) = norm_back(attn_order, x, grad_middle, *reduce_rows(da1, dp_bits, "da1"), gain_all)
    q_total = add_low(*reduce_rows(dot_tn(a1, dq).astype(BF), ctx_bits, "dq_w"))
    kv_total = add_low(*reduce_rows(dot_tn(a1, dkv_low).astype(BF), ctx_bits, "dkv_w"))
    qkv_total = jnp.concatenate([q_total, kv_total], -1).reshape(dp, depth, qkv_cols)
    qkv_back = lax.all_to_all(qkv_total, "dp", 0, 0, tiled=True)
    out_total = dot_tn(heads, grad_branch).astype(BF).reshape(ctx, depth, width)
    out_total = relative(out_total, c_index, out_bits).reshape(ctx * depth, width)
    out_two = reduce_rows(out_total, out_bits, "dout_w")
    output_grad = out_two[0].astype(F32) + out_two[1].astype(F32)

    gate_grad, up_grad, mlp_sum = unpack(both_back, [gate_weight, up_weight], gain_two)
    down_grad = unpack(down_back, None, None)[0].T
    query_grad, key_grad, value_grad, attn_sum = run(
        functools.partial(unpack_qkv_kernel, dp),
        [query_weight, key_weight, value_weight, gain_one, qkv_back],
        [shape_of(w.shape, F32) for w in (query_weight, key_weight, value_weight, gain_one)],
    )
    return (
        result.reshape(seqs, seq_dev, width),
        grad_tokens.reshape(seqs, seq_dev, width),
        attn_sum[:, 0],
        query_grad,
        key_grad,
        value_grad,
        output_grad,
        mlp_sum[:, 0],
        gate_grad,
        up_grad,
        down_grad,
    )


def solution(mesh):
    dp, ctx = mesh.shape["dp"], mesh.shape["ctx"]

    def local(*args):
        return shards(dp, ctx, *args)

    weight = P(("dp", "ctx"), None)
    flat = P(("dp", "ctx"))
    acts = P("dp", "ctx", None)
    down = P(None, ("dp", "ctx"))
    return jax.shard_map(
        local,
        mesh=mesh,
        in_specs=(acts, acts, flat, weight, weight, weight, weight, flat, weight, weight, down),
        out_specs=(acts, acts, flat, weight, weight, weight, weight, flat, weight, weight, down),
        check_vma=False,
    )
```

```python
import functools
import math

import jax
import jax.numpy as jnp
from jax import lax
from jax.experimental import pallas as pl
from jax.experimental.pallas import tpu as pltpu
from jax.sharding import PartitionSpec as P

HEADS = 32
KV_HEADS = 4
HEAD_DIM = 64
GROUPS = HEADS // KV_HEADS
HEAD_COLS = GROUPS * HEAD_DIM
FACTOR = 1.0 / math.sqrt(HEAD_DIM)

norm_eps = 1e-05
rope_base = 10000.0

BF = jnp.bfloat16
F32 = jnp.float32
MIB = 1 << 20


def dot(left, right):
    return jnp.dot(left, right, preferred_element_type=F32)


def dot_nt(left, right):
    return lax.dot_general(left, right, (((1,), (1,)), ((), ())), preferred_element_type=F32)


def dot_tn(left, right):
    return lax.dot_general(left, right, (((0,), (0,)), ((), ())), preferred_element_type=F32)


def shape_of(shape, kind):
    return jax.ShapeDtypeStruct(shape, kind)


def run(kernel, ins, outs, specs=None, out_specs=None, grid=None, vmem=32, scratch=(), flops=0):
    whole = pl.BlockSpec(memory_space=pltpu.VMEM)
    moved = sum(math.prod(a.shape) * a.dtype.itemsize for a in list(ins) + list(outs))
    extra = {} if grid is None else {"grid": grid}
    name = kernel.func.__name__ if isinstance(kernel, functools.partial) else kernel.__name__
    return pl.pallas_call(
        kernel,
        name=name,
        out_shape=list(outs),
        in_specs=specs or [whole] * len(ins),
        out_specs=out_specs or [whole] * len(outs),
        scratch_shapes=list(scratch),
        compiler_params=pltpu.CompilerParams(vmem_limit_bytes=vmem * MIB),
        cost_estimate=pl.CostEstimate(flops=0, bytes_accessed=0, transcendentals=0),
        **extra,
    )(*ins)


SMEM = pl.BlockSpec(memory_space=pltpu.SMEM)


class Bit:
    def __init__(self, axis, bit, size):
        self.axis, self.bit = axis, bit
        self.pairs = [(i, i ^ (1 << bit)) for i in range(size)]

    def mine(self):
        return (lax.axis_index(self.axis) >> self.bit) & 1

    def swap(self, value, what):
        with jax.named_scope(f"{what}_{self.axis}{self.bit}"):
            return lax.ppermute(value, self.axis, self.pairs)


def swap_difference(value, axis, size, difference, what):
    with jax.named_scope(f"{what}_{axis}"):
        return lax.ppermute(value, axis, [(i, i ^ difference) for i in range(size)])


def after(value, *others):
    return lax.optimization_barrier((value,) + others)[0]


class Order:
    def __init__(self, names, rel, gathered, depth):
        self.names, self.rel, self.gathered, self.depth = names, rel, gathered, depth
        self.whole_tiles = rel[-1] is names[-1] and not gathered
        self.fast = depth == 64 and len(names) == 5 and (
            self.whole_tiles or (rel[-1] is not names[-1] and rel[-1] not in gathered)
        )
        self.mine = jnp.stack(
            [b.mine() if b in gathered else jnp.zeros((), jnp.int32) for b in names]
        ).astype(jnp.int32)

    def to_tiles(self, read, write, mine):
        lanes = lax.broadcasted_iota(jnp.int32, (1, 128), 1)
        head = self.rel[:-1]
        last = self.rel[-1]
        for q in range(16):
            value = {b: (q >> (3 - i)) & 1 for i, b in enumerate(head)}
            if self.whole_tiles:
                write(q, read(sum(value[b] << (3 - i) for i, b in enumerate(self.names[:-1]))))
                continue

            def source(low):
                index = 0
                for i, b in enumerate(self.names[:-1]):
                    v = low if b is last else value[b]
                    if b in self.gathered:
                        v = v ^ mine[i]
                    index = index * 2 + v
                return read(index)

            a, b = source(0), source(1)
            side = value[self.names[-1]]
            low = lambda: jnp.where(lanes < 64, a, pltpu.roll(b, 64, 1))
            high = lambda: jnp.where(lanes < 64, pltpu.roll(a, 64, 1), b)
            if self.names[-1] in self.gathered:
                write(q, jnp.where((side ^ mine[4]) == 0, low(), high()))
            else:
                write(q, low() if side == 0 else high())

    def from_tiles(self, read, write, mine):
        lanes = lax.broadcasted_iota(jnp.int32, (1, 128), 1)
        for t in range(16):
            value = {b: (t >> (3 - i)) & 1 for i, b in enumerate(self.names[:-1])}
            if self.whole_tiles:
                write(t, read(sum(value[b] << (3 - i) for i, b in enumerate(self.rel[:-1]))))
                continue

            def source(y):
                index = 0
                for b in self.rel[:-1]:
                    v = y if b is self.names[-1] else value[b]
                    if b in self.gathered:
                        v = v ^ mine[self.names.index(b)]
                    index = index * 2 + v
                return read(index)

            low, high = source(0), source(1)
            if value[self.rel[-1]] == 0:
                write(t, jnp.where(lanes < 64, low, pltpu.roll(high, 64, 1)))
            else:
                write(t, jnp.where(lanes < 64, pltpu.roll(low, 64, 1), high))

    def to_rel(self, array):
        count, width = array.shape
        out = array.reshape((count,) + (2,) * len(self.names) + (self.depth,))
        for b in self.gathered:
            k = self.names.index(b) + 1
            out = jnp.where(b.mine() == 1, jnp.flip(out, k), out)
        axes = [self.names.index(b) + 1 for b in self.rel]
        return out.transpose([0] + axes + [len(self.names) + 1]).reshape(count, width)

    def from_rel(self, array):
        count, width = array.shape
        out = array.reshape((count,) + (2,) * len(self.names) + (self.depth,))
        axes = [self.rel.index(b) + 1 for b in self.names]
        out = out.transpose([0] + axes + [len(self.names) + 1])
        for b in self.gathered:
            k = self.names.index(b) + 1
            out = jnp.where(b.mine() == 1, jnp.flip(out, k), out)
        return out.reshape(count, width)


def tile(index):
    start = index * 128
    return pl.ds(start if isinstance(start, int) else pl.multiple_of(start, 128), 128)


def row_specs(count, rows, width, steps):
    return [pl.BlockSpec((rows // steps, width), lambda i: (i, 0))] * count


def inverse_of(x):
    return lax.rsqrt(jnp.mean(x * x, -1, keepdims=True) + norm_eps)


def norm_kernel(order, mine_ref, x_ref, gain_ref, out_ref):
    mine = [mine_ref[i] for i in range(5)]
    inverse = inverse_of(x_ref[...].astype(F32))

    def write(q, value):
        out_ref[:, tile(q)] = value.astype(BF)

    def read(i):
        return x_ref[:, tile(i)].astype(F32) * inverse * gain_ref[:, tile(i)]

    order.to_tiles(read, write, mine)


def norm_to(order, x, gain):
    if not order.fast:
        x = x.astype(F32)
        return order.to_rel((x * inverse_of(x) * gain).astype(BF))
    rows, width = x.shape
    specs = row_specs(2, rows, width, 2)
    return run(
        functools.partial(norm_kernel, order),
        [order.mine, x, gain],
        [shape_of((rows, width), BF)],
        [SMEM, specs[0], pl.BlockSpec((1, width), lambda i: (0, 0))],
        [specs[1]],
        (2,),
    )[0]


def order_kernel(order, mine_ref, x_ref, out_ref):
    mine = [mine_ref[i] for i in range(5)]

    def write(q, value):
        out_ref[:, tile(q)] = value.astype(out_ref.dtype)

    order.to_tiles(lambda i: x_ref[:, tile(i)].astype(F32), write, mine)


def order_to(order, x):
    if not order.fast:
        return order.to_rel(x)
    rows, width = x.shape
    specs = row_specs(2, rows, width, 2)
    return run(
        functools.partial(order_kernel, order),
        [order.mine, x],
        [shape_of((rows, width), x.dtype)],
        [SMEM, specs[0]],
        [specs[1]],
        (2,),
    )[0]


def middle_kernel(order, mine_ref, x_ref, a_ref, b_ref, mid_ref, out_ref):
    mine = [mine_ref[i] for i in range(5)]
    mid = x_ref[...].astype(F32) + a_ref[...].astype(F32) + b_ref[...].astype(F32)
    mid_ref[...] = mid
    inverse = inverse_of(mid)

    def write(q, value):
        out_ref[:, tile(q)] = value.astype(BF)

    order.to_tiles(lambda i: mid_ref[:, tile(i)] * inverse, write, mine)


def middle_to(order, x, a, b):
    rows, width = x.shape
    if not order.fast:
        mid = x.astype(F32) + a.astype(F32) + b.astype(F32)
        return mid, order.to_rel((mid * inverse_of(mid)).astype(BF))
    specs = row_specs(5, rows, width, 2)
    return run(
        functools.partial(middle_kernel, order),
        [order.mine, x, a, b],
        [shape_of((rows, width), F32), shape_of((rows, width), BF)],
        [SMEM] + specs[:3],
        specs[:2],
        (2,),
    )


def back_kernel(order, scaled, mine_ref, x_ref, g_ref, a_ref, b_ref, *outs):
    mine = [mine_ref[i] for i in range(5)]
    scratch = outs[-1]
    if scaled:
        gain_ref, outs = outs[0], outs[1:]
    inverse = inverse_of(x_ref[...].astype(F32))

    def write(t, value):
        scratch[:, tile(t)] = value * gain_ref[:, tile(t)] if scaled else value

    def read(i):
        return a_ref[:, tile(i)].astype(F32) + b_ref[:, tile(i)].astype(F32)

    order.from_tiles(read, write, mine)
    normed = x_ref[...].astype(F32) * inverse
    scaled = scratch[...]
    shared = jnp.mean(scaled * normed, -1, keepdims=True)
    total = g_ref[...].astype(F32) + inverse * (scaled - normed * shared)
    outs[0][...] = total
    if len(outs) == 3:
        outs[1][...] = total.astype(BF)


def norm_back(order, x, g, a, b, gain=None, low=False):
    rows, width = x.shape
    scaled = gain is not None
    if not order.fast:
        x = x.astype(F32)
        inverse = inverse_of(x)
        normed = x * inverse
        grad = a.astype(F32) + b.astype(F32)
        grad = order.from_rel(grad)
        grad = grad * gain if scaled else grad
        shared = jnp.mean(grad * normed, -1, keepdims=True)
        total = g.astype(F32) + inverse * (grad - normed * shared)
        return (total, total.astype(BF)) if low else (total,)
    specs = row_specs(6, rows, width, 2)
    outs = [shape_of((rows, width), F32)] + ([shape_of((rows, width), BF)] if low else [])
    return run(
        functools.partial(back_kernel, order, scaled),
        [order.mine, x, g, a, b] + ([gain] if scaled else []),
        outs,
        [SMEM] + specs[:4] + [pl.BlockSpec((1, width), lambda i: (0, 0))] * scaled,
        specs[: len(outs)],
        (2,),
        scratch=[pltpu.VMEM((rows // 2, width), F32)],
    )


def result_kernel(order, mine_ref, mid_ref, a_ref, b_ref, out_ref):
    mine = [mine_ref[i] for i in range(5)]

    def write(t, value):
        out_ref[:, tile(t)] = (mid_ref[:, tile(t)] + value).astype(BF)

    order.from_tiles(
        lambda i: a_ref[:, tile(i)].astype(F32) + b_ref[:, tile(i)].astype(F32), write, mine
    )


def result_of(order, mid, a, b):
    rows, width = mid.shape
    if not order.fast:
        return (mid + order.from_rel(a.astype(F32) + b.astype(F32))).astype(BF)
    specs = row_specs(4, rows, width, 2)
    return run(
        functools.partial(result_kernel, order),
        [order.mine, mid, a, b],
        [shape_of((rows, width), BF)],
        [SMEM] + specs[:3],
        specs[:1],
        (2,),
    )[0]


def pack_kernel(count, kinds, *refs):
    out_ref = refs[-1]
    cols = out_ref.shape[-1]
    depth = refs[0].shape[0]
    for m in range(kinds):
        value = refs[m][...].astype(F32)
        if len(refs) > kinds + 1:
            value = value * refs[kinds][...]
        for t in range(count):
            out_ref[t, m * depth : (m + 1) * depth] = value[:, t * cols : (t + 1) * cols].astype(BF)


def pack(weights, gain, count):
    depth, width = weights[0].shape
    return run(
        functools.partial(pack_kernel, count, len(weights)),
        weights + ([] if gain is None else [gain]),
        [shape_of((count, len(weights) * depth, width // count), BF)],
    )[0]


def unpack_kernel(count, kinds, scaled, *refs):
    p_ref = refs[0]
    cols = p_ref.shape[-1]
    depth = p_ref.shape[1] // kinds
    outs = refs[-kinds - 1 : -1] if scaled else refs[-kinds:]
    total = jnp.zeros((depth, 1), F32)
    for m in range(kinds):
        for t in range(count):
            part = p_ref[t, m * depth : (m + 1) * depth].astype(F32)
            lanes = slice(t * cols, (t + 1) * cols)
            if scaled:
                total = total + jnp.sum(part * refs[1 + m][:, lanes].astype(F32), -1, keepdims=True)
                part = part * refs[1 + kinds][...]
            outs[m][:, lanes] = part
    if scaled:
        refs[-1][...] = total


def unpack(parts, weights, gain):
    count, depth, cols = parts.shape
    if gain is None:
        outs = [shape_of((depth, count * cols), F32)]
        return run(functools.partial(unpack_kernel, count, 1, False), [parts], outs)
    kinds = len(weights)
    outs = [shape_of((depth // kinds, count * cols), F32)] * kinds + [shape_of((depth // kinds, 1), F32)]
    return run(functools.partial(unpack_kernel, count, kinds, True), [parts] + weights + [gain], outs)


def pack_qkv_kernel(count, me_ref, q_ref, k_ref, v_ref, out_ref):
    for t in range(count):
        slot = me_ref[0] ^ t
        out_ref[slot, :, :HEAD_COLS] = q_ref[:, t * HEAD_COLS : (t + 1) * HEAD_COLS]
        lanes = slice(t * HEAD_DIM, (t + 1) * HEAD_DIM)
        both = jnp.concatenate([k_ref[:, lanes].astype(F32), v_ref[:, lanes].astype(F32)], -1)
        out_ref[slot, :, HEAD_COLS:] = both.astype(BF)


def place_kernel(count, me_ref, *refs):
    for r in range(count):
        refs[-1][me_ref[0] ^ r] = refs[r][...]


def columns_kernel(kinds, in_ref, *outs):
    count, depth, units = in_ref.shape
    depth = depth // kinds
    step = max(1, 128 // depth)
    for m in range(kinds):
        for t in range(0, count, step):
            rows = [in_ref[t + i, m * depth : (m + 1) * depth] for i in range(step)]
            both = jnp.concatenate(rows, 0).astype(F32)
            outs[m][:, t * depth : (t + step) * depth] = both.T.astype(BF)


def rows_kernel(kinds, depth, *refs):
    out_ref = refs[-1]
    count = out_ref.shape[0]
    units = out_ref.shape[2]
    step = max(1, 128 // depth)
    for m in range(kinds):
        for t in range(0, count, step):
            lanes = slice(t * depth, (t + step) * depth)
            both = sum(r[m * units : (m + 1) * units, lanes].astype(F32) for r in refs[:-1]).T
            for i in range(step):
                out_ref[t + i, m * depth : (m + 1) * depth] = both[i * depth : (i + 1) * depth].astype(BF)


def unpack_qkv_kernel(count, q_ref, k_ref, v_ref, g_ref, p_ref, qo_ref, ko_ref, vo_ref, sum_ref):
    gain = g_ref[...]
    total = jnp.zeros_like(gain)
    for t in range(count):
        part = p_ref[t].astype(F32)
        lanes = slice(t * HEAD_COLS, (t + 1) * HEAD_COLS)
        thin = slice(t * HEAD_DIM, (t + 1) * HEAD_DIM)
        gq = part[:, :HEAD_COLS]
        gk = part[:, HEAD_COLS : HEAD_COLS + HEAD_DIM]
        gv = part[:, HEAD_COLS + HEAD_DIM :]
        total = total + jnp.sum(gq * q_ref[:, lanes].astype(F32), -1, keepdims=True)
        total = total + jnp.sum(gk * k_ref[:, thin].astype(F32), -1, keepdims=True)
        total = total + jnp.sum(gv * v_ref[:, thin].astype(F32), -1, keepdims=True)
        qo_ref[:, lanes] = gq
        ko_ref[:, thin] = gk
        vo_ref[:, thin] = gv
    sum_ref[...] = total / gain


def swap_halves(values):
    width = values.shape[-1]
    lanes = lax.broadcasted_iota(jnp.int32, (1, width), 1)
    return jnp.where(
        lanes % HEAD_DIM < HEAD_DIM // 2,
        pltpu.roll(values, width - HEAD_DIM // 2, 1),
        pltpu.roll(values, HEAD_DIM // 2, 1),
    )


def project_kernel(repeat, count, *refs):
    a_ref, cos_ref, sin_ref = refs[:3]
    w_refs, q_ref, kv_ref = refs[3 : 3 + count], refs[-2], refs[-1]
    piece = w_refs[0].shape[0]
    raw = None
    for k in range(count):
        term = dot(a_ref[:, k * piece : (k + 1) * piece], w_refs[k][...])
        raw = term if raw is None else raw + term
    cosine = jnp.concatenate([cos_ref[...]] * repeat, 0)
    sine = jnp.concatenate([sin_ref[...]] * repeat, 0)
    out = (raw * cosine + swap_halves(raw) * sine).astype(BF)
    q_ref[...] = out[:, :HEAD_COLS]
    kv_ref[...] = out[:, HEAD_COLS:]


def project(a1, cosine, sine, parts):
    rows, width = a1.shape
    seq_dev, cols = cosine.shape
    block = min(2 * seq_dev, rows)
    fixed = lambda i: (0, 0)
    moving = lambda i: (i, 0)
    return run(
        functools.partial(project_kernel, block // seq_dev, len(parts)),
        [a1, cosine, sine] + parts,
        [shape_of((rows, HEAD_COLS), BF), shape_of((rows, 2 * HEAD_DIM), BF)],
        [pl.BlockSpec((block, width), moving)]
        + [pl.BlockSpec((seq_dev, cols), fixed)] * 2
        + [pl.BlockSpec(p.shape, fixed) for p in parts],
        [pl.BlockSpec((block, HEAD_COLS), moving), pl.BlockSpec((block, 2 * HEAD_DIM), moving)],
        (rows // block,),
        flops=2 * rows * width * cols,
    )


def stack_heads(values):
    return jnp.concatenate(
        [values[:, j * HEAD_DIM : (j + 1) * HEAD_DIM] for j in range(GROUPS)], 0
    )


def soft_weights(queries, keys, key_ref, seq_dev):
    scores = dot_nt(queries, keys) * FACTOR
    place = lax.broadcasted_iota(jnp.int32, (queries.shape[0], 1), 0) % seq_dev
    return jnp.where(place >= key_ref[...], jnp.exp(scores), 0.0)


def attend_kernel(q_ref, kv_ref, key_ref, o_ref):
    seq_dev = q_ref.shape[0]
    both = kv_ref[...].reshape(-1, 2 * HEAD_DIM)
    keys, values = both[:, :HEAD_DIM], both[:, HEAD_DIM:]
    weights = soft_weights(stack_heads(q_ref[...]), keys, key_ref, seq_dev)
    totals = jnp.sum(weights, -1, keepdims=True)
    attended = dot(weights.astype(BF), values) / totals
    for j in range(GROUPS):
        rows = attended[j * seq_dev : (j + 1) * seq_dev]
        o_ref[:, j * HEAD_DIM : (j + 1) * HEAD_DIM] = rows.astype(BF)


def attend(queries, kv, key_places, seq_dev):
    rows = queries.shape[0]
    count, seqs = kv.shape[:2]
    return run(
        attend_kernel,
        [queries, kv, key_places],
        [shape_of((rows, HEAD_COLS), BF)],
        [
            pl.BlockSpec((seq_dev, HEAD_COLS), lambda s: (s, 0)),
            pl.BlockSpec((count, 1, seq_dev, 2 * HEAD_DIM), lambda s: (0, s, 0, 0)),
            pl.BlockSpec((1, count * seq_dev), lambda s: (0, 0)),
        ],
        [pl.BlockSpec((seq_dev, HEAD_COLS), lambda s: (s, 0))],
        (seqs,),
        flops=4 * rows * GROUPS * HEAD_DIM * count * seq_dev,
    )[0]


def attend_back_kernel(q_ref, kv_ref, key_ref, do_ref, cos_ref, sin_ref, dq_ref, dkv_ref, mid_ref):
    seq_dev = q_ref.shape[0]
    both = kv_ref[...].reshape(-1, 2 * HEAD_DIM)
    keys, values = both[:, :HEAD_DIM], both[:, HEAD_DIM:]
    queries = stack_heads(q_ref[...])
    weights = soft_weights(queries, keys, key_ref, seq_dev)
    totals = jnp.sum(weights, -1, keepdims=True)
    low = weights.astype(BF)
    attended = dot(low, values) / totals
    grads = stack_heads(do_ref[...])
    deltas = jnp.sum(grads * attended, -1, keepdims=True) / totals
    mixed = (grads / totals).astype(BF)
    scores = (weights * (dot_nt(mixed, values) - deltas)).astype(BF)
    turned = dot(scores, keys) * FACTOR
    for j in range(GROUPS):
        mid_ref[:, j * HEAD_DIM : (j + 1) * HEAD_DIM] = turned[j * seq_dev : (j + 1) * seq_dev]
    whole = mid_ref[...]
    dq_ref[...] = (whole * cos_ref[...] - swap_halves(whole) * sin_ref[...]).astype(BF)
    grad_keys = dot_tn(scores, queries) * FACTOR
    grad_values = dot_tn(low, mixed)
    joined = jnp.concatenate([grad_keys, grad_values], -1)
    dkv_ref[...] = joined.astype(BF).reshape(dkv_ref.shape)


def attend_back(queries, kv, key_places, grads, cosine, sine, seq_dev):
    rows = queries.shape[0]
    count, seqs = kv.shape[:2]
    own = pl.BlockSpec((seq_dev, HEAD_COLS), lambda s: (s, 0))
    table = pl.BlockSpec((seq_dev, HEAD_COLS), lambda s: (0, 0))
    blocks = pl.BlockSpec((count, 1, seq_dev, 2 * HEAD_DIM), lambda s: (0, s, 0, 0))
    return run(
        attend_back_kernel,
        [queries, kv, key_places, grads, cosine, sine],
        [shape_of((rows, HEAD_COLS), BF), shape_of(kv.shape, BF)],
        [own, blocks, pl.BlockSpec((1, count * seq_dev), lambda s: (0, 0)), own, table, table],
        [own, blocks],
        (seqs,),
        scratch=[pltpu.VMEM((seq_dev, HEAD_COLS), F32)],
        flops=14 * rows * GROUPS * HEAD_DIM * count * seq_dev,
    )


def turn_back_kernel(repeat, a_ref, b_ref, cos_ref, sin_ref, out_ref):
    total = a_ref[...].astype(F32) + b_ref[...].astype(F32)
    cosine = jnp.concatenate([cos_ref[...]] * repeat, 0)
    sine = jnp.concatenate([sin_ref[...]] * repeat, 0)
    out_ref[...] = (total * cosine - swap_halves(total) * sine).astype(BF)


def wide_kernel(product, left_ref, *refs):
    rights, out_ref = refs[:-1], refs[-1]
    cols = out_ref.shape[1] // len(rights)
    for k, right in enumerate(rights):
        out_ref[:, k * cols : (k + 1) * cols] = product(left_ref[...], right[...]).astype(BF)


def wide(product, left, rights, width, block):
    rows, depth = left.shape
    return run(
        functools.partial(wide_kernel, product),
        [left] + rights,
        [shape_of((rows, width), BF)],
        [pl.BlockSpec((block, depth), lambda i: (i, 0))]
        + [pl.BlockSpec(r.shape, lambda i: (0, 0)) for r in rights],
        [pl.BlockSpec((block, width), lambda i: (i, 0))],
        (rows // block,),
        vmem=48,
        flops=2 * rows * depth * width,
    )[0]


def gate_kernel(a_ref, gate_ref, up_ref, hid_ref, one_ref, two_ref):
    units, cols = hid_ref.shape[1], gate_ref.shape[1]
    gate = up = None
    for k in range(a_ref.shape[1] // cols):
        part = a_ref[:, k * cols : (k + 1) * cols]
        g = dot_nt(part, gate_ref[k * units : (k + 1) * units])
        u = dot_nt(part, up_ref[k * units : (k + 1) * units])
        gate = g if gate is None else gate + g
        up = u if up is None else up + u
    sigmoid = jax.nn.sigmoid(gate)
    active = gate * sigmoid
    hid_ref[...] = (active * up).astype(BF)
    one_ref[...] = up * sigmoid * (1.0 + gate * (1.0 - sigmoid))
    two_ref[...] = active


def gate_up(a2, gate, up, units, block):
    rows, width = a2.shape
    moving = lambda i: (i, 0)
    out = pl.BlockSpec((block, units), moving)
    return run(
        gate_kernel,
        [a2, gate, up],
        [shape_of((rows, units), BF), shape_of((rows, units), F32), shape_of((rows, units), F32)],
        [pl.BlockSpec((block, width), moving)] + [pl.BlockSpec(gate.shape, lambda i: (0, 0))] * 2,
        [out, out, out],
        (rows // block,),
        vmem=48,
    )


def hidden_kernel(g_ref, one_ref, two_ref, down_ref, gate_ref, up_ref, dboth_ref, out_ref):
    units, cols = one_ref.shape[1], down_ref.shape[1]
    pieces = g_ref.shape[1] // cols
    total = None
    for k in range(pieces):
        term = dot_nt(g_ref[:, k * cols : (k + 1) * cols], down_ref[k * units : (k + 1) * units])
        total = term if total is None else total + term
    dgate = (total * one_ref[...]).astype(BF)
    dup = (total * two_ref[...]).astype(BF)
    dboth_ref[:, :units] = dgate
    dboth_ref[:, units:] = dup
    for k in range(pieces):
        part = dot(dgate, gate_ref[k * units : (k + 1) * units])
        part = part + dot(dup, up_ref[k * units : (k + 1) * units])
        out_ref[:, k * cols : (k + 1) * cols] = part.astype(BF)


def hidden_back(gb, one, two, down, gate, up, block):
    rows, width = gb.shape
    units = one.shape[1]
    moving = lambda i: (i, 0)
    fixed = lambda i: (0, 0)
    thin = pl.BlockSpec((block, units), moving)
    full = pl.BlockSpec((block, width), moving)
    return run(
        hidden_kernel,
        [gb, one, two, down, gate, up],
        [shape_of((rows, 2 * units), BF), shape_of((rows, width), BF)],
        [full, thin, thin] + [pl.BlockSpec(down.shape, fixed)] * 3,
        [pl.BlockSpec((block, 2 * units), moving), full],
        (rows // block,),
        vmem=56,
    )


def result_rows_kernel(h_ref, down_ref, out_ref):
    units, cols = h_ref.shape[1], down_ref.shape[1]
    for k in range(out_ref.shape[1] // cols):
        part = dot(h_ref[...], down_ref[k * units : (k + 1) * units])
        out_ref[:, k * cols : (k + 1) * cols] = part.astype(BF)


def result_rows(hidden, down, width, block):
    rows, units = hidden.shape
    moving = lambda i: (i, 0)
    return run(
        result_rows_kernel,
        [hidden, down],
        [shape_of((rows, width), BF)],
        [pl.BlockSpec((block, units), moving), pl.BlockSpec(down.shape, lambda i: (0, 0))],
        [pl.BlockSpec((block, width), moving)],
        (rows // block,),
    )[0]


def weight_grad_kernel(left_ref, right_ref, out_ref):
    out_ref[...] = dot_tn(left_ref[...], right_ref[...]).astype(BF)


def weight_grad(left, right, pieces):
    rows, units = left.shape
    cols = right.shape[1] // pieces
    return run(
        weight_grad_kernel,
        [left, right],
        [shape_of((pieces * units, cols), BF)],
        [pl.BlockSpec((rows, units), lambda i: (0, 0)), pl.BlockSpec((rows, cols), lambda i: (0, i))],
        [pl.BlockSpec((units, cols), lambda i: (i, 0))],
        (pieces,),
        vmem=48,
    )[0]


def gather_rows(value, bits, what):
    acc = value
    for bit in bits:
        acc = jnp.concatenate([acc, bit.swap(acc, what)], 0)
    return acc


def reduce_rows(acc, bits, what, last_after=()):
    for bit in list(reversed(bits))[:-1]:
        half = acc.shape[0] // 2
        got = bit.swap(acc[half:], what)
        acc = (acc[:half].astype(F32) + got.astype(F32)).astype(BF)
    half = acc.shape[0] // 2
    last = after(acc[half:], *last_after) if last_after else acc[half:]
    return acc[:half], bits[0].swap(last, what)


def gather_team(value, bit_x, near, bit_core, what, marks):
    half = value.shape[0] // 2
    by_x, by_near = bit_x.swap(value, what), near.swap(value, what)
    diagonal = [bit_x.swap(by_near[:half], what), near.swap(by_x[half:], what)]
    four = after(jnp.concatenate([value, by_x, by_near] + diagonal, 0), *marks)
    return jnp.concatenate([four, bit_core.swap(four, what)], 0)


def add_low(a, b):
    return (a.astype(F32) + b.astype(F32)).astype(BF)


def reduce_team(acc, bit_x, near, bit_core, what):
    half = acc.shape[0] // 2
    return reduce_four(acc[:half], bit_core.swap(acc[half:], what), bit_x, near, what)


def reduce_four(acc, got, bit_x, near, what):
    half = acc.shape[0]
    acc = add_low(acc, got)
    rows = half // 4
    own, by_x, by_near = acc[:rows], acc[rows : 2 * rows], acc[2 * rows : 3 * rows]
    first, second = acc[3 * rows : 3 * rows + rows // 2], acc[3 * rows + rows // 2 :]
    got_near = bit_x.swap(first, what)
    got_x = near.swap(second, what)
    by_near = jnp.concatenate([add_low(by_near[: rows // 2], got_near), by_near[rows // 2 :]], 0)
    by_x = jnp.concatenate([by_x[: rows // 2], add_low(by_x[rows // 2 :], got_x)], 0)
    return (add_low(own, bit_x.swap(by_x, what)), near.swap(by_near, what)), by_x


def absolute(blocks, index, bits):
    def one(j):
        other = index ^ j
        slot = sum(((other >> b.bit) & 1) << i for i, b in enumerate(bits))
        return lax.dynamic_index_in_dim(blocks, slot, 0, False)

    return jnp.stack([one(j) for j in range(blocks.shape[0])])


def relative(blocks, index, bits):
    def one(r):
        code = sum(((r >> i) & 1) << b.bit for i, b in enumerate(bits))
        return lax.dynamic_index_in_dim(blocks, index ^ code, 0, False)

    return jnp.stack([one(r) for r in range(blocks.shape[0])])


def shards(
    dp,
    ctx,
    tokens,
    cotangent,
    attn_gain,
    query_weight,
    key_weight,
    value_weight,
    output_weight,
    mlp_gain,
    gate_weight,
    up_weight,
    down_weight,
):
    seqs, seq_dev, width = tokens.shape
    rows = seqs * seq_dev
    depth = query_weight.shape[0]
    c_index = lax.axis_index("ctx")

    bit_x, bit_core = Bit("dp", 1, dp), Bit("dp", 0, dp)
    ctx_bits = [Bit("ctx", b, ctx) for b in reversed(range(ctx.bit_length() - 1))]
    near = ctx_bits[-1]
    far = [b for b in ctx_bits if b is not near]
    dp_bits = [bit_x, bit_core]
    names = dp_bits + ctx_bits
    attn_order = Order(names, list(reversed(ctx_bits)) + dp_bits, ctx_bits, depth)
    mlp_order = Order(names, far + dp_bits + [near], [], depth)
    x = tokens.reshape(rows, width)
    cot = cotangent.reshape(rows, width)
    gain_one = attn_gain.astype(F32)[:, None]
    gain_two = mlp_gain.astype(F32)[:, None]

    team_groups = []
    for c in range(ctx):
        if not (c >> near.bit) & 1:
            team_groups.append([d * ctx + (c | (n << near.bit)) for d in range(dp) for n in range(2)])
    team = 2 * dp

    def mlp_trade(parts):
        return lax.all_to_all(
            parts, ("dp", "ctx"), 0, 0, axis_index_groups=team_groups, tiled=True
        )

    def mlp_slices(weights, gain, *marks):
        kinds = len(weights)
        parts = after(mlp_trade(pack(weights, gain, team)), *marks)
        shape = (parts.shape[2], team * depth)
        return run(functools.partial(columns_kernel, kinds), [parts], [shape_of(shape, BF)] * kinds)

    def mlp_rows(sums, kinds):
        shape = (team, kinds * depth, sums[0].shape[0] // kinds)
        return mlp_trade(run(functools.partial(rows_kernel, kinds, depth), sums, [shape_of(shape, BF)])[0])

    far_groups = []
    for n in range(2):
        far_groups.append([c for c in range(ctx) if (c >> near.bit) & 1 == n])
    pieces = ctx // 2

    def far_gather(own):
        return lax.all_gather(own, "ctx", axis=0, tiled=True, axis_index_groups=far_groups)

    def far_reduce(terms):
        return lax.psum_scatter(
            terms, "ctx", scatter_dimension=0, tiled=True, axis_index_groups=far_groups
        )

    qkv_cols = HEAD_COLS + 2 * HEAD_DIM
    me = lax.axis_index("dp").astype(jnp.int32).reshape(1)
    slices = run(
        functools.partial(pack_qkv_kernel, dp),
        [me, query_weight, key_weight, value_weight],
        [shape_of((dp, depth, qkv_cols), BF)],
        [SMEM] + [pl.BlockSpec(memory_space=pltpu.VMEM)] * 3,
    )[0]
    out_acc = [output_weight]
    for bit in ctx_bits[:-1]:
        out_acc.append(jnp.concatenate([out_acc[-1], bit.swap(out_acc[-1], "out")], 0))
    slices = [slices[0]] + [swap_difference(slices[r], "dp", dp, r, "slice") for r in range(1, dp)]
    own = run(
        functools.partial(place_kernel, dp),
        [me, after(slices[0], out_acc[1])] + slices[1:],
        [shape_of((dp, depth, qkv_cols), BF)],
        [SMEM] + [pl.BlockSpec(memory_space=pltpu.VMEM)] * dp,
    )[0].reshape(dp * depth, qkv_cols)
    halves = [own]
    for i, bit in enumerate(ctx_bits[:-1]):
        sent = halves[-1] if i == 0 else after(halves[-1], out_acc[i + 1])
        halves.append(jnp.concatenate([sent, bit.swap(sent, "qkv")], 0))
    qkv = [halves[-1], ctx_bits[-1].swap(halves[-1], "qkv")]
    out_rel = after(out_acc[-1], qkv[1])
    out_rel = jnp.concatenate([out_rel, ctx_bits[-1].swap(out_rel, "out")], 0)
    out_full = absolute(out_rel.reshape(ctx, depth, width), c_index, ctx_bits)
    out_full = out_full.reshape(ctx * depth, width)

    gain_all = jnp.broadcast_to(after(attn_gain, own)[None], (dp * ctx, depth))
    gain_all = lax.all_to_all(gain_all, ("dp", "ctx"), 0, 0, tiled=True)
    gain_all = gain_all.reshape(1, width).astype(F32)
    a1_half = gather_rows(norm_to(attn_order, x, gain_all), dp_bits[:1], "a1")
    a1 = gather_rows(a1_half, dp_bits[1:], "a1")
    gate_own, up_own = mlp_slices([after(gate_weight, halves[1]), up_weight], gain_two, halves[-1], a1_half)
    gate = far_gather(gate_own)
    (down_own,) = mlp_slices([after(down_weight.T, gate_own)], None)
    units = down_own.shape[0]

    places = jnp.arange(seq_dev, dtype=jnp.int32)
    half_dim = HEAD_DIM // 2
    freqs = rope_base ** (-(jnp.arange(half_dim, dtype=F32) * 2.0) / HEAD_DIM)
    angles = (c_index * seq_dev + places).astype(F32)[:, None] * freqs[None, :]
    cosine, sine = jnp.cos(angles), jnp.sin(angles)
    cosine = jnp.concatenate([cosine, cosine] * (GROUPS + 1) + [jnp.ones((seq_dev, HEAD_DIM), F32)], -1)
    sine = jnp.concatenate([-sine, sine] * (GROUPS + 1) + [jnp.zeros((seq_dev, HEAD_DIM), F32)], -1)
    rel = jnp.arange(ctx, dtype=jnp.int32)
    others = sum(((rel >> i) & 1) << b.bit for i, b in enumerate(ctx_bits)) ^ c_index
    key_places = (((others - c_index) * seq_dev)[:, None] + places[None, :]).reshape(1, -1)

    queries, kv_own = project(a1, cosine, sine, qkv)
    all_seqs = dp * seqs
    kv = kv_own
    for i, bit in enumerate(ctx_bits):
        if i == 1:
            kv = after(kv, down_own)
        if i == len(ctx_bits) - 1:
            up = far_gather(after(up_own, kv))
            down = far_gather(after(down_own, kv))
        kv = jnp.concatenate([kv, bit.swap(kv, "kv")], 0)
    gb = gather_team(order_to(mlp_order, after(cot, qkv[1])), bit_x, near, bit_core, "gb", [])
    kv = kv.reshape(ctx, all_seqs, seq_dev, 2 * HEAD_DIM)
    heads = attend(queries, after(kv, gb), key_places, seq_dev)
    branch = dot(heads, out_full).astype(BF)
    branch = reduce_rows(branch, dp_bits, "branch")
    middle, a2 = middle_to(mlp_order, x, *branch)

    a2 = gather_team(a2, bit_x, near, bit_core, "a2", [])
    block = min(256, a2.shape[0])
    hidden, one, two = gate_up(a2, gate, up, units, block)
    down_back = far_reduce(weight_grad(hidden, gb, pieces))
    dboth, da2 = hidden_back(gb, one, two, down, gate, up, block)
    half = da2.shape[0] // 2
    da2_got = bit_core.swap(da2[half:], "da2")
    da2_two, da2_mark = reduce_four(da2[:half], da2_got, bit_x, near, "da2")
    both_back = far_reduce(weight_grad(dboth, after(a2, da2_mark), pieces))
    grad_middle, db = norm_back(mlp_order, middle, cot, *da2_two, low=True)
    grad_branch = gather_rows(db, dp_bits, "db")

    grad_heads = dot_nt(grad_branch, out_full)
    dq, dkv = attend_back(
        queries, kv, key_places, grad_heads, cosine[:, :HEAD_COLS], sine[:, :HEAD_COLS], seq_dev
    )

    dkv_steps = []
    acc = dkv.reshape(-1, 2 * HEAD_DIM)
    for bit in reversed(ctx_bits):
        half = acc.shape[0] // 2
        dkv_steps.append((acc[:half], bit.swap(acc[half:], "dkv")))
        acc = add_low(*dkv_steps[-1])
    dkv_two = dkv_steps[-1]
    dkv_first, dkv_last = dkv_steps[0][1], dkv_steps[-1][1]

    down_back = mlp_rows([after(down_back, dq)], 1)
    down_out = result_rows(after(hidden, dq), down, width, block)
    result_two = reduce_team(down_out, bit_x, near, bit_core, "result")[0]
    result = result_of(mlp_order, middle, *result_two)
    both_back = mlp_rows([after(both_back, dkv_last, *result_two)], 2)
    dkv_low = run(
        functools.partial(turn_back_kernel, all_seqs),
        list(dkv_two) + [cosine[:, HEAD_COLS:], sine[:, HEAD_COLS:]],
        [shape_of((dp * rows, 2 * HEAD_DIM), BF)],
    )[0]
    draw = jnp.concatenate([dq, dkv_low], -1)
    da1 = wide(dot_nt, draw, qkv, width, min(256, dp * rows))
    da1_two = reduce_rows(da1, dp_bits, "da1")
    (grad_tokens,) = norm_back(attn_order, x, grad_middle, *da1_two, gain_all)
    q_total = add_low(*reduce_rows(dot_tn(a1, dq).astype(BF), ctx_bits, "dq_w", [down_back]))
    kv_total = add_low(*reduce_rows(
        dot_tn(a1, dkv_low).astype(BF), ctx_bits, "dkv_w", [*da1_two]
    ))
    out_total = dot_tn(heads, grad_branch).astype(BF).reshape(ctx, depth, width)
    out_total = relative(after(out_total, dkv_steps[1][1]), c_index, ctx_bits).reshape(ctx * depth, width)
    out_two = reduce_rows(out_total, ctx_bits, "dout_w")
    qkv_total = jnp.concatenate([q_total, kv_total], -1).reshape(dp, depth, qkv_cols)
    qkv_back = lax.all_to_all(qkv_total, "dp", 0, 0, tiled=True)
    output_grad = out_two[0].astype(F32) + out_two[1].astype(F32)

    gate_grad, up_grad, mlp_sum = unpack(both_back, [gate_weight, up_weight], gain_two)
    down_grad = unpack(down_back, None, None)[0].T
    query_grad, key_grad, value_grad, attn_sum = run(
        functools.partial(unpack_qkv_kernel, dp),
        [query_weight, key_weight, value_weight, gain_one, qkv_back],
        [shape_of(w.shape, F32) for w in (query_weight, key_weight, value_weight, gain_one)],
    )
    return (
        result.reshape(seqs, seq_dev, width),
        grad_tokens.reshape(seqs, seq_dev, width),
        attn_sum[:, 0],
        query_grad,
        key_grad,
        value_grad,
        output_grad,
        mlp_sum[:, 0],
        gate_grad,
        up_grad,
        down_grad,
    )


def solution(mesh):
    dp, ctx = mesh.shape["dp"], mesh.shape["ctx"]

    def local(*args):
        return shards(dp, ctx, *args)

    weight = P(("dp", "ctx"), None)
    flat = P(("dp", "ctx"))
    acts = P("dp", "ctx", None)
    down = P(None, ("dp", "ctx"))
    return jax.shard_map(
        local,
        mesh=mesh,
        in_specs=(acts, acts, flat, weight, weight, weight, weight, flat, weight, weight, down),
        out_specs=(acts, acts, flat, weight, weight, weight, weight, flat, weight, weight, down),
        check_vma=False,
    )
```

```python
import functools
import math

import jax
import jax.numpy as jnp
from jax import lax
from jax.experimental import pallas as pl
from jax.experimental.pallas import tpu as pltpu
from jax.sharding import PartitionSpec as P

HEADS = 32
KV_HEADS = 4
HEAD_DIM = 64
GROUPS = HEADS // KV_HEADS
HEAD_COLS = GROUPS * HEAD_DIM
FACTOR = 1.0 / math.sqrt(HEAD_DIM)

norm_eps = 1e-05
rope_base = 10000.0

BF = jnp.bfloat16
F32 = jnp.float32
MIB = 1 << 20


def dot(left, right):
    return jnp.dot(left, right, preferred_element_type=F32)


def dot_nt(left, right):
    return lax.dot_general(left, right, (((1,), (1,)), ((), ())), preferred_element_type=F32)


def dot_tn(left, right):
    return lax.dot_general(left, right, (((0,), (0,)), ((), ())), preferred_element_type=F32)


def shape_of(shape, kind):
    return jax.ShapeDtypeStruct(shape, kind)


def run(kernel, ins, outs, specs=None, out_specs=None, grid=None, vmem=32, scratch=(), flops=0):
    whole = pl.BlockSpec(memory_space=pltpu.VMEM)
    moved = sum(math.prod(a.shape) * a.dtype.itemsize for a in list(ins) + list(outs))
    extra = {} if grid is None else {"grid": grid}
    name = kernel.func.__name__ if isinstance(kernel, functools.partial) else kernel.__name__
    return pl.pallas_call(
        kernel,
        name=name,
        out_shape=list(outs),
        in_specs=specs or [whole] * len(ins),
        out_specs=out_specs or [whole] * len(outs),
        scratch_shapes=list(scratch),
        compiler_params=pltpu.CompilerParams(vmem_limit_bytes=vmem * MIB),
        cost_estimate=pl.CostEstimate(flops=0, bytes_accessed=0, transcendentals=0),
        **extra,
    )(*ins)


SMEM = pl.BlockSpec(memory_space=pltpu.SMEM)


class Bit:
    def __init__(self, axis, bit, size):
        self.axis, self.bit = axis, bit
        self.pairs = [(i, i ^ (1 << bit)) for i in range(size)]

    def mine(self):
        return (lax.axis_index(self.axis) >> self.bit) & 1

    def swap(self, value, what):
        with jax.named_scope(f"{what}_{self.axis}{self.bit}"):
            return lax.ppermute(value, self.axis, self.pairs)


def swap_difference(value, axis, size, difference, what):
    with jax.named_scope(f"{what}_{axis}"):
        return lax.ppermute(value, axis, [(i, i ^ difference) for i in range(size)])


def after(value, *others):
    return lax.optimization_barrier((value,) + others)[0]


class Order:
    def __init__(self, names, rel, gathered, depth):
        self.names, self.rel, self.gathered, self.depth = names, rel, gathered, depth
        self.whole_tiles = rel[-1] is names[-1] and not gathered
        self.fast = depth == 64 and len(names) == 5 and (
            self.whole_tiles or (rel[-1] is not names[-1] and rel[-1] not in gathered)
        )
        self.mine = jnp.stack(
            [b.mine() if b in gathered else jnp.zeros((), jnp.int32) for b in names]
        ).astype(jnp.int32)

    def to_tiles(self, read, write, mine):
        lanes = lax.broadcasted_iota(jnp.int32, (1, 128), 1)
        head = self.rel[:-1]
        last = self.rel[-1]
        for q in range(16):
            value = {b: (q >> (3 - i)) & 1 for i, b in enumerate(head)}
            if self.whole_tiles:
                write(q, read(sum(value[b] << (3 - i) for i, b in enumerate(self.names[:-1]))))
                continue

            def source(low):
                index = 0
                for i, b in enumerate(self.names[:-1]):
                    v = low if b is last else value[b]
                    if b in self.gathered:
                        v = v ^ mine[i]
                    index = index * 2 + v
                return read(index)

            a, b = source(0), source(1)
            side = value[self.names[-1]]
            low = lambda: jnp.where(lanes < 64, a, pltpu.roll(b, 64, 1))
            high = lambda: jnp.where(lanes < 64, pltpu.roll(a, 64, 1), b)
            if self.names[-1] in self.gathered:
                write(q, jnp.where((side ^ mine[4]) == 0, low(), high()))
            else:
                write(q, low() if side == 0 else high())

    def from_tiles(self, read, write, mine):
        lanes = lax.broadcasted_iota(jnp.int32, (1, 128), 1)
        for t in range(16):
            value = {b: (t >> (3 - i)) & 1 for i, b in enumerate(self.names[:-1])}
            if self.whole_tiles:
                write(t, read(sum(value[b] << (3 - i) for i, b in enumerate(self.rel[:-1]))))
                continue

            def source(y):
                index = 0
                for b in self.rel[:-1]:
                    v = y if b is self.names[-1] else value[b]
                    if b in self.gathered:
                        v = v ^ mine[self.names.index(b)]
                    index = index * 2 + v
                return read(index)

            low, high = source(0), source(1)
            if value[self.rel[-1]] == 0:
                write(t, jnp.where(lanes < 64, low, pltpu.roll(high, 64, 1)))
            else:
                write(t, jnp.where(lanes < 64, pltpu.roll(low, 64, 1), high))

    def to_rel(self, array):
        count, width = array.shape
        out = array.reshape((count,) + (2,) * len(self.names) + (self.depth,))
        for b in self.gathered:
            k = self.names.index(b) + 1
            out = jnp.where(b.mine() == 1, jnp.flip(out, k), out)
        axes = [self.names.index(b) + 1 for b in self.rel]
        return out.transpose([0] + axes + [len(self.names) + 1]).reshape(count, width)

    def from_rel(self, array):
        count, width = array.shape
        out = array.reshape((count,) + (2,) * len(self.names) + (self.depth,))
        axes = [self.rel.index(b) + 1 for b in self.names]
        out = out.transpose([0] + axes + [len(self.names) + 1])
        for b in self.gathered:
            k = self.names.index(b) + 1
            out = jnp.where(b.mine() == 1, jnp.flip(out, k), out)
        return out.reshape(count, width)


def tile(index):
    start = index * 128
    return pl.ds(start if isinstance(start, int) else pl.multiple_of(start, 128), 128)


def row_specs(count, rows, width, steps):
    return [pl.BlockSpec((rows // steps, width), lambda i: (i, 0))] * count


def inverse_of(x):
    return lax.rsqrt(jnp.mean(x * x, -1, keepdims=True) + norm_eps)


def norm_kernel(order, mine_ref, x_ref, gain_ref, out_ref):
    mine = [mine_ref[i] for i in range(5)]
    inverse = inverse_of(x_ref[...].astype(F32))

    def write(q, value):
        out_ref[:, tile(q)] = value.astype(BF)

    def read(i):
        return x_ref[:, tile(i)].astype(F32) * inverse * gain_ref[:, tile(i)]

    order.to_tiles(read, write, mine)


def norm_to(order, x, gain):
    if not order.fast:
        x = x.astype(F32)
        return order.to_rel((x * inverse_of(x) * gain).astype(BF))
    rows, width = x.shape
    specs = row_specs(2, rows, width, 2)
    return run(
        functools.partial(norm_kernel, order),
        [order.mine, x, gain],
        [shape_of((rows, width), BF)],
        [SMEM, specs[0], pl.BlockSpec((1, width), lambda i: (0, 0))],
        [specs[1]],
        (2,),
    )[0]


def order_kernel(order, mine_ref, x_ref, out_ref):
    mine = [mine_ref[i] for i in range(5)]

    def write(q, value):
        out_ref[:, tile(q)] = value.astype(out_ref.dtype)

    order.to_tiles(lambda i: x_ref[:, tile(i)].astype(F32), write, mine)


def order_to(order, x):
    if not order.fast:
        return order.to_rel(x)
    rows, width = x.shape
    specs = row_specs(2, rows, width, 2)
    return run(
        functools.partial(order_kernel, order),
        [order.mine, x],
        [shape_of((rows, width), x.dtype)],
        [SMEM, specs[0]],
        [specs[1]],
        (2,),
    )[0]


def middle_kernel(order, mine_ref, x_ref, a_ref, b_ref, mid_ref, out_ref):
    mine = [mine_ref[i] for i in range(5)]
    mid = x_ref[...].astype(F32) + a_ref[...].astype(F32) + b_ref[...].astype(F32)
    mid_ref[...] = mid
    inverse = inverse_of(mid)

    def write(q, value):
        out_ref[:, tile(q)] = value.astype(BF)

    order.to_tiles(lambda i: mid_ref[:, tile(i)] * inverse, write, mine)


def middle_to(order, x, a, b):
    rows, width = x.shape
    if not order.fast:
        mid = x.astype(F32) + a.astype(F32) + b.astype(F32)
        return mid, order.to_rel((mid * inverse_of(mid)).astype(BF))
    specs = row_specs(5, rows, width, 2)
    return run(
        functools.partial(middle_kernel, order),
        [order.mine, x, a, b],
        [shape_of((rows, width), F32), shape_of((rows, width), BF)],
        [SMEM] + specs[:3],
        specs[:2],
        (2,),
    )


def back_kernel(order, scaled, mine_ref, x_ref, g_ref, a_ref, b_ref, *outs):
    mine = [mine_ref[i] for i in range(5)]
    scratch = outs[-1]
    if scaled:
        gain_ref, outs = outs[0], outs[1:]
    inverse = inverse_of(x_ref[...].astype(F32))

    def write(t, value):
        scratch[:, tile(t)] = value * gain_ref[:, tile(t)] if scaled else value

    def read(i):
        return a_ref[:, tile(i)].astype(F32) + b_ref[:, tile(i)].astype(F32)

    order.from_tiles(read, write, mine)
    normed = x_ref[...].astype(F32) * inverse
    scaled = scratch[...]
    shared = jnp.mean(scaled * normed, -1, keepdims=True)
    total = g_ref[...].astype(F32) + inverse * (scaled - normed * shared)
    outs[0][...] = total
    if len(outs) == 3:
        outs[1][...] = total.astype(BF)


def norm_back(order, x, g, a, b, gain=None, low=False):
    rows, width = x.shape
    scaled = gain is not None
    if not order.fast:
        x = x.astype(F32)
        inverse = inverse_of(x)
        normed = x * inverse
        grad = a.astype(F32) + b.astype(F32)
        grad = order.from_rel(grad)
        grad = grad * gain if scaled else grad
        shared = jnp.mean(grad * normed, -1, keepdims=True)
        total = g.astype(F32) + inverse * (grad - normed * shared)
        return (total, total.astype(BF)) if low else (total,)
    specs = row_specs(6, rows, width, 2)
    outs = [shape_of((rows, width), F32)] + ([shape_of((rows, width), BF)] if low else [])
    return run(
        functools.partial(back_kernel, order, scaled),
        [order.mine, x, g, a, b] + ([gain] if scaled else []),
        outs,
        [SMEM] + specs[:4] + [pl.BlockSpec((1, width), lambda i: (0, 0))] * scaled,
        specs[: len(outs)],
        (2,),
        scratch=[pltpu.VMEM((rows // 2, width), F32)],
    )


def result_kernel(order, mine_ref, mid_ref, a_ref, b_ref, out_ref):
    mine = [mine_ref[i] for i in range(5)]

    def write(t, value):
        out_ref[:, tile(t)] = (mid_ref[:, tile(t)] + value).astype(BF)

    order.from_tiles(
        lambda i: a_ref[:, tile(i)].astype(F32) + b_ref[:, tile(i)].astype(F32), write, mine
    )


def result_of(order, mid, a, b):
    rows, width = mid.shape
    if not order.fast:
        return (mid + order.from_rel(a.astype(F32) + b.astype(F32))).astype(BF)
    specs = row_specs(4, rows, width, 2)
    return run(
        functools.partial(result_kernel, order),
        [order.mine, mid, a, b],
        [shape_of((rows, width), BF)],
        [SMEM] + specs[:3],
        specs[:1],
        (2,),
    )[0]


def pack_kernel(count, kinds, *refs):
    out_ref = refs[-1]
    cols = out_ref.shape[-1]
    depth = refs[0].shape[0]
    for m in range(kinds):
        value = refs[m][...].astype(F32)
        if len(refs) > kinds + 1:
            value = value * refs[kinds][...]
        for t in range(count):
            out_ref[t, m * depth : (m + 1) * depth] = value[:, t * cols : (t + 1) * cols].astype(BF)


def pack(weights, gain, count):
    depth, width = weights[0].shape
    return run(
        functools.partial(pack_kernel, count, len(weights)),
        weights + ([] if gain is None else [gain]),
        [shape_of((count, len(weights) * depth, width // count), BF)],
    )[0]


def unpack_kernel(p_ref, gate_ref, up_ref, gain_ref, gate_out, up_out, down_out, sum_ref):
    count, depth, cols = p_ref.shape
    depth = depth // 3
    total = jnp.zeros((depth, 1), F32)
    for t in range(count):
        lanes = slice(t * cols, (t + 1) * cols)
        for m, (w_ref, out_ref) in enumerate([(gate_ref, gate_out), (up_ref, up_out)]):
            part = p_ref[t, m * depth : (m + 1) * depth].astype(F32)
            total = total + jnp.sum(part * w_ref[:, lanes].astype(F32), -1, keepdims=True)
            out_ref[:, lanes] = part * gain_ref[...]
        down_out[:, lanes] = p_ref[t, 2 * depth :].astype(F32)
    sum_ref[...] = total


def pack_qkv_kernel(count, me_ref, q_ref, k_ref, v_ref, out_ref):
    for t in range(count):
        slot = me_ref[0] ^ t
        out_ref[slot, :, :HEAD_COLS] = q_ref[:, t * HEAD_COLS : (t + 1) * HEAD_COLS]
        lanes = slice(t * HEAD_DIM, (t + 1) * HEAD_DIM)
        both = jnp.concatenate([k_ref[:, lanes].astype(F32), v_ref[:, lanes].astype(F32)], -1)
        out_ref[slot, :, HEAD_COLS:] = both.astype(BF)


def place_kernel(count, me_ref, *refs):
    for r in range(count):
        refs[-1][me_ref[0] ^ r] = refs[r][...]


def columns_kernel(kinds, in_ref, *outs):
    count, depth, units = in_ref.shape
    depth = depth // kinds
    step = max(1, 128 // depth)
    for m in range(kinds):
        for t in range(0, count, step):
            rows = [in_ref[t + i, m * depth : (m + 1) * depth] for i in range(step)]
            both = jnp.concatenate(rows, 0).astype(F32)
            outs[m][:, t * depth : (t + step) * depth] = both.T.astype(BF)


def rows_kernel(depth, *refs):
    out_ref = refs[-1]
    count, _, units = out_ref.shape
    step = max(1, 128 // depth)
    m = 0
    for ref in refs[:-1]:
        for first in range(0, ref.shape[0], units):
            for t in range(0, count, step):
                lanes = slice(t * depth, (t + step) * depth)
                both = ref[first : first + units, lanes].astype(F32).T
                for i in range(step):
                    rows = both[i * depth : (i + 1) * depth]
                    out_ref[t + i, m * depth : (m + 1) * depth] = rows.astype(BF)
            m += 1


def unpack_qkv_kernel(count, q_ref, k_ref, v_ref, g_ref, p_ref, qo_ref, ko_ref, vo_ref, sum_ref):
    gain = g_ref[...]
    total = jnp.zeros_like(gain)
    for t in range(count):
        part = p_ref[t].astype(F32)
        lanes = slice(t * HEAD_COLS, (t + 1) * HEAD_COLS)
        thin = slice(t * HEAD_DIM, (t + 1) * HEAD_DIM)
        gq = part[:, :HEAD_COLS]
        gk = part[:, HEAD_COLS : HEAD_COLS + HEAD_DIM]
        gv = part[:, HEAD_COLS + HEAD_DIM :]
        total = total + jnp.sum(gq * q_ref[:, lanes].astype(F32), -1, keepdims=True)
        total = total + jnp.sum(gk * k_ref[:, thin].astype(F32), -1, keepdims=True)
        total = total + jnp.sum(gv * v_ref[:, thin].astype(F32), -1, keepdims=True)
        qo_ref[:, lanes] = gq
        ko_ref[:, thin] = gk
        vo_ref[:, thin] = gv
    sum_ref[...] = total / gain


def swap_halves(values):
    width = values.shape[-1]
    lanes = lax.broadcasted_iota(jnp.int32, (1, width), 1)
    return jnp.where(
        lanes % HEAD_DIM < HEAD_DIM // 2,
        pltpu.roll(values, width - HEAD_DIM // 2, 1),
        pltpu.roll(values, HEAD_DIM // 2, 1),
    )


def project_kernel(repeat, count, *refs):
    a_ref, cos_ref, sin_ref = refs[:3]
    w_refs, q_ref, kv_ref = refs[3 : 3 + count], refs[-2], refs[-1]
    piece = w_refs[0].shape[0]
    raw = None
    for k in range(count):
        term = dot(a_ref[:, k * piece : (k + 1) * piece], w_refs[k][...])
        raw = term if raw is None else raw + term
    cosine = jnp.concatenate([cos_ref[...]] * repeat, 0)
    sine = jnp.concatenate([sin_ref[...]] * repeat, 0)
    out = (raw * cosine + swap_halves(raw) * sine).astype(BF)
    q_ref[...] = out[:, :HEAD_COLS]
    kv_ref[...] = out[:, HEAD_COLS:]


def project(a1, cosine, sine, parts):
    rows, width = a1.shape
    seq_dev, cols = cosine.shape
    block = min(2 * seq_dev, rows)
    fixed = lambda i: (0, 0)
    moving = lambda i: (i, 0)
    return run(
        functools.partial(project_kernel, block // seq_dev, len(parts)),
        [a1, cosine, sine] + parts,
        [shape_of((rows, HEAD_COLS), BF), shape_of((rows, 2 * HEAD_DIM), BF)],
        [pl.BlockSpec((block, width), moving)]
        + [pl.BlockSpec((seq_dev, cols), fixed)] * 2
        + [pl.BlockSpec(p.shape, fixed) for p in parts],
        [pl.BlockSpec((block, HEAD_COLS), moving), pl.BlockSpec((block, 2 * HEAD_DIM), moving)],
        (rows // block,),
        flops=2 * rows * width * cols,
    )


def stack_heads(values):
    return jnp.concatenate(
        [values[:, j * HEAD_DIM : (j + 1) * HEAD_DIM] for j in range(GROUPS)], 0
    )


def soft_weights(queries, keys, key_ref, seq_dev):
    scores = dot_nt(queries, keys) * FACTOR
    place = lax.broadcasted_iota(jnp.int32, (queries.shape[0], 1), 0) % seq_dev
    return jnp.where(place >= key_ref[...], jnp.exp(scores), 0.0)


def attend_kernel(q_ref, kv_ref, key_ref, o_ref):
    seq_dev = q_ref.shape[0]
    both = kv_ref[...].reshape(-1, 2 * HEAD_DIM)
    keys, values = both[:, :HEAD_DIM], both[:, HEAD_DIM:]
    weights = soft_weights(stack_heads(q_ref[...]), keys, key_ref, seq_dev)
    totals = jnp.sum(weights, -1, keepdims=True)
    attended = dot(weights.astype(BF), values) / totals
    for j in range(GROUPS):
        rows = attended[j * seq_dev : (j + 1) * seq_dev]
        o_ref[:, j * HEAD_DIM : (j + 1) * HEAD_DIM] = rows.astype(BF)


def attend(queries, kv, key_places, seq_dev):
    rows = queries.shape[0]
    count, seqs = kv.shape[:2]
    return run(
        attend_kernel,
        [queries, kv, key_places],
        [shape_of((rows, HEAD_COLS), BF)],
        [
            pl.BlockSpec((seq_dev, HEAD_COLS), lambda s: (s, 0)),
            pl.BlockSpec((count, 1, seq_dev, 2 * HEAD_DIM), lambda s: (0, s, 0, 0)),
            pl.BlockSpec((1, count * seq_dev), lambda s: (0, 0)),
        ],
        [pl.BlockSpec((seq_dev, HEAD_COLS), lambda s: (s, 0))],
        (seqs,),
        flops=4 * rows * GROUPS * HEAD_DIM * count * seq_dev,
    )[0]


def attend_back_kernel(q_ref, kv_ref, key_ref, do_ref, cos_ref, sin_ref, dq_ref, dkv_ref, mid_ref):
    seq_dev = q_ref.shape[0]
    both = kv_ref[...].reshape(-1, 2 * HEAD_DIM)
    keys, values = both[:, :HEAD_DIM], both[:, HEAD_DIM:]
    queries = stack_heads(q_ref[...])
    weights = soft_weights(queries, keys, key_ref, seq_dev)
    totals = jnp.sum(weights, -1, keepdims=True)
    low = weights.astype(BF)
    attended = dot(low, values) / totals
    grads = stack_heads(do_ref[...])
    deltas = jnp.sum(grads * attended, -1, keepdims=True) / totals
    mixed = (grads / totals).astype(BF)
    scores = (weights * (dot_nt(mixed, values) - deltas)).astype(BF)
    turned = dot(scores, keys) * FACTOR
    for j in range(GROUPS):
        mid_ref[:, j * HEAD_DIM : (j + 1) * HEAD_DIM] = turned[j * seq_dev : (j + 1) * seq_dev]
    whole = mid_ref[...]
    cosine, sine = cos_ref[:, :HEAD_COLS], sin_ref[:, :HEAD_COLS]
    dq_ref[...] = (whole * cosine - swap_halves(whole) * sine).astype(BF)
    grad_keys = dot_tn(scores, queries) * FACTOR
    grad_values = dot_tn(low, mixed)
    joined = jnp.concatenate([grad_keys, grad_values], -1)
    dkv_ref[...] = joined.astype(BF).reshape(dkv_ref.shape)


def attend_back(queries, kv, key_places, grads, cosine, sine, seq_dev):
    rows = queries.shape[0]
    count, seqs = kv.shape[:2]
    own = pl.BlockSpec((seq_dev, HEAD_COLS), lambda s: (s, 0))
    table = pl.BlockSpec(cosine.shape, lambda s: (0, 0))
    blocks = pl.BlockSpec((count, 1, seq_dev, 2 * HEAD_DIM), lambda s: (0, s, 0, 0))
    return run(
        attend_back_kernel,
        [queries, kv, key_places, grads, cosine, sine],
        [shape_of((rows, HEAD_COLS), BF), shape_of(kv.shape, BF)],
        [own, blocks, pl.BlockSpec((1, count * seq_dev), lambda s: (0, 0)), own, table, table],
        [own, blocks],
        (seqs,),
        scratch=[pltpu.VMEM((seq_dev, HEAD_COLS), F32)],
        flops=14 * rows * GROUPS * HEAD_DIM * count * seq_dev,
    )


def turn_back_kernel(repeat, a_ref, b_ref, cos_ref, sin_ref, out_ref):
    total = a_ref[...].astype(F32) + b_ref[...].astype(F32)
    cosine = jnp.concatenate([cos_ref[:, HEAD_COLS:]] * repeat, 0)
    sine = jnp.concatenate([sin_ref[:, HEAD_COLS:]] * repeat, 0)
    out_ref[...] = (total * cosine - swap_halves(total) * sine).astype(BF)


def wide_kernel(product, left_ref, *refs):
    rights, out_ref = refs[:-1], refs[-1]
    cols = out_ref.shape[1] // len(rights)
    for k, right in enumerate(rights):
        out_ref[:, k * cols : (k + 1) * cols] = product(left_ref[...], right[...]).astype(BF)


def wide(product, left, rights, width, block):
    rows, depth = left.shape
    return run(
        functools.partial(wide_kernel, product),
        [left] + rights,
        [shape_of((rows, width), BF)],
        [pl.BlockSpec((block, depth), lambda i: (i, 0))]
        + [pl.BlockSpec(r.shape, lambda i: (0, 0)) for r in rights],
        [pl.BlockSpec((block, width), lambda i: (i, 0))],
        (rows // block,),
        vmem=48,
        flops=2 * rows * depth * width,
    )[0]


def gate_kernel(a_ref, gate_ref, up_ref, hid_ref, one_ref, two_ref):
    units, cols = hid_ref.shape[1], gate_ref.shape[1]
    gate = up = None
    for k in range(a_ref.shape[1] // cols):
        part = a_ref[:, k * cols : (k + 1) * cols]
        g = dot_nt(part, gate_ref[k * units : (k + 1) * units])
        u = dot_nt(part, up_ref[k * units : (k + 1) * units])
        gate = g if gate is None else gate + g
        up = u if up is None else up + u
    sigmoid = jax.nn.sigmoid(gate)
    active = gate * sigmoid
    hid_ref[...] = (active * up).astype(BF)
    one_ref[...] = up * sigmoid * (1.0 + gate * (1.0 - sigmoid))
    two_ref[...] = active


def gate_up(a2, gate, up, units, block):
    rows, width = a2.shape
    moving = lambda i: (i, 0)
    out = pl.BlockSpec((block, units), moving)
    return run(
        gate_kernel,
        [a2, gate, up],
        [shape_of((rows, units), BF), shape_of((rows, units), F32), shape_of((rows, units), F32)],
        [pl.BlockSpec((block, width), moving)] + [pl.BlockSpec(gate.shape, lambda i: (0, 0))] * 2,
        [out, out, out],
        (rows // block,),
        vmem=48,
    )


def hidden_kernel(g_ref, one_ref, two_ref, down_ref, gate_ref, up_ref, dboth_ref, out_ref):
    units, cols = one_ref.shape[1], down_ref.shape[1]
    pieces = g_ref.shape[1] // cols
    total = None
    for k in range(pieces):
        term = dot_nt(g_ref[:, k * cols : (k + 1) * cols], down_ref[k * units : (k + 1) * units])
        total = term if total is None else total + term
    dgate = (total * one_ref[...]).astype(BF)
    dup = (total * two_ref[...]).astype(BF)
    dboth_ref[:, :units] = dgate
    dboth_ref[:, units:] = dup
    for k in range(pieces):
        part = dot(dgate, gate_ref[k * units : (k + 1) * units])
        part = part + dot(dup, up_ref[k * units : (k + 1) * units])
        out_ref[:, k * cols : (k + 1) * cols] = part.astype(BF)


def hidden_back(gb, one, two, down, gate, up, block):
    rows, width = gb.shape
    units = one.shape[1]
    moving = lambda i: (i, 0)
    fixed = lambda i: (0, 0)
    thin = pl.BlockSpec((block, units), moving)
    full = pl.BlockSpec((block, width), moving)
    return run(
        hidden_kernel,
        [gb, one, two, down, gate, up],
        [shape_of((rows, 2 * units), BF), shape_of((rows, width), BF)],
        [full, thin, thin] + [pl.BlockSpec(down.shape, fixed)] * 3,
        [pl.BlockSpec((block, 2 * units), moving), full],
        (rows // block,),
        vmem=56,
    )


def result_rows_kernel(h_ref, down_ref, out_ref):
    units, cols = h_ref.shape[1], down_ref.shape[1]
    for k in range(out_ref.shape[1] // cols):
        part = dot(h_ref[...], down_ref[k * units : (k + 1) * units])
        out_ref[:, k * cols : (k + 1) * cols] = part.astype(BF)


def result_rows(hidden, down, width, block):
    rows, units = hidden.shape
    moving = lambda i: (i, 0)
    return run(
        result_rows_kernel,
        [hidden, down],
        [shape_of((rows, width), BF)],
        [pl.BlockSpec((block, units), moving), pl.BlockSpec(down.shape, lambda i: (0, 0))],
        [pl.BlockSpec((block, width), moving)],
        (rows // block,),
    )[0]


def weight_grad_kernel(left_ref, right_ref, out_ref):
    out_ref[...] = dot_tn(left_ref[...], right_ref[...]).astype(BF)


def weight_grad(left, right, pieces):
    rows, units = left.shape
    cols = right.shape[1] // pieces
    return run(
        weight_grad_kernel,
        [left, right],
        [shape_of((pieces * units, cols), BF)],
        [pl.BlockSpec((rows, units), lambda i: (0, 0)), pl.BlockSpec((rows, cols), lambda i: (0, i))],
        [pl.BlockSpec((units, cols), lambda i: (i, 0))],
        (pieces,),
        vmem=48,
    )[0]


def gather_rows(value, bits, what):
    acc = value
    for bit in bits:
        acc = jnp.concatenate([acc, bit.swap(acc, what)], 0)
    return acc


def reduce_rows(acc, bits, what):
    steps = []
    for bit in reversed(bits):
        half = acc.shape[0] // 2
        steps.append((acc[:half], bit.swap(acc[half:], what)))
        acc = add_low(*steps[-1])
    return steps


def gather_team(value, bit_x, near, bit_core, what, marks):
    half = value.shape[0] // 2
    by_x, by_near = bit_x.swap(value, what), near.swap(value, what)
    diagonal = [bit_x.swap(by_near[:half], what), near.swap(by_x[half:], what)]
    four = after(jnp.concatenate([value, by_x, by_near] + diagonal, 0), *marks)
    return jnp.concatenate([four, bit_core.swap(four, what)], 0)


def add_low(a, b):
    return (a.astype(F32) + b.astype(F32)).astype(BF)


def reduce_four(acc, got, bit_x, near, what):
    half = acc.shape[0]
    acc = add_low(acc, got)
    rows = half // 4
    own, by_x, by_near = acc[:rows], acc[rows : 2 * rows], acc[2 * rows : 3 * rows]
    first, second = acc[3 * rows : 3 * rows + rows // 2], acc[3 * rows + rows // 2 :]
    got_near = bit_x.swap(first, what)
    got_x = near.swap(second, what)
    by_near = jnp.concatenate([add_low(by_near[: rows // 2], got_near), by_near[rows // 2 :]], 0)
    by_x = jnp.concatenate([by_x[: rows // 2], add_low(by_x[rows // 2 :], got_x)], 0)
    return (add_low(own, bit_x.swap(by_x, what)), near.swap(by_near, what)), by_x


def absolute(blocks, index, bits):
    def one(j):
        other = index ^ j
        slot = sum(((other >> b.bit) & 1) << i for i, b in enumerate(bits))
        return lax.dynamic_index_in_dim(blocks, slot, 0, False)

    return jnp.stack([one(j) for j in range(blocks.shape[0])])


def relative(blocks, index, bits):
    def one(r):
        code = sum(((r >> i) & 1) << b.bit for i, b in enumerate(bits))
        return lax.dynamic_index_in_dim(blocks, index ^ code, 0, False)

    return jnp.stack([one(r) for r in range(blocks.shape[0])])


def shards(
    dp,
    ctx,
    tokens,
    cotangent,
    attn_gain,
    query_weight,
    key_weight,
    value_weight,
    output_weight,
    mlp_gain,
    gate_weight,
    up_weight,
    down_weight,
):
    seqs, seq_dev, width = tokens.shape
    rows = seqs * seq_dev
    depth = query_weight.shape[0]
    c_index = lax.axis_index("ctx")

    bit_x, bit_core = Bit("dp", 1, dp), Bit("dp", 0, dp)
    ctx_bits = [Bit("ctx", b, ctx) for b in reversed(range(ctx.bit_length() - 1))]
    near = ctx_bits[-1]
    far = [b for b in ctx_bits if b is not near]
    dp_bits = [bit_x, bit_core]
    names = dp_bits + ctx_bits
    attn_order = Order(names, list(reversed(ctx_bits)) + dp_bits, ctx_bits, depth)
    mlp_order = Order(names, far + dp_bits + [near], [], depth)
    x = tokens.reshape(rows, width)
    cot = cotangent.reshape(rows, width)
    gain_one = attn_gain.astype(F32)[:, None]
    gain_two = mlp_gain.astype(F32)[:, None]

    team_groups = []
    for c in range(ctx):
        if not (c >> near.bit) & 1:
            team_groups.append([d * ctx + (c | (n << near.bit)) for d in range(dp) for n in range(2)])
    team = 2 * dp

    def mlp_trade(parts):
        return lax.all_to_all(
            parts, ("dp", "ctx"), 0, 0, axis_index_groups=team_groups, tiled=True
        )

    def mlp_slices(weights, gain, *marks):
        kinds = len(weights)
        parts = after(mlp_trade(pack(weights, gain, team)), *marks)
        shape = (parts.shape[2], team * depth)
        return run(functools.partial(columns_kernel, kinds), [parts], [shape_of(shape, BF)] * kinds)

    def mlp_rows(sums):
        kinds = sum(t.shape[0] for t in sums) // units
        shape = (team, kinds * depth, units)
        return mlp_trade(run(functools.partial(rows_kernel, depth), sums, [shape_of(shape, BF)])[0])

    far_groups = []
    for n in range(2):
        far_groups.append([c for c in range(ctx) if (c >> near.bit) & 1 == n])
    pieces = ctx // 2

    def far_gather(own):
        return lax.all_gather(own, "ctx", axis=0, tiled=True, axis_index_groups=far_groups)

    def far_reduce(terms):
        return lax.psum_scatter(
            terms, "ctx", scatter_dimension=0, tiled=True, axis_index_groups=far_groups
        )

    qkv_cols = HEAD_COLS + 2 * HEAD_DIM
    me = lax.axis_index("dp").astype(jnp.int32).reshape(1)
    slices = run(
        functools.partial(pack_qkv_kernel, dp),
        [me, query_weight, key_weight, value_weight],
        [shape_of((dp, depth, qkv_cols), BF)],
        [SMEM] + [pl.BlockSpec(memory_space=pltpu.VMEM)] * 3,
    )[0]
    out_acc = [output_weight]
    for bit in ctx_bits[:-1]:
        out_acc.append(jnp.concatenate([out_acc[-1], bit.swap(out_acc[-1], "out")], 0))
    slices = [slices[0]] + [swap_difference(slices[r], "dp", dp, r, "slice") for r in range(1, dp)]
    own = run(
        functools.partial(place_kernel, dp),
        [me, after(slices[0], out_acc[1])] + slices[1:],
        [shape_of((dp, depth, qkv_cols), BF)],
        [SMEM] + [pl.BlockSpec(memory_space=pltpu.VMEM)] * dp,
    )[0].reshape(dp * depth, qkv_cols)
    halves = [own]
    for i, bit in enumerate(ctx_bits[:-1]):
        sent = halves[-1] if i == 0 else after(halves[-1], out_acc[i + 1])
        halves.append(jnp.concatenate([sent, bit.swap(sent, "qkv")], 0))
    qkv = [halves[-1], ctx_bits[-1].swap(halves[-1], "qkv")]
    out_rel = after(out_acc[-1], qkv[1])
    out_rel = jnp.concatenate([out_rel, ctx_bits[-1].swap(out_rel, "out")], 0)
    out_full = absolute(out_rel.reshape(ctx, depth, width), c_index, ctx_bits)
    out_full = out_full.reshape(ctx * depth, width)

    gate_own, up_own = mlp_slices([after(gate_weight, own), up_weight], gain_two, halves[-1])
    gain_all = jnp.broadcast_to(after(attn_gain, gate_own)[None], (dp * ctx, depth))
    gain_all = lax.all_to_all(gain_all, ("dp", "ctx"), 0, 0, tiled=True)
    gain_all = gain_all.reshape(1, width).astype(F32)
    a1_half = gather_rows(norm_to(attn_order, x, gain_all), dp_bits[:1], "a1")
    a1 = gather_rows(a1_half, dp_bits[1:], "a1")
    gate = far_gather(gate_own)
    (down_own,) = mlp_slices([after(down_weight.T, gain_all)], None)
    units = down_own.shape[0]

    places = jnp.arange(seq_dev, dtype=jnp.int32)
    half_dim = HEAD_DIM // 2
    freqs = rope_base ** (-(jnp.arange(half_dim, dtype=F32) * 2.0) / HEAD_DIM)
    angles = (c_index * seq_dev + places).astype(F32)[:, None] * freqs[None, :]
    cosine, sine = jnp.cos(angles), jnp.sin(angles)
    cosine = jnp.concatenate([cosine, cosine] * (GROUPS + 1) + [jnp.ones((seq_dev, HEAD_DIM), F32)], -1)
    sine = jnp.concatenate([-sine, sine] * (GROUPS + 1) + [jnp.zeros((seq_dev, HEAD_DIM), F32)], -1)
    rel = jnp.arange(ctx, dtype=jnp.int32)
    others = sum(((rel >> i) & 1) << b.bit for i, b in enumerate(ctx_bits)) ^ c_index
    key_places = (((others - c_index) * seq_dev)[:, None] + places[None, :]).reshape(1, -1)

    queries, kv_own = project(a1, cosine, sine, qkv)
    all_seqs = dp * seqs
    kv = kv_own
    for i, bit in enumerate(ctx_bits):
        if i == 1:
            kv = after(kv, down_own)
        if i == len(ctx_bits) - 1:
            up = far_gather(after(up_own, kv))
            down = far_gather(after(down_own, kv))
        kv = jnp.concatenate([kv, bit.swap(kv, "kv")], 0)
    kv = kv.reshape(ctx, all_seqs, seq_dev, 2 * HEAD_DIM)
    heads = attend(queries, kv, key_places, seq_dev)
    branch = dot(heads, out_full).astype(BF)
    branch = reduce_rows(branch, dp_bits, "branch")[-1]
    middle, a2 = middle_to(mlp_order, x, *branch)

    gb = gather_team(order_to(mlp_order, after(cot, middle)), bit_x, near, bit_core, "gb", [])
    a2 = gather_team(a2, bit_x, near, bit_core, "a2", [])
    block = min(256, a2.shape[0])
    hidden, one, two = gate_up(a2, gate, up, units, block)
    down_terms = weight_grad(hidden, gb, pieces)
    down_back = far_reduce(down_terms)
    dboth, da2 = hidden_back(after(gb, down_terms), one, two, down, gate, up, block)
    half = da2.shape[0] // 2
    da2_got = bit_core.swap(da2[half:], "da2")
    da2_two, da2_mark = reduce_four(da2[:half], da2_got, bit_x, near, "da2")
    down_out = result_rows(after(hidden, da2), down, width, block)
    result_got = bit_core.swap(after(down_out[half:], da2_mark), "result")
    both_terms = weight_grad(dboth, after(a2, da2_mark), pieces)
    both_back = far_reduce(both_terms)
    grad_middle, db = norm_back(mlp_order, middle, after(cot, both_terms, result_got), *da2_two, low=True)
    grad_branch = gather_rows(db, dp_bits, "db")
    result_two, result_mark = reduce_four(
        down_out[:half], after(result_got, db), bit_x, near, "result"
    )
    result = result_of(mlp_order, middle, *result_two)

    grad_heads = dot_nt(grad_branch, out_full)
    dq, dkv = attend_back(
        queries, kv, after(key_places, *result_two), grad_heads, cosine, sine, seq_dev
    )

    class Sum:
        def __init__(self, terms, what):
            self.terms, self.what, self.bits = terms, what, list(reversed(ctx_bits))

        def step(self, *marks):
            half = self.terms.shape[0] // 2
            sent = after(self.terms[half:], *marks) if marks else self.terms[half:]
            self.pair = self.terms[:half], self.bits.pop(0).swap(sent, self.what)
            self.terms = add_low(*self.pair)
            return self.pair[1]

        def finish(self, *marks):
            while self.bits:
                self.step(*marks)
            return self.pair

    dkv_sum = Sum(dkv.reshape(-1, 2 * HEAD_DIM), "dkv")
    dkv_first = dkv_sum.step()
    dq_sum = Sum(dot_tn(a1, after(dq, dkv_first)).astype(BF), "dq_w")
    dq_first = dq_sum.step()
    dkv_sum.step(down_back)
    dkv_two = dkv_sum.finish()
    dkv_low = run(
        functools.partial(turn_back_kernel, all_seqs),
        [after(dkv_two[0], dq_first), dkv_two[1]] + [cosine, sine],
        [shape_of((dp * rows, 2 * HEAD_DIM), BF)],
    )[0]
    kv_sum = Sum(dot_tn(a1, dkv_low).astype(BF), "dkv_w")
    kv_first = kv_sum.step()
    da1 = wide(dot_nt, jnp.concatenate([dq, dkv_low], -1), qkv, width, min(256, dp * rows))
    da1_steps = reduce_rows(da1, dp_bits, "da1")
    da1_two = da1_steps[-1]
    (grad_tokens,) = norm_back(attn_order, x, grad_middle, *da1_two, gain_all)
    dq_second = dq_sum.step()
    kv_second = kv_sum.step(dq_second, da1_steps[0][1])
    out_total = dot_tn(heads, grad_branch).astype(BF).reshape(ctx, depth, width)
    out_total = relative(after(out_total, kv_first), c_index, ctx_bits).reshape(ctx * depth, width)
    out_sum = Sum(out_total, "dout_w")
    out_first = out_sum.step()
    all_back = mlp_rows([after(both_back, kv_first), down_back])
    dq_two = dq_sum.finish()
    kv_two = kv_sum.finish(dq_two[1], *da1_two)
    out_second = out_sum.step()
    out_two = out_sum.finish()
    output_grad = out_two[0].astype(F32) + out_two[1].astype(F32)
    qkv_total = jnp.concatenate([add_low(*dq_two), add_low(*kv_two)], -1).reshape(dp, depth, qkv_cols)
    qkv_back = lax.all_to_all(after(qkv_total, all_back), "dp", 0, 0, tiled=True)

    wide_shape = shape_of(gate_weight.shape, F32)
    gate_grad, up_grad, down_grad, mlp_sum = run(
        unpack_kernel,
        [all_back, gate_weight, up_weight, gain_two],
        [wide_shape, wide_shape, wide_shape, shape_of((depth, 1), F32)],
    )
    down_grad = down_grad.T
    query_grad, key_grad, value_grad, attn_sum = run(
        functools.partial(unpack_qkv_kernel, dp),
        [query_weight, key_weight, value_weight, gain_one, qkv_back],
        [shape_of(w.shape, F32) for w in (query_weight, key_weight, value_weight, gain_one)],
    )
    return (
        result.reshape(seqs, seq_dev, width),
        grad_tokens.reshape(seqs, seq_dev, width),
        attn_sum[:, 0],
        query_grad,
        key_grad,
        value_grad,
        output_grad,
        mlp_sum[:, 0],
        gate_grad,
        up_grad,
        down_grad,
    )


def solution(mesh):
    dp, ctx = mesh.shape["dp"], mesh.shape["ctx"]

    def local(*args):
        return shards(dp, ctx, *args)

    weight = P(("dp", "ctx"), None)
    flat = P(("dp", "ctx"))
    acts = P("dp", "ctx", None)
    down = P(None, ("dp", "ctx"))
    return jax.shard_map(
        local,
        mesh=mesh,
        in_specs=(acts, acts, flat, weight, weight, weight, weight, flat, weight, weight, down),
        out_specs=(acts, acts, flat, weight, weight, weight, weight, flat, weight, weight, down),
        check_vma=False,
    )
```

```python
import functools
import math

import jax
import jax.numpy as jnp
from jax import lax
from jax.experimental import pallas as pl
from jax.experimental.pallas import tpu as pltpu
from jax.sharding import PartitionSpec as P

HEADS = 32
KV_HEADS = 4
HEAD_DIM = 64
GROUPS = HEADS // KV_HEADS
HEAD_COLS = GROUPS * HEAD_DIM
FACTOR = 1.0 / math.sqrt(HEAD_DIM)

norm_eps = 1e-05
rope_base = 10000.0

BF = jnp.bfloat16
F32 = jnp.float32
MIB = 1 << 20


def dot(left, right):
    return jnp.dot(left, right, preferred_element_type=F32)


def dot_nt(left, right):
    return lax.dot_general(left, right, (((1,), (1,)), ((), ())), preferred_element_type=F32)


def dot_tn(left, right):
    return lax.dot_general(left, right, (((0,), (0,)), ((), ())), preferred_element_type=F32)


def shape_of(shape, kind):
    return jax.ShapeDtypeStruct(shape, kind)


def run(kernel, ins, outs, specs=None, out_specs=None, grid=None, vmem=32, scratch=(), flops=0):
    whole = pl.BlockSpec(memory_space=pltpu.VMEM)
    moved = sum(math.prod(a.shape) * a.dtype.itemsize for a in list(ins) + list(outs))
    extra = {} if grid is None else {"grid": grid}
    name = kernel.func.__name__ if isinstance(kernel, functools.partial) else kernel.__name__
    return pl.pallas_call(
        kernel,
        name=name,
        out_shape=list(outs),
        in_specs=specs or [whole] * len(ins),
        out_specs=out_specs or [whole] * len(outs),
        scratch_shapes=list(scratch),
        compiler_params=pltpu.CompilerParams(vmem_limit_bytes=vmem * MIB),
        cost_estimate=pl.CostEstimate(flops=0, bytes_accessed=0, transcendentals=0),
        **extra,
    )(*ins)


SMEM = pl.BlockSpec(memory_space=pltpu.SMEM)


class Bit:
    def __init__(self, axis, bit, size):
        self.axis, self.bit = axis, bit
        self.pairs = [(i, i ^ (1 << bit)) for i in range(size)]

    def mine(self):
        return (lax.axis_index(self.axis) >> self.bit) & 1

    def swap(self, value, what):
        with jax.named_scope(f"{what}_{self.axis}{self.bit}"):
            return lax.ppermute(value, self.axis, self.pairs)


def swap_difference(value, axis, size, difference, what):
    with jax.named_scope(f"{what}_{axis}"):
        return lax.ppermute(value, axis, [(i, i ^ difference) for i in range(size)])


def after(value, *others):
    return lax.optimization_barrier((value,) + others)[0]


class Order:
    def __init__(self, names, rel, gathered, depth):
        self.names, self.rel, self.gathered, self.depth = names, rel, gathered, depth
        self.whole_tiles = rel[-1] is names[-1] and not gathered
        self.fast = depth == 64 and len(names) == 5 and (
            self.whole_tiles or (rel[-1] is not names[-1] and rel[-1] not in gathered)
        )
        self.mine = jnp.stack(
            [b.mine() if b in gathered else jnp.zeros((), jnp.int32) for b in names]
        ).astype(jnp.int32)

    def to_tiles(self, read, write, mine):
        lanes = lax.broadcasted_iota(jnp.int32, (1, 128), 1)
        head = self.rel[:-1]
        last = self.rel[-1]
        for q in range(16):
            value = {b: (q >> (3 - i)) & 1 for i, b in enumerate(head)}
            if self.whole_tiles:
                write(q, read(sum(value[b] << (3 - i) for i, b in enumerate(self.names[:-1]))))
                continue

            def source(low):
                index = 0
                for i, b in enumerate(self.names[:-1]):
                    v = low if b is last else value[b]
                    if b in self.gathered:
                        v = v ^ mine[i]
                    index = index * 2 + v
                return read(index)

            a, b = source(0), source(1)
            side = value[self.names[-1]]
            low = lambda: jnp.where(lanes < 64, a, pltpu.roll(b, 64, 1))
            high = lambda: jnp.where(lanes < 64, pltpu.roll(a, 64, 1), b)
            if self.names[-1] in self.gathered:
                write(q, jnp.where((side ^ mine[4]) == 0, low(), high()))
            else:
                write(q, low() if side == 0 else high())

    def from_tiles(self, read, write, mine):
        lanes = lax.broadcasted_iota(jnp.int32, (1, 128), 1)
        for t in range(16):
            value = {b: (t >> (3 - i)) & 1 for i, b in enumerate(self.names[:-1])}
            if self.whole_tiles:
                write(t, read(sum(value[b] << (3 - i) for i, b in enumerate(self.rel[:-1]))))
                continue

            def source(y):
                index = 0
                for b in self.rel[:-1]:
                    v = y if b is self.names[-1] else value[b]
                    if b in self.gathered:
                        v = v ^ mine[self.names.index(b)]
                    index = index * 2 + v
                return read(index)

            low, high = source(0), source(1)
            if value[self.rel[-1]] == 0:
                write(t, jnp.where(lanes < 64, low, pltpu.roll(high, 64, 1)))
            else:
                write(t, jnp.where(lanes < 64, pltpu.roll(low, 64, 1), high))

    def to_rel(self, array):
        count, width = array.shape
        out = array.reshape((count,) + (2,) * len(self.names) + (self.depth,))
        for b in self.gathered:
            k = self.names.index(b) + 1
            out = jnp.where(b.mine() == 1, jnp.flip(out, k), out)
        axes = [self.names.index(b) + 1 for b in self.rel]
        return out.transpose([0] + axes + [len(self.names) + 1]).reshape(count, width)

    def from_rel(self, array):
        count, width = array.shape
        out = array.reshape((count,) + (2,) * len(self.names) + (self.depth,))
        axes = [self.rel.index(b) + 1 for b in self.names]
        out = out.transpose([0] + axes + [len(self.names) + 1])
        for b in self.gathered:
            k = self.names.index(b) + 1
            out = jnp.where(b.mine() == 1, jnp.flip(out, k), out)
        return out.reshape(count, width)


def tile(index):
    start = index * 128
    return pl.ds(start if isinstance(start, int) else pl.multiple_of(start, 128), 128)


def row_specs(count, rows, width, steps):
    return [pl.BlockSpec((rows // steps, width), lambda i: (i, 0))] * count


def inverse_of(x):
    return lax.rsqrt(jnp.mean(x * x, -1, keepdims=True) + norm_eps)


def norm_kernel(order, mine_ref, x_ref, gain_ref, out_ref):
    mine = [mine_ref[i] for i in range(5)]
    inverse = inverse_of(x_ref[...].astype(F32))

    def write(q, value):
        out_ref[:, tile(q)] = value.astype(BF)

    def read(i):
        return x_ref[:, tile(i)].astype(F32) * inverse * gain_ref[:, tile(i)]

    order.to_tiles(read, write, mine)


def norm_to(order, x, gain):
    if not order.fast:
        x = x.astype(F32)
        return order.to_rel((x * inverse_of(x) * gain).astype(BF))
    rows, width = x.shape
    specs = row_specs(2, rows, width, 2)
    return run(
        functools.partial(norm_kernel, order),
        [order.mine, x, gain],
        [shape_of((rows, width), BF)],
        [SMEM, specs[0], pl.BlockSpec((1, width), lambda i: (0, 0))],
        [specs[1]],
        (2,),
    )[0]


def order_kernel(order, mine_ref, x_ref, out_ref):
    mine = [mine_ref[i] for i in range(5)]

    def write(q, value):
        out_ref[:, tile(q)] = value.astype(out_ref.dtype)

    order.to_tiles(lambda i: x_ref[:, tile(i)].astype(F32), write, mine)


def order_to(order, x):
    if not order.fast:
        return order.to_rel(x)
    rows, width = x.shape
    specs = row_specs(2, rows, width, 2)
    return run(
        functools.partial(order_kernel, order),
        [order.mine, x],
        [shape_of((rows, width), x.dtype)],
        [SMEM, specs[0]],
        [specs[1]],
        (2,),
    )[0]


def middle_kernel(order, mine_ref, x_ref, a_ref, b_ref, mid_ref, out_ref):
    mine = [mine_ref[i] for i in range(5)]
    mid = x_ref[...].astype(F32) + a_ref[...].astype(F32) + b_ref[...].astype(F32)
    mid_ref[...] = mid
    inverse = inverse_of(mid)

    def write(q, value):
        out_ref[:, tile(q)] = value.astype(BF)

    order.to_tiles(lambda i: mid_ref[:, tile(i)] * inverse, write, mine)


def middle_to(order, x, a, b):
    rows, width = x.shape
    if not order.fast:
        mid = x.astype(F32) + a.astype(F32) + b.astype(F32)
        return mid, order.to_rel((mid * inverse_of(mid)).astype(BF))
    specs = row_specs(5, rows, width, 2)
    return run(
        functools.partial(middle_kernel, order),
        [order.mine, x, a, b],
        [shape_of((rows, width), F32), shape_of((rows, width), BF)],
        [SMEM] + specs[:3],
        specs[:2],
        (2,),
    )


def back_kernel(order, scaled, mine_ref, x_ref, g_ref, a_ref, b_ref, *outs):
    mine = [mine_ref[i] for i in range(5)]
    scratch = outs[-1]
    if scaled:
        gain_ref, outs = outs[0], outs[1:]
    inverse = inverse_of(x_ref[...].astype(F32))

    def write(t, value):
        scratch[:, tile(t)] = value * gain_ref[:, tile(t)] if scaled else value

    def read(i):
        return a_ref[:, tile(i)].astype(F32) + b_ref[:, tile(i)].astype(F32)

    order.from_tiles(read, write, mine)
    normed = x_ref[...].astype(F32) * inverse
    scaled = scratch[...]
    shared = jnp.mean(scaled * normed, -1, keepdims=True)
    total = g_ref[...].astype(F32) + inverse * (scaled - normed * shared)
    outs[0][...] = total
    if len(outs) == 3:
        outs[1][...] = total.astype(BF)


def norm_back(order, x, g, a, b, gain=None, low=False):
    rows, width = x.shape
    scaled = gain is not None
    if not order.fast:
        x = x.astype(F32)
        inverse = inverse_of(x)
        normed = x * inverse
        grad = a.astype(F32) + b.astype(F32)
        grad = order.from_rel(grad)
        grad = grad * gain if scaled else grad
        shared = jnp.mean(grad * normed, -1, keepdims=True)
        total = g.astype(F32) + inverse * (grad - normed * shared)
        return (total, total.astype(BF)) if low else (total,)
    specs = row_specs(6, rows, width, 2)
    outs = [shape_of((rows, width), F32)] + ([shape_of((rows, width), BF)] if low else [])
    return run(
        functools.partial(back_kernel, order, scaled),
        [order.mine, x, g, a, b] + ([gain] if scaled else []),
        outs,
        [SMEM] + specs[:4] + [pl.BlockSpec((1, width), lambda i: (0, 0))] * scaled,
        specs[: len(outs)],
        (2,),
        scratch=[pltpu.VMEM((rows // 2, width), F32)],
    )


def result_kernel(order, mine_ref, mid_ref, a_ref, b_ref, out_ref):
    mine = [mine_ref[i] for i in range(5)]

    def write(t, value):
        out_ref[:, tile(t)] = (mid_ref[:, tile(t)] + value).astype(BF)

    order.from_tiles(
        lambda i: a_ref[:, tile(i)].astype(F32) + b_ref[:, tile(i)].astype(F32), write, mine
    )


def result_of(order, mid, a, b):
    rows, width = mid.shape
    if not order.fast:
        return (mid + order.from_rel(a.astype(F32) + b.astype(F32))).astype(BF)
    specs = row_specs(4, rows, width, 2)
    return run(
        functools.partial(result_kernel, order),
        [order.mine, mid, a, b],
        [shape_of((rows, width), BF)],
        [SMEM] + specs[:3],
        specs[:1],
        (2,),
    )[0]


def pack_kernel(count, kinds, *refs):
    out_ref = refs[-1]
    cols = out_ref.shape[-1]
    depth = refs[0].shape[0]
    for m in range(kinds):
        value = refs[m][...].astype(F32)
        if len(refs) > kinds + 1:
            value = value * refs[kinds][...]
        for t in range(count):
            out_ref[t, m * depth : (m + 1) * depth] = value[:, t * cols : (t + 1) * cols].astype(BF)


def pack(weights, gain, count):
    depth, width = weights[0].shape
    return run(
        functools.partial(pack_kernel, count, len(weights)),
        weights + ([] if gain is None else [gain]),
        [shape_of((count, len(weights) * depth, width // count), BF)],
    )[0]


def unpack_kernel(p_ref, gate_ref, up_ref, gain_ref, gate_out, up_out, down_out, sum_ref):
    count, depth, cols = p_ref.shape
    depth = depth // 3
    total = jnp.zeros((depth, 1), F32)
    for t in range(count):
        lanes = slice(t * cols, (t + 1) * cols)
        for m, (w_ref, out_ref) in enumerate([(gate_ref, gate_out), (up_ref, up_out)]):
            part = p_ref[t, m * depth : (m + 1) * depth].astype(F32)
            total = total + jnp.sum(part * w_ref[:, lanes].astype(F32), -1, keepdims=True)
            out_ref[:, lanes] = part * gain_ref[...]
        down_out[:, lanes] = p_ref[t, 2 * depth :].astype(F32)
    sum_ref[...] = total


def pack_qkv_kernel(count, me_ref, q_ref, k_ref, v_ref, out_ref):
    for t in range(count):
        slot = me_ref[0] ^ t
        out_ref[slot, :, :HEAD_COLS] = q_ref[:, t * HEAD_COLS : (t + 1) * HEAD_COLS]
        lanes = slice(t * HEAD_DIM, (t + 1) * HEAD_DIM)
        both = jnp.concatenate([k_ref[:, lanes].astype(F32), v_ref[:, lanes].astype(F32)], -1)
        out_ref[slot, :, HEAD_COLS:] = both.astype(BF)


def place_kernel(count, me_ref, *refs):
    for r in range(count):
        refs[-1][me_ref[0] ^ r] = refs[r][...]


def columns_kernel(kinds, in_ref, *outs):
    count, depth, units = in_ref.shape
    depth = depth // kinds
    step = max(1, 128 // depth)
    for m in range(kinds):
        for t in range(0, count, step):
            rows = [in_ref[t + i, m * depth : (m + 1) * depth] for i in range(step)]
            both = jnp.concatenate(rows, 0).astype(F32)
            outs[m][:, t * depth : (t + step) * depth] = both.T.astype(BF)


def rows_kernel(depth, *refs):
    out_ref = refs[-1]
    count, _, units = out_ref.shape
    step = max(1, 128 // depth)
    m = 0
    for ref in refs[:-1]:
        for first in range(0, ref.shape[0], units):
            for t in range(0, count, step):
                lanes = slice(t * depth, (t + step) * depth)
                both = ref[first : first + units, lanes].astype(F32).T
                for i in range(step):
                    rows = both[i * depth : (i + 1) * depth]
                    out_ref[t + i, m * depth : (m + 1) * depth] = rows.astype(BF)
            m += 1


def unpack_qkv_kernel(count, q_ref, k_ref, v_ref, g_ref, p_ref, qo_ref, ko_ref, vo_ref, sum_ref):
    gain = g_ref[...]
    total = jnp.zeros_like(gain)
    for t in range(count):
        part = p_ref[t].astype(F32)
        lanes = slice(t * HEAD_COLS, (t + 1) * HEAD_COLS)
        thin = slice(t * HEAD_DIM, (t + 1) * HEAD_DIM)
        gq = part[:, :HEAD_COLS]
        gk = part[:, HEAD_COLS : HEAD_COLS + HEAD_DIM]
        gv = part[:, HEAD_COLS + HEAD_DIM :]
        total = total + jnp.sum(gq * q_ref[:, lanes].astype(F32), -1, keepdims=True)
        total = total + jnp.sum(gk * k_ref[:, thin].astype(F32), -1, keepdims=True)
        total = total + jnp.sum(gv * v_ref[:, thin].astype(F32), -1, keepdims=True)
        qo_ref[:, lanes] = gq
        ko_ref[:, thin] = gk
        vo_ref[:, thin] = gv
    sum_ref[...] = total / gain


def swap_halves(values):
    width = values.shape[-1]
    lanes = lax.broadcasted_iota(jnp.int32, (1, width), 1)
    return jnp.where(
        lanes % HEAD_DIM < HEAD_DIM // 2,
        pltpu.roll(values, width - HEAD_DIM // 2, 1),
        pltpu.roll(values, HEAD_DIM // 2, 1),
    )


def project_kernel(repeat, count, *refs):
    a_ref, cos_ref, sin_ref = refs[:3]
    w_refs, q_ref, kv_ref = refs[3 : 3 + count], refs[-2], refs[-1]
    piece = w_refs[0].shape[0]
    raw = None
    for k in range(count):
        term = dot(a_ref[:, k * piece : (k + 1) * piece], w_refs[k][...])
        raw = term if raw is None else raw + term
    cosine = jnp.concatenate([cos_ref[...]] * repeat, 0)
    sine = jnp.concatenate([sin_ref[...]] * repeat, 0)
    out = (raw * cosine + swap_halves(raw) * sine).astype(BF)
    q_ref[...] = out[:, :HEAD_COLS]
    kv_ref[...] = out[:, HEAD_COLS:]


def project(a1, cosine, sine, parts):
    rows, width = a1.shape
    seq_dev, cols = cosine.shape
    block = min(2 * seq_dev, rows)
    fixed = lambda i: (0, 0)
    moving = lambda i: (i, 0)
    return run(
        functools.partial(project_kernel, block // seq_dev, len(parts)),
        [a1, cosine, sine] + parts,
        [shape_of((rows, HEAD_COLS), BF), shape_of((rows, 2 * HEAD_DIM), BF)],
        [pl.BlockSpec((block, width), moving)]
        + [pl.BlockSpec((seq_dev, cols), fixed)] * 2
        + [pl.BlockSpec(p.shape, fixed) for p in parts],
        [pl.BlockSpec((block, HEAD_COLS), moving), pl.BlockSpec((block, 2 * HEAD_DIM), moving)],
        (rows // block,),
        flops=2 * rows * width * cols,
    )


def stack_heads(values):
    return jnp.concatenate(
        [values[:, j * HEAD_DIM : (j + 1) * HEAD_DIM] for j in range(GROUPS)], 0
    )


def soft_weights(queries, keys, key_ref, seq_dev):
    scores = dot_nt(queries, keys) * FACTOR
    place = lax.broadcasted_iota(jnp.int32, (queries.shape[0], 1), 0) % seq_dev
    return jnp.where(place >= key_ref[...], jnp.exp(scores), 0.0)


def attend_kernel(q_ref, kv_ref, key_ref, o_ref):
    seq_dev = q_ref.shape[0]
    both = kv_ref[...].reshape(-1, 2 * HEAD_DIM)
    keys, values = both[:, :HEAD_DIM], both[:, HEAD_DIM:]
    weights = soft_weights(stack_heads(q_ref[...]), keys, key_ref, seq_dev)
    totals = jnp.sum(weights, -1, keepdims=True)
    attended = dot(weights.astype(BF), values) / totals
    for j in range(GROUPS):
        rows = attended[j * seq_dev : (j + 1) * seq_dev]
        o_ref[:, j * HEAD_DIM : (j + 1) * HEAD_DIM] = rows.astype(BF)


def attend(queries, kv, key_places, seq_dev):
    rows = queries.shape[0]
    count, seqs = kv.shape[:2]
    return run(
        attend_kernel,
        [queries, kv, key_places],
        [shape_of((rows, HEAD_COLS), BF)],
        [
            pl.BlockSpec((seq_dev, HEAD_COLS), lambda s: (s, 0)),
            pl.BlockSpec((count, 1, seq_dev, 2 * HEAD_DIM), lambda s: (0, s, 0, 0)),
            pl.BlockSpec((1, count * seq_dev), lambda s: (0, 0)),
        ],
        [pl.BlockSpec((seq_dev, HEAD_COLS), lambda s: (s, 0))],
        (seqs,),
        flops=4 * rows * GROUPS * HEAD_DIM * count * seq_dev,
    )[0]


def attend_back_kernel(q_ref, kv_ref, key_ref, do_ref, cos_ref, sin_ref, dq_ref, dkv_ref, mid_ref):
    seq_dev = q_ref.shape[0]
    both = kv_ref[...].reshape(-1, 2 * HEAD_DIM)
    keys, values = both[:, :HEAD_DIM], both[:, HEAD_DIM:]
    queries = stack_heads(q_ref[...])
    weights = soft_weights(queries, keys, key_ref, seq_dev)
    totals = jnp.sum(weights, -1, keepdims=True)
    low = weights.astype(BF)
    attended = dot(low, values) / totals
    grads = stack_heads(do_ref[...])
    deltas = jnp.sum(grads * attended, -1, keepdims=True) / totals
    mixed = (grads / totals).astype(BF)
    scores = (weights * (dot_nt(mixed, values) - deltas)).astype(BF)
    turned = dot(scores, keys) * FACTOR
    for j in range(GROUPS):
        mid_ref[:, j * HEAD_DIM : (j + 1) * HEAD_DIM] = turned[j * seq_dev : (j + 1) * seq_dev]
    whole = mid_ref[...]
    cosine, sine = cos_ref[:, :HEAD_COLS], sin_ref[:, :HEAD_COLS]
    dq_ref[...] = (whole * cosine - swap_halves(whole) * sine).astype(BF)
    grad_keys = dot_tn(scores, queries) * FACTOR
    grad_values = dot_tn(low, mixed)
    joined = jnp.concatenate([grad_keys, grad_values], -1)
    dkv_ref[...] = joined.astype(BF).reshape(dkv_ref.shape)


def attend_back(queries, kv, key_places, grads, cosine, sine, seq_dev):
    rows = queries.shape[0]
    count, seqs = kv.shape[:2]
    own = pl.BlockSpec((seq_dev, HEAD_COLS), lambda s: (s, 0))
    table = pl.BlockSpec(cosine.shape, lambda s: (0, 0))
    blocks = pl.BlockSpec((count, 1, seq_dev, 2 * HEAD_DIM), lambda s: (0, s, 0, 0))
    return run(
        attend_back_kernel,
        [queries, kv, key_places, grads, cosine, sine],
        [shape_of((rows, HEAD_COLS), BF), shape_of(kv.shape, BF)],
        [own, blocks, pl.BlockSpec((1, count * seq_dev), lambda s: (0, 0)), own, table, table],
        [own, blocks],
        (seqs,),
        scratch=[pltpu.VMEM((seq_dev, HEAD_COLS), F32)],
        flops=14 * rows * GROUPS * HEAD_DIM * count * seq_dev,
    )


def turn_back_kernel(repeat, a_ref, b_ref, cos_ref, sin_ref, out_ref):
    total = a_ref[...].astype(F32) + b_ref[...].astype(F32)
    cosine = jnp.concatenate([cos_ref[:, HEAD_COLS:]] * repeat, 0)
    sine = jnp.concatenate([sin_ref[:, HEAD_COLS:]] * repeat, 0)
    out_ref[...] = (total * cosine - swap_halves(total) * sine).astype(BF)


def wide_kernel(product, left_ref, *refs):
    rights, out_ref = refs[:-1], refs[-1]
    cols = out_ref.shape[1] // len(rights)
    for k, right in enumerate(rights):
        out_ref[:, k * cols : (k + 1) * cols] = product(left_ref[...], right[...]).astype(BF)


def wide(product, left, rights, width, block):
    rows, depth = left.shape
    return run(
        functools.partial(wide_kernel, product),
        [left] + rights,
        [shape_of((rows, width), BF)],
        [pl.BlockSpec((block, depth), lambda i: (i, 0))]
        + [pl.BlockSpec(r.shape, lambda i: (0, 0)) for r in rights],
        [pl.BlockSpec((block, width), lambda i: (i, 0))],
        (rows // block,),
        vmem=48,
        flops=2 * rows * depth * width,
    )[0]


def either(first_ref, second_ref):
    steps = pl.num_programs(0)
    return jnp.where(pl.program_id(0) < steps // 2, first_ref[...], second_ref[...])


def either_specs(block, width, steps):
    return [
        pl.BlockSpec((block, width), lambda i: (jnp.minimum(i, steps // 2 - 1), 0)),
        pl.BlockSpec((block, width), lambda i: (jnp.maximum(i - steps // 2, 0), 0)),
    ]


def gate_kernel(first_ref, second_ref, gate_ref, up_ref, hid_ref, one_ref, two_ref):
    units, cols = hid_ref.shape[1], gate_ref.shape[1]
    rows = either(first_ref, second_ref)
    gate = up = None
    for k in range(rows.shape[1] // cols):
        part = rows[:, k * cols : (k + 1) * cols]
        g = dot_nt(part, gate_ref[k * units : (k + 1) * units])
        u = dot_nt(part, up_ref[k * units : (k + 1) * units])
        gate = g if gate is None else gate + g
        up = u if up is None else up + u
    sigmoid = jax.nn.sigmoid(gate)
    active = gate * sigmoid
    hid_ref[...] = (active * up).astype(BF)
    one_ref[...] = up * sigmoid * (1.0 + gate * (1.0 - sigmoid))
    two_ref[...] = active


def gate_up(a2, gate, up, units, block):
    rows, width = 2 * a2[0].shape[0], a2[0].shape[1]
    moving = lambda i: (i, 0)
    out = pl.BlockSpec((block, units), moving)
    return run(
        gate_kernel,
        [*a2, gate, up],
        [shape_of((rows, units), BF), shape_of((rows, units), F32), shape_of((rows, units), F32)],
        either_specs(block, width, rows // block) + [pl.BlockSpec(gate.shape, lambda i: (0, 0))] * 2,
        [out, out, out],
        (rows // block,),
        vmem=48,
    )


def hidden_kernel(first_ref, second_ref, one_ref, two_ref, down_ref, gate_ref, up_ref, dboth_ref, out_ref):
    units, cols = one_ref.shape[1], down_ref.shape[1]
    rows = either(first_ref, second_ref)
    pieces = rows.shape[1] // cols
    total = None
    for k in range(pieces):
        term = dot_nt(rows[:, k * cols : (k + 1) * cols], down_ref[k * units : (k + 1) * units])
        total = term if total is None else total + term
    dgate = (total * one_ref[...]).astype(BF)
    dup = (total * two_ref[...]).astype(BF)
    dboth_ref[:, :units] = dgate
    dboth_ref[:, units:] = dup
    for k in range(pieces):
        part = dot(dgate, gate_ref[k * units : (k + 1) * units])
        part = part + dot(dup, up_ref[k * units : (k + 1) * units])
        out_ref[:, k * cols : (k + 1) * cols] = part.astype(BF)


def hidden_back(gb, one, two, down, gate, up, block):
    rows, width = 2 * gb[0].shape[0], gb[0].shape[1]
    units = one.shape[1]
    moving = lambda i: (i, 0)
    fixed = lambda i: (0, 0)
    thin = pl.BlockSpec((block, units), moving)
    full = pl.BlockSpec((block, width), moving)
    return run(
        hidden_kernel,
        [*gb, one, two, down, gate, up],
        [shape_of((rows, 2 * units), BF), shape_of((rows, width), BF)],
        either_specs(block, width, rows // block) + [thin, thin] + [pl.BlockSpec(down.shape, fixed)] * 3,
        [pl.BlockSpec((block, 2 * units), moving), full],
        (rows // block,),
        vmem=56,
    )


def result_rows_kernel(h_ref, down_ref, out_ref):
    units, cols = h_ref.shape[1], down_ref.shape[1]
    for k in range(out_ref.shape[1] // cols):
        part = dot(h_ref[...], down_ref[k * units : (k + 1) * units])
        out_ref[:, k * cols : (k + 1) * cols] = part.astype(BF)


def result_rows(hidden, down, width, block):
    rows, units = hidden.shape
    moving = lambda i: (i, 0)
    return run(
        result_rows_kernel,
        [hidden, down],
        [shape_of((rows, width), BF)],
        [pl.BlockSpec((block, units), moving), pl.BlockSpec(down.shape, lambda i: (0, 0))],
        [pl.BlockSpec((block, width), moving)],
        (rows // block,),
    )[0]


def weight_grad_kernel(left_ref, first_ref, second_ref, out_ref):
    half = first_ref.shape[0]
    total = dot_tn(left_ref[:half], first_ref[...]) + dot_tn(left_ref[half:], second_ref[...])
    out_ref[...] = total.astype(BF)


def weight_grad(left, right, pieces):
    rows, units = left.shape
    cols = right[0].shape[1] // pieces
    return run(
        weight_grad_kernel,
        [left, *right],
        [shape_of((pieces * units, cols), BF)],
        [pl.BlockSpec((rows, units), lambda i: (0, 0)), *[pl.BlockSpec((rows // 2, cols), lambda i: (0, i))] * 2],
        [pl.BlockSpec((units, cols), lambda i: (i, 0))],
        (pieces,),
        vmem=48,
    )[0]


def gather_rows(value, bits, what):
    acc = value
    for bit in bits:
        acc = jnp.concatenate([acc, bit.swap(acc, what)], 0)
    return acc


def reduce_rows(acc, bits, what):
    steps = []
    for bit in reversed(bits):
        half = acc.shape[0] // 2
        steps.append((acc[:half], bit.swap(acc[half:], what)))
        acc = add_low(*steps[-1])
    return steps


def gather_team(value, bit_x, near, bit_core, what, marks):
    half = value.shape[0] // 2
    by_x, by_near = bit_x.swap(value, what), near.swap(value, what)
    diagonal = [bit_x.swap(by_near[:half], what), near.swap(by_x[half:], what)]
    four = after(jnp.concatenate([value, by_x, by_near] + diagonal, 0), *marks)
    return four, bit_core.swap(four, what)


def add_low(a, b):
    return (a.astype(F32) + b.astype(F32)).astype(BF)


def reduce_four(acc, got, bit_x, near, what):
    half = acc.shape[0]
    acc = add_low(acc, got)
    rows = half // 4
    own, by_x, by_near = acc[:rows], acc[rows : 2 * rows], acc[2 * rows : 3 * rows]
    first, second = acc[3 * rows : 3 * rows + rows // 2], acc[3 * rows + rows // 2 :]
    got_near = bit_x.swap(first, what)
    got_x = near.swap(second, what)
    by_near = jnp.concatenate([add_low(by_near[: rows // 2], got_near), by_near[rows // 2 :]], 0)
    by_x = jnp.concatenate([by_x[: rows // 2], add_low(by_x[rows // 2 :], got_x)], 0)
    return (add_low(own, bit_x.swap(by_x, what)), near.swap(by_near, what)), by_x


def absolute(blocks, index, bits):
    def one(j):
        other = index ^ j
        slot = sum(((other >> b.bit) & 1) << i for i, b in enumerate(bits))
        return lax.dynamic_index_in_dim(blocks, slot, 0, False)

    return jnp.stack([one(j) for j in range(blocks.shape[0])])


def relative(blocks, index, bits):
    def one(r):
        code = sum(((r >> i) & 1) << b.bit for i, b in enumerate(bits))
        return lax.dynamic_index_in_dim(blocks, index ^ code, 0, False)

    return jnp.stack([one(r) for r in range(blocks.shape[0])])


def shards(
    dp,
    ctx,
    tokens,
    cotangent,
    attn_gain,
    query_weight,
    key_weight,
    value_weight,
    output_weight,
    mlp_gain,
    gate_weight,
    up_weight,
    down_weight,
):
    seqs, seq_dev, width = tokens.shape
    rows = seqs * seq_dev
    depth = query_weight.shape[0]
    c_index = lax.axis_index("ctx")

    bit_x, bit_core = Bit("dp", 1, dp), Bit("dp", 0, dp)
    ctx_bits = [Bit("ctx", b, ctx) for b in reversed(range(ctx.bit_length() - 1))]
    near = ctx_bits[-1]
    far = [b for b in ctx_bits if b is not near]
    dp_bits = [bit_x, bit_core]
    names = dp_bits + ctx_bits
    attn_order = Order(names, list(reversed(ctx_bits)) + dp_bits, ctx_bits, depth)
    mlp_order = Order(names, far + dp_bits + [near], [], depth)
    x = tokens.reshape(rows, width)
    cot = cotangent.reshape(rows, width)
    gain_one = attn_gain.astype(F32)[:, None]
    gain_two = mlp_gain.astype(F32)[:, None]

    team_groups = []
    for c in range(ctx):
        if not (c >> near.bit) & 1:
            team_groups.append([d * ctx + (c | (n << near.bit)) for d in range(dp) for n in range(2)])
    team = 2 * dp

    def mlp_trade(parts):
        return lax.all_to_all(
            parts, ("dp", "ctx"), 0, 0, axis_index_groups=team_groups, tiled=True
        )

    def mlp_slices(weights, gain, *marks):
        kinds = len(weights)
        parts = after(mlp_trade(pack(weights, gain, team)), *marks)
        shape = (parts.shape[2], team * depth)
        return run(functools.partial(columns_kernel, kinds), [parts], [shape_of(shape, BF)] * kinds)

    def mlp_rows(sums):
        kinds = sum(t.shape[0] for t in sums) // units
        shape = (team, kinds * depth, units)
        return mlp_trade(run(functools.partial(rows_kernel, depth), sums, [shape_of(shape, BF)])[0])

    far_groups = []
    for n in range(2):
        far_groups.append([c for c in range(ctx) if (c >> near.bit) & 1 == n])
    pieces = ctx // 2

    def far_gather(own):
        return lax.all_gather(own, "ctx", axis=0, tiled=True, axis_index_groups=far_groups)

    def far_reduce(terms):
        return lax.psum_scatter(
            terms, "ctx", scatter_dimension=0, tiled=True, axis_index_groups=far_groups
        )

    qkv_cols = HEAD_COLS + 2 * HEAD_DIM
    me = lax.axis_index("dp").astype(jnp.int32).reshape(1)
    slices = run(
        functools.partial(pack_qkv_kernel, dp),
        [me, query_weight, key_weight, value_weight],
        [shape_of((dp, depth, qkv_cols), BF)],
        [SMEM] + [pl.BlockSpec(memory_space=pltpu.VMEM)] * 3,
    )[0]
    out_acc = [output_weight]
    for bit in ctx_bits[:-1]:
        out_acc.append(jnp.concatenate([out_acc[-1], bit.swap(out_acc[-1], "out")], 0))
    slices = [slices[0]] + [swap_difference(slices[r], "dp", dp, r, "slice") for r in range(1, dp)]
    own = run(
        functools.partial(place_kernel, dp),
        [me, after(slices[0], out_acc[1])] + slices[1:],
        [shape_of((dp, depth, qkv_cols), BF)],
        [SMEM] + [pl.BlockSpec(memory_space=pltpu.VMEM)] * dp,
    )[0].reshape(dp * depth, qkv_cols)
    halves = [own]
    for i, bit in enumerate(ctx_bits[:-1]):
        sent = halves[-1] if i == 0 else after(halves[-1], out_acc[i + 1])
        halves.append(jnp.concatenate([sent, bit.swap(sent, "qkv")], 0))
    qkv = [halves[-1], ctx_bits[-1].swap(halves[-1], "qkv")]
    out_rel = after(out_acc[-1], qkv[1])
    out_rel = jnp.concatenate([out_rel, ctx_bits[-1].swap(out_rel, "out")], 0)
    out_full = absolute(out_rel.reshape(ctx, depth, width), c_index, ctx_bits)
    out_full = out_full.reshape(ctx * depth, width)

    gate_own, up_own = mlp_slices([after(gate_weight, own), up_weight], gain_two, halves[-1])
    gain_all = jnp.broadcast_to(after(attn_gain, gate_own)[None], (dp * ctx, depth))
    gain_all = lax.all_to_all(gain_all, ("dp", "ctx"), 0, 0, tiled=True)
    gain_all = gain_all.reshape(1, width).astype(F32)
    a1_half = gather_rows(norm_to(attn_order, x, gain_all), dp_bits[:1], "a1")
    a1 = gather_rows(a1_half, dp_bits[1:], "a1")
    gate = far_gather(gate_own)
    (down_own,) = mlp_slices([after(down_weight.T, gain_all)], None)
    units = down_own.shape[0]

    places = jnp.arange(seq_dev, dtype=jnp.int32)
    half_dim = HEAD_DIM // 2
    freqs = rope_base ** (-(jnp.arange(half_dim, dtype=F32) * 2.0) / HEAD_DIM)
    angles = (c_index * seq_dev + places).astype(F32)[:, None] * freqs[None, :]
    cosine, sine = jnp.cos(angles), jnp.sin(angles)
    cosine = jnp.concatenate([cosine, cosine] * (GROUPS + 1) + [jnp.ones((seq_dev, HEAD_DIM), F32)], -1)
    sine = jnp.concatenate([-sine, sine] * (GROUPS + 1) + [jnp.zeros((seq_dev, HEAD_DIM), F32)], -1)
    rel = jnp.arange(ctx, dtype=jnp.int32)
    others = sum(((rel >> i) & 1) << b.bit for i, b in enumerate(ctx_bits)) ^ c_index
    key_places = (((others - c_index) * seq_dev)[:, None] + places[None, :]).reshape(1, -1)

    queries, kv_own = project(a1, cosine, sine, qkv)
    all_seqs = dp * seqs
    kv = kv_own
    for i, bit in enumerate(ctx_bits):
        if i == 1:
            kv = after(kv, down_own)
        if i == len(ctx_bits) - 2:
            up = far_gather(after(up_own, kv))
            down = far_gather(after(down_own, kv))
        kv = jnp.concatenate([kv, bit.swap(kv, "kv")], 0)
    kv = kv.reshape(ctx, all_seqs, seq_dev, 2 * HEAD_DIM)
    heads = attend(queries, kv, key_places, seq_dev)
    branch = dot(heads, out_full).astype(BF)
    branch = reduce_rows(branch, dp_bits, "branch")[-1]
    middle, a2 = middle_to(mlp_order, x, *branch)

    gb = gather_team(order_to(mlp_order, after(cot, middle)), bit_x, near, bit_core, "gb", [])
    a2 = gather_team(a2, bit_x, near, bit_core, "a2", [])
    block = min(256, a2[0].shape[0])
    hidden, one, two = gate_up(a2, gate, up, units, block)
    down_terms = weight_grad(hidden, gb, pieces)
    down_back = far_reduce(down_terms)
    dboth, da2 = hidden_back((after(gb[0], down_terms), gb[1]), one, two, down, gate, up, block)
    half = da2.shape[0] // 2
    da2_got = bit_core.swap(da2[half:], "da2")
    da2_two, da2_mark = reduce_four(da2[:half], da2_got, bit_x, near, "da2")
    down_out = result_rows(after(hidden, da2), down, width, block)
    result_got = bit_core.swap(after(down_out[half:], da2_mark), "result")
    both_terms = weight_grad(dboth, (after(a2[0], da2_mark), a2[1]), pieces)
    both_back = far_reduce(both_terms)
    grad_middle, db = norm_back(mlp_order, middle, after(cot, both_terms, result_got), *da2_two, low=True)
    grad_branch = gather_rows(db, dp_bits, "db")
    result_two, result_mark = reduce_four(
        down_out[:half], after(result_got, db), bit_x, near, "result"
    )
    result = result_of(mlp_order, middle, *result_two)

    grad_heads = dot_nt(grad_branch, out_full)
    dq, dkv = attend_back(
        queries, kv, after(key_places, *result_two), grad_heads, cosine, sine, seq_dev
    )

    class Sum:
        def __init__(self, terms, what):
            self.terms, self.what, self.bits = terms, what, list(reversed(ctx_bits))

        def step(self, *marks):
            half = self.terms.shape[0] // 2
            sent = after(self.terms[half:], *marks) if marks else self.terms[half:]
            self.pair = self.terms[:half], self.bits.pop(0).swap(sent, self.what)
            self.terms = add_low(*self.pair)
            return self.pair[1]

        def finish(self, *marks):
            while self.bits:
                self.step(*marks)
            return self.pair

    dkv_sum = Sum(dkv.reshape(-1, 2 * HEAD_DIM), "dkv")
    dkv_first = dkv_sum.step()
    dq_sum = Sum(dot_tn(a1, after(dq, dkv_first)).astype(BF), "dq_w")
    dq_first = dq_sum.step()
    dkv_sum.step(down_back)
    dkv_two = dkv_sum.finish()
    dkv_low = run(
        functools.partial(turn_back_kernel, all_seqs),
        [after(dkv_two[0], dq_first), dkv_two[1]] + [cosine, sine],
        [shape_of((dp * rows, 2 * HEAD_DIM), BF)],
    )[0]
    kv_sum = Sum(dot_tn(a1, dkv_low).astype(BF), "dkv_w")
    kv_first = kv_sum.step()
    da1 = wide(dot_nt, jnp.concatenate([dq, dkv_low], -1), qkv, width, min(256, dp * rows))
    da1_steps = reduce_rows(da1, dp_bits, "da1")
    da1_two = da1_steps[-1]
    (grad_tokens,) = norm_back(attn_order, x, grad_middle, *da1_two, gain_all)
    dq_second = dq_sum.step()
    kv_second = kv_sum.step(dq_second, da1_steps[0][1])
    out_total = dot_tn(heads, grad_branch).astype(BF).reshape(ctx, depth, width)
    out_total = relative(after(out_total, kv_first), c_index, ctx_bits).reshape(ctx * depth, width)
    out_sum = Sum(out_total, "dout_w")
    out_first = out_sum.step()
    all_back = mlp_rows([after(both_back, kv_first), down_back])
    dq_two = dq_sum.finish()
    kv_two = kv_sum.finish(dq_two[1], *da1_two)
    out_second = out_sum.step(kv_second)
    out_two = out_sum.finish()
    output_grad = out_two[0].astype(F32) + out_two[1].astype(F32)
    qkv_total = jnp.concatenate([add_low(*dq_two), add_low(*kv_two)], -1).reshape(dp, depth, qkv_cols)
    qkv_back = lax.all_to_all(after(qkv_total, all_back), "dp", 0, 0, tiled=True)

    wide_shape = shape_of(gate_weight.shape, F32)
    gate_grad, up_grad, down_grad, mlp_sum = run(
        unpack_kernel,
        [all_back, gate_weight, up_weight, gain_two],
        [wide_shape, wide_shape, wide_shape, shape_of((depth, 1), F32)],
    )
    down_grad = down_grad.T
    query_grad, key_grad, value_grad, attn_sum = run(
        functools.partial(unpack_qkv_kernel, dp),
        [query_weight, key_weight, value_weight, gain_one, qkv_back],
        [shape_of(w.shape, F32) for w in (query_weight, key_weight, value_weight, gain_one)],
    )
    return (
        result.reshape(seqs, seq_dev, width),
        grad_tokens.reshape(seqs, seq_dev, width),
        attn_sum[:, 0],
        query_grad,
        key_grad,
        value_grad,
        output_grad,
        mlp_sum[:, 0],
        gate_grad,
        up_grad,
        down_grad,
    )


def solution(mesh):
    dp, ctx = mesh.shape["dp"], mesh.shape["ctx"]

    def local(*args):
        return shards(dp, ctx, *args)

    weight = P(("dp", "ctx"), None)
    flat = P(("dp", "ctx"))
    acts = P("dp", "ctx", None)
    down = P(None, ("dp", "ctx"))
    return jax.shard_map(
        local,
        mesh=mesh,
        in_specs=(acts, acts, flat, weight, weight, weight, weight, flat, weight, weight, down),
        out_specs=(acts, acts, flat, weight, weight, weight, weight, flat, weight, weight, down),
        check_vma=False,
    )
```

```python
import functools
import math

import jax
import jax.numpy as jnp
from jax import lax
from jax.experimental import pallas as pl
from jax.experimental.pallas import tpu as pltpu
from jax.sharding import PartitionSpec as P

HEADS = 32
KV_HEADS = 4
HEAD_DIM = 64
GROUPS = HEADS // KV_HEADS
HEAD_COLS = GROUPS * HEAD_DIM
FACTOR = 1.0 / math.sqrt(HEAD_DIM)

norm_eps = 1e-05
rope_base = 10000.0

BF = jnp.bfloat16
F32 = jnp.float32
MIB = 1 << 20


def dot(left, right):
    return jnp.dot(left, right, preferred_element_type=F32)


def dot_nt(left, right):
    return lax.dot_general(left, right, (((1,), (1,)), ((), ())), preferred_element_type=F32)


def dot_tn(left, right):
    return lax.dot_general(left, right, (((0,), (0,)), ((), ())), preferred_element_type=F32)


def shape_of(shape, kind):
    return jax.ShapeDtypeStruct(shape, kind)


def run(kernel, ins, outs, specs=None, out_specs=None, grid=None, vmem=32, scratch=(), flops=0):
    whole = pl.BlockSpec(memory_space=pltpu.VMEM)
    moved = sum(math.prod(a.shape) * a.dtype.itemsize for a in list(ins) + list(outs))
    extra = {} if grid is None else {"grid": grid}
    name = kernel.func.__name__ if isinstance(kernel, functools.partial) else kernel.__name__
    return pl.pallas_call(
        kernel,
        name=name,
        out_shape=list(outs),
        in_specs=specs or [whole] * len(ins),
        out_specs=out_specs or [whole] * len(outs),
        scratch_shapes=list(scratch),
        compiler_params=pltpu.CompilerParams(vmem_limit_bytes=vmem * MIB),
        cost_estimate=pl.CostEstimate(flops=0, bytes_accessed=0, transcendentals=0),
        **extra,
    )(*ins)


SMEM = pl.BlockSpec(memory_space=pltpu.SMEM)


class Bit:
    def __init__(self, axis, bit, size):
        self.axis, self.bit = axis, bit
        self.pairs = [(i, i ^ (1 << bit)) for i in range(size)]

    def mine(self):
        return (lax.axis_index(self.axis) >> self.bit) & 1

    def swap(self, value, what):
        with jax.named_scope(f"{what}_{self.axis}{self.bit}"):
            return lax.ppermute(value, self.axis, self.pairs)


def swap_difference(value, axis, size, difference, what):
    with jax.named_scope(f"{what}_{axis}"):
        return lax.ppermute(value, axis, [(i, i ^ difference) for i in range(size)])


def after(value, *others):
    return lax.optimization_barrier((value,) + others)[0]


class Order:
    def __init__(self, names, rel, gathered, depth):
        self.names, self.rel, self.gathered, self.depth = names, rel, gathered, depth
        self.whole_tiles = rel[-1] is names[-1] and not gathered
        self.fast = depth == 64 and len(names) == 5 and (
            self.whole_tiles or (rel[-1] is not names[-1] and rel[-1] not in gathered)
        )
        self.mine = jnp.stack(
            [b.mine() if b in gathered else jnp.zeros((), jnp.int32) for b in names]
        ).astype(jnp.int32)

    def to_tiles(self, read, write, mine):
        lanes = lax.broadcasted_iota(jnp.int32, (1, 128), 1)
        head = self.rel[:-1]
        last = self.rel[-1]
        for q in range(16):
            value = {b: (q >> (3 - i)) & 1 for i, b in enumerate(head)}
            if self.whole_tiles:
                write(q, read(sum(value[b] << (3 - i) for i, b in enumerate(self.names[:-1]))))
                continue

            def source(low):
                index = 0
                for i, b in enumerate(self.names[:-1]):
                    v = low if b is last else value[b]
                    if b in self.gathered:
                        v = v ^ mine[i]
                    index = index * 2 + v
                return read(index)

            a, b = source(0), source(1)
            side = value[self.names[-1]]
            low = lambda: jnp.where(lanes < 64, a, pltpu.roll(b, 64, 1))
            high = lambda: jnp.where(lanes < 64, pltpu.roll(a, 64, 1), b)
            if self.names[-1] in self.gathered:
                write(q, jnp.where((side ^ mine[4]) == 0, low(), high()))
            else:
                write(q, low() if side == 0 else high())

    def from_tiles(self, read, write, mine):
        lanes = lax.broadcasted_iota(jnp.int32, (1, 128), 1)
        for t in range(16):
            value = {b: (t >> (3 - i)) & 1 for i, b in enumerate(self.names[:-1])}
            if self.whole_tiles:
                write(t, read(sum(value[b] << (3 - i) for i, b in enumerate(self.rel[:-1]))))
                continue

            def source(y):
                index = 0
                for b in self.rel[:-1]:
                    v = y if b is self.names[-1] else value[b]
                    if b in self.gathered:
                        v = v ^ mine[self.names.index(b)]
                    index = index * 2 + v
                return read(index)

            low, high = source(0), source(1)
            if value[self.rel[-1]] == 0:
                write(t, jnp.where(lanes < 64, low, pltpu.roll(high, 64, 1)))
            else:
                write(t, jnp.where(lanes < 64, pltpu.roll(low, 64, 1), high))

    def to_rel(self, array):
        count, width = array.shape
        out = array.reshape((count,) + (2,) * len(self.names) + (self.depth,))
        for b in self.gathered:
            k = self.names.index(b) + 1
            out = jnp.where(b.mine() == 1, jnp.flip(out, k), out)
        axes = [self.names.index(b) + 1 for b in self.rel]
        return out.transpose([0] + axes + [len(self.names) + 1]).reshape(count, width)

    def from_rel(self, array):
        count, width = array.shape
        out = array.reshape((count,) + (2,) * len(self.names) + (self.depth,))
        axes = [self.rel.index(b) + 1 for b in self.names]
        out = out.transpose([0] + axes + [len(self.names) + 1])
        for b in self.gathered:
            k = self.names.index(b) + 1
            out = jnp.where(b.mine() == 1, jnp.flip(out, k), out)
        return out.reshape(count, width)


def tile(index):
    start = index * 128
    return pl.ds(start if isinstance(start, int) else pl.multiple_of(start, 128), 128)


def row_specs(count, rows, width, steps):
    return [pl.BlockSpec((rows // steps, width), lambda i: (i, 0))] * count


def inverse_of(x):
    return lax.rsqrt(jnp.mean(x * x, -1, keepdims=True) + norm_eps)


def norm_kernel(order, mine_ref, x_ref, gain_ref, out_ref):
    mine = [mine_ref[i] for i in range(5)]
    inverse = inverse_of(x_ref[...].astype(F32))

    def write(q, value):
        out_ref[:, tile(q)] = value.astype(BF)

    def read(i):
        return x_ref[:, tile(i)].astype(F32) * inverse * gain_ref[:, tile(i)]

    order.to_tiles(read, write, mine)


def norm_to(order, x, gain):
    if not order.fast:
        x = x.astype(F32)
        return order.to_rel((x * inverse_of(x) * gain).astype(BF))
    rows, width = x.shape
    specs = row_specs(2, rows, width, 2)
    return run(
        functools.partial(norm_kernel, order),
        [order.mine, x, gain],
        [shape_of((rows, width), BF)],
        [SMEM, specs[0], pl.BlockSpec((1, width), lambda i: (0, 0))],
        [specs[1]],
        (2,),
    )[0]


def order_kernel(order, mine_ref, x_ref, out_ref):
    mine = [mine_ref[i] for i in range(5)]

    def write(q, value):
        out_ref[:, tile(q)] = value.astype(out_ref.dtype)

    order.to_tiles(lambda i: x_ref[:, tile(i)].astype(F32), write, mine)


def order_to(order, x):
    if not order.fast:
        return order.to_rel(x)
    rows, width = x.shape
    specs = row_specs(2, rows, width, 2)
    return run(
        functools.partial(order_kernel, order),
        [order.mine, x],
        [shape_of((rows, width), x.dtype)],
        [SMEM, specs[0]],
        [specs[1]],
        (2,),
    )[0]


def middle_kernel(order, mine_ref, x_ref, a_ref, b_ref, mid_ref, out_ref):
    mine = [mine_ref[i] for i in range(5)]
    mid = x_ref[...].astype(F32) + a_ref[...].astype(F32) + b_ref[...].astype(F32)
    mid_ref[...] = mid
    inverse = inverse_of(mid)

    def write(q, value):
        out_ref[:, tile(q)] = value.astype(BF)

    order.to_tiles(lambda i: mid_ref[:, tile(i)] * inverse, write, mine)


def middle_to(order, x, a, b):
    rows, width = x.shape
    if not order.fast:
        mid = x.astype(F32) + a.astype(F32) + b.astype(F32)
        return mid, order.to_rel((mid * inverse_of(mid)).astype(BF))
    specs = row_specs(5, rows, width, 2)
    return run(
        functools.partial(middle_kernel, order),
        [order.mine, x, a, b],
        [shape_of((rows, width), F32), shape_of((rows, width), BF)],
        [SMEM] + specs[:3],
        specs[:2],
        (2,),
    )


def back_kernel(order, scaled, mine_ref, x_ref, g_ref, a_ref, b_ref, *outs):
    mine = [mine_ref[i] for i in range(5)]
    scratch = outs[-1]
    if scaled:
        gain_ref, outs = outs[0], outs[1:]
    inverse = inverse_of(x_ref[...].astype(F32))

    def write(t, value):
        scratch[:, tile(t)] = value * gain_ref[:, tile(t)] if scaled else value

    def read(i):
        return a_ref[:, tile(i)].astype(F32) + b_ref[:, tile(i)].astype(F32)

    order.from_tiles(read, write, mine)
    normed = x_ref[...].astype(F32) * inverse
    scaled = scratch[...]
    shared = jnp.mean(scaled * normed, -1, keepdims=True)
    total = g_ref[...].astype(F32) + inverse * (scaled - normed * shared)
    outs[0][...] = total
    if len(outs) == 3:
        outs[1][...] = total.astype(BF)


def norm_back(order, x, g, a, b, gain=None, low=False):
    rows, width = x.shape
    scaled = gain is not None
    if not order.fast:
        x = x.astype(F32)
        inverse = inverse_of(x)
        normed = x * inverse
        grad = a.astype(F32) + b.astype(F32)
        grad = order.from_rel(grad)
        grad = grad * gain if scaled else grad
        shared = jnp.mean(grad * normed, -1, keepdims=True)
        total = g.astype(F32) + inverse * (grad - normed * shared)
        return (total, total.astype(BF)) if low else (total,)
    specs = row_specs(6, rows, width, 2)
    outs = [shape_of((rows, width), F32)] + ([shape_of((rows, width), BF)] if low else [])
    return run(
        functools.partial(back_kernel, order, scaled),
        [order.mine, x, g, a, b] + ([gain] if scaled else []),
        outs,
        [SMEM] + specs[:4] + [pl.BlockSpec((1, width), lambda i: (0, 0))] * scaled,
        specs[: len(outs)],
        (2,),
        scratch=[pltpu.VMEM((rows // 2, width), F32)],
    )


def result_kernel(order, mine_ref, mid_ref, a_ref, b_ref, out_ref):
    mine = [mine_ref[i] for i in range(5)]

    def write(t, value):
        out_ref[:, tile(t)] = (mid_ref[:, tile(t)] + value).astype(BF)

    order.from_tiles(
        lambda i: a_ref[:, tile(i)].astype(F32) + b_ref[:, tile(i)].astype(F32), write, mine
    )


def result_of(order, mid, a, b):
    rows, width = mid.shape
    if not order.fast:
        return (mid + order.from_rel(a.astype(F32) + b.astype(F32))).astype(BF)
    specs = row_specs(4, rows, width, 2)
    return run(
        functools.partial(result_kernel, order),
        [order.mine, mid, a, b],
        [shape_of((rows, width), BF)],
        [SMEM] + specs[:3],
        specs[:1],
        (2,),
    )[0]


def pack_kernel(count, kinds, *refs):
    out_ref = refs[-1]
    cols = out_ref.shape[-1]
    depth = refs[0].shape[0]
    for m in range(kinds):
        value = refs[m][...].astype(F32)
        if len(refs) > kinds + 1:
            value = value * refs[kinds][...]
        for t in range(count):
            out_ref[t, m * depth : (m + 1) * depth] = value[:, t * cols : (t + 1) * cols].astype(BF)


def pack(weights, gain, count):
    depth, width = weights[0].shape
    return run(
        functools.partial(pack_kernel, count, len(weights)),
        weights + ([] if gain is None else [gain]),
        [shape_of((count, len(weights) * depth, width // count), BF)],
    )[0]


def unpack_kernel(p_ref, gate_ref, up_ref, gain_ref, gate_out, up_out, down_out, sum_ref):
    count, depth, cols = p_ref.shape
    depth = depth // 3
    total = jnp.zeros((depth, 1), F32)
    for t in range(count):
        lanes = slice(t * cols, (t + 1) * cols)
        for m, (w_ref, out_ref) in enumerate([(gate_ref, gate_out), (up_ref, up_out)]):
            part = p_ref[t, m * depth : (m + 1) * depth].astype(F32)
            total = total + jnp.sum(part * w_ref[:, lanes].astype(F32), -1, keepdims=True)
            out_ref[:, lanes] = part * gain_ref[...]
        down_out[:, lanes] = p_ref[t, 2 * depth :].astype(F32)
    sum_ref[...] = total


def pack_qkv_kernel(count, me_ref, q_ref, k_ref, v_ref, out_ref):
    for t in range(count):
        slot = me_ref[0] ^ t
        out_ref[slot, :, :HEAD_COLS] = q_ref[:, t * HEAD_COLS : (t + 1) * HEAD_COLS]
        lanes = slice(t * HEAD_DIM, (t + 1) * HEAD_DIM)
        both = jnp.concatenate([k_ref[:, lanes].astype(F32), v_ref[:, lanes].astype(F32)], -1)
        out_ref[slot, :, HEAD_COLS:] = both.astype(BF)


def place_kernel(count, me_ref, *refs):
    for r in range(count):
        refs[-1][me_ref[0] ^ r] = refs[r][...]


def columns_kernel(kinds, in_ref, *outs):
    count, depth, units = in_ref.shape
    depth = depth // kinds
    step = max(1, 128 // depth)
    for m in range(kinds):
        for t in range(0, count, step):
            rows = [in_ref[t + i, m * depth : (m + 1) * depth] for i in range(step)]
            both = jnp.concatenate(rows, 0).astype(F32)
            outs[m][:, t * depth : (t + step) * depth] = both.T.astype(BF)


def rows_kernel(depth, *refs):
    out_ref = refs[-1]
    count, _, units = out_ref.shape
    step = max(1, 128 // depth)
    m = 0
    for ref in refs[:-1]:
        for first in range(0, ref.shape[0], units):
            for t in range(0, count, step):
                lanes = slice(t * depth, (t + step) * depth)
                both = ref[first : first + units, lanes].astype(F32).T
                for i in range(step):
                    rows = both[i * depth : (i + 1) * depth]
                    out_ref[t + i, m * depth : (m + 1) * depth] = rows.astype(BF)
            m += 1


def unpack_qkv_kernel(count, q_ref, k_ref, v_ref, g_ref, p_ref, qo_ref, ko_ref, vo_ref, sum_ref):
    gain = g_ref[...]
    total = jnp.zeros_like(gain)
    for t in range(count):
        part = p_ref[t].astype(F32)
        lanes = slice(t * HEAD_COLS, (t + 1) * HEAD_COLS)
        thin = slice(t * HEAD_DIM, (t + 1) * HEAD_DIM)
        gq = part[:, :HEAD_COLS]
        gk = part[:, HEAD_COLS : HEAD_COLS + HEAD_DIM]
        gv = part[:, HEAD_COLS + HEAD_DIM :]
        total = total + jnp.sum(gq * q_ref[:, lanes].astype(F32), -1, keepdims=True)
        total = total + jnp.sum(gk * k_ref[:, thin].astype(F32), -1, keepdims=True)
        total = total + jnp.sum(gv * v_ref[:, thin].astype(F32), -1, keepdims=True)
        qo_ref[:, lanes] = gq
        ko_ref[:, thin] = gk
        vo_ref[:, thin] = gv
    sum_ref[...] = total / gain


def swap_halves(values):
    width = values.shape[-1]
    lanes = lax.broadcasted_iota(jnp.int32, (1, width), 1)
    return jnp.where(
        lanes % HEAD_DIM < HEAD_DIM // 2,
        pltpu.roll(values, width - HEAD_DIM // 2, 1),
        pltpu.roll(values, HEAD_DIM // 2, 1),
    )


def project_kernel(repeat, count, *refs):
    a_ref, cos_ref, sin_ref = refs[:3]
    w_refs, q_ref, kv_ref = refs[3 : 3 + count], refs[-2], refs[-1]
    piece = w_refs[0].shape[0]
    raw = None
    for k in range(count):
        term = dot(a_ref[:, k * piece : (k + 1) * piece], w_refs[k][...])
        raw = term if raw is None else raw + term
    cosine = jnp.concatenate([cos_ref[...]] * repeat, 0)
    sine = jnp.concatenate([sin_ref[...]] * repeat, 0)
    out = (raw * cosine + swap_halves(raw) * sine).astype(BF)
    q_ref[...] = out[:, :HEAD_COLS]
    kv_ref[...] = out[:, HEAD_COLS:]


def project(a1, cosine, sine, parts):
    rows, width = a1.shape
    seq_dev, cols = cosine.shape
    block = min(2 * seq_dev, rows)
    fixed = lambda i: (0, 0)
    moving = lambda i: (i, 0)
    return run(
        functools.partial(project_kernel, block // seq_dev, len(parts)),
        [a1, cosine, sine] + parts,
        [shape_of((rows, HEAD_COLS), BF), shape_of((rows, 2 * HEAD_DIM), BF)],
        [pl.BlockSpec((block, width), moving)]
        + [pl.BlockSpec((seq_dev, cols), fixed)] * 2
        + [pl.BlockSpec(p.shape, fixed) for p in parts],
        [pl.BlockSpec((block, HEAD_COLS), moving), pl.BlockSpec((block, 2 * HEAD_DIM), moving)],
        (rows // block,),
        flops=2 * rows * width * cols,
    )


def stack_heads(values):
    return jnp.concatenate(
        [values[:, j * HEAD_DIM : (j + 1) * HEAD_DIM] for j in range(GROUPS)], 0
    )


def soft_weights(queries, keys, key_ref, seq_dev):
    scores = dot_nt(queries, keys) * FACTOR
    place = lax.broadcasted_iota(jnp.int32, (queries.shape[0], 1), 0) % seq_dev
    return jnp.where(place >= key_ref[...], jnp.exp(scores), 0.0)


def attend_kernel(q_ref, kv_ref, key_ref, o_ref):
    seq_dev = q_ref.shape[0]
    both = kv_ref[...].reshape(-1, 2 * HEAD_DIM)
    keys, values = both[:, :HEAD_DIM], both[:, HEAD_DIM:]
    weights = soft_weights(stack_heads(q_ref[...]), keys, key_ref, seq_dev)
    totals = jnp.sum(weights, -1, keepdims=True)
    attended = dot(weights.astype(BF), values) / totals
    for j in range(GROUPS):
        rows = attended[j * seq_dev : (j + 1) * seq_dev]
        o_ref[:, j * HEAD_DIM : (j + 1) * HEAD_DIM] = rows.astype(BF)


def attend(queries, kv, key_places, seq_dev):
    rows = queries.shape[0]
    count, seqs = kv.shape[:2]
    return run(
        attend_kernel,
        [queries, kv, key_places],
        [shape_of((rows, HEAD_COLS), BF)],
        [
            pl.BlockSpec((seq_dev, HEAD_COLS), lambda s: (s, 0)),
            pl.BlockSpec((count, 1, seq_dev, 2 * HEAD_DIM), lambda s: (0, s, 0, 0)),
            pl.BlockSpec((1, count * seq_dev), lambda s: (0, 0)),
        ],
        [pl.BlockSpec((seq_dev, HEAD_COLS), lambda s: (s, 0))],
        (seqs,),
        flops=4 * rows * GROUPS * HEAD_DIM * count * seq_dev,
    )[0]


def attend_back_kernel(q_ref, kv_ref, key_ref, do_ref, cos_ref, sin_ref, dq_ref, dkv_ref, mid_ref):
    seq_dev = q_ref.shape[0]
    both = kv_ref[...].reshape(-1, 2 * HEAD_DIM)
    keys, values = both[:, :HEAD_DIM], both[:, HEAD_DIM:]
    queries = stack_heads(q_ref[...])
    weights = soft_weights(queries, keys, key_ref, seq_dev)
    totals = jnp.sum(weights, -1, keepdims=True)
    low = weights.astype(BF)
    attended = dot(low, values) / totals
    grads = stack_heads(do_ref[...])
    deltas = jnp.sum(grads * attended, -1, keepdims=True) / totals
    mixed = (grads / totals).astype(BF)
    scores = (weights * (dot_nt(mixed, values) - deltas)).astype(BF)
    turned = dot(scores, keys) * FACTOR
    for j in range(GROUPS):
        mid_ref[:, j * HEAD_DIM : (j + 1) * HEAD_DIM] = turned[j * seq_dev : (j + 1) * seq_dev]
    whole = mid_ref[...]
    cosine, sine = cos_ref[:, :HEAD_COLS], sin_ref[:, :HEAD_COLS]
    dq_ref[...] = (whole * cosine - swap_halves(whole) * sine).astype(BF)
    grad_keys = dot_tn(scores, queries) * FACTOR
    grad_values = dot_tn(low, mixed)
    joined = jnp.concatenate([grad_keys, grad_values], -1)
    dkv_ref[...] = joined.astype(BF).reshape(dkv_ref.shape)


def attend_back(queries, kv, key_places, grads, cosine, sine, seq_dev):
    rows = queries.shape[0]
    count, seqs = kv.shape[:2]
    own = pl.BlockSpec((seq_dev, HEAD_COLS), lambda s: (s, 0))
    table = pl.BlockSpec(cosine.shape, lambda s: (0, 0))
    blocks = pl.BlockSpec((count, 1, seq_dev, 2 * HEAD_DIM), lambda s: (0, s, 0, 0))
    return run(
        attend_back_kernel,
        [queries, kv, key_places, grads, cosine, sine],
        [shape_of((rows, HEAD_COLS), BF), shape_of(kv.shape, BF)],
        [own, blocks, pl.BlockSpec((1, count * seq_dev), lambda s: (0, 0)), own, table, table],
        [own, blocks],
        (seqs,),
        scratch=[pltpu.VMEM((seq_dev, HEAD_COLS), F32)],
        flops=14 * rows * GROUPS * HEAD_DIM * count * seq_dev,
    )


def turn_back_kernel(repeat, a_ref, b_ref, cos_ref, sin_ref, out_ref):
    total = a_ref[...].astype(F32) + b_ref[...].astype(F32)
    cosine = jnp.concatenate([cos_ref[:, HEAD_COLS:]] * repeat, 0)
    sine = jnp.concatenate([sin_ref[:, HEAD_COLS:]] * repeat, 0)
    out_ref[...] = (total * cosine - swap_halves(total) * sine).astype(BF)


def wide_kernel(product, left_ref, *refs):
    rights, out_ref = refs[:-1], refs[-1]
    cols = out_ref.shape[1] // len(rights)
    for k, right in enumerate(rights):
        out_ref[:, k * cols : (k + 1) * cols] = product(left_ref[...], right[...]).astype(BF)


def wide(product, left, rights, width, block):
    rows, depth = left.shape
    return run(
        functools.partial(wide_kernel, product),
        [left] + rights,
        [shape_of((rows, width), BF)],
        [pl.BlockSpec((block, depth), lambda i: (i, 0))]
        + [pl.BlockSpec(r.shape, lambda i: (0, 0)) for r in rights],
        [pl.BlockSpec((block, width), lambda i: (i, 0))],
        (rows // block,),
        vmem=48,
        flops=2 * rows * depth * width,
    )[0]


def either(first_ref, second_ref):
    steps = pl.num_programs(0)
    return jnp.where(pl.program_id(0) < steps // 2, first_ref[...], second_ref[...])


def either_specs(block, width, steps):
    return [
        pl.BlockSpec((block, width), lambda i: (jnp.minimum(i, steps // 2 - 1), 0)),
        pl.BlockSpec((block, width), lambda i: (jnp.maximum(i - steps // 2, 0), 0)),
    ]


def gate_kernel(first_ref, second_ref, gate_ref, up_ref, hid_ref, one_ref, two_ref):
    units, cols = hid_ref.shape[1], gate_ref.shape[1]
    rows = either(first_ref, second_ref)
    gate = up = None
    for k in range(rows.shape[1] // cols):
        part = rows[:, k * cols : (k + 1) * cols]
        g = dot_nt(part, gate_ref[k * units : (k + 1) * units])
        u = dot_nt(part, up_ref[k * units : (k + 1) * units])
        gate = g if gate is None else gate + g
        up = u if up is None else up + u
    sigmoid = jax.nn.sigmoid(gate)
    active = gate * sigmoid
    hid_ref[...] = (active * up).astype(BF)
    one_ref[...] = up * sigmoid * (1.0 + gate * (1.0 - sigmoid))
    two_ref[...] = active


def gate_up(a2, gate, up, units, block):
    rows, width = 2 * a2[0].shape[0], a2[0].shape[1]
    moving = lambda i: (i, 0)
    out = pl.BlockSpec((block, units), moving)
    return run(
        gate_kernel,
        [*a2, gate, up],
        [shape_of((rows, units), BF), shape_of((rows, units), F32), shape_of((rows, units), F32)],
        either_specs(block, width, rows // block) + [pl.BlockSpec(gate.shape, lambda i: (0, 0))] * 2,
        [out, out, out],
        (rows // block,),
        vmem=48,
    )


def hidden_kernel(first_ref, second_ref, one_ref, two_ref, down_ref, gate_ref, up_ref, dboth_ref, out_ref):
    units, cols = one_ref.shape[1], down_ref.shape[1]
    rows = either(first_ref, second_ref)
    pieces = rows.shape[1] // cols
    total = None
    for k in range(pieces):
        term = dot_nt(rows[:, k * cols : (k + 1) * cols], down_ref[k * units : (k + 1) * units])
        total = term if total is None else total + term
    dgate = (total * one_ref[...]).astype(BF)
    dup = (total * two_ref[...]).astype(BF)
    dboth_ref[:, :units] = dgate
    dboth_ref[:, units:] = dup
    for k in range(pieces):
        part = dot(dgate, gate_ref[k * units : (k + 1) * units])
        part = part + dot(dup, up_ref[k * units : (k + 1) * units])
        out_ref[:, k * cols : (k + 1) * cols] = part.astype(BF)


def hidden_back(gb, one, two, down, gate, up, block):
    rows, width = 2 * gb[0].shape[0], gb[0].shape[1]
    units = one.shape[1]
    moving = lambda i: (i, 0)
    fixed = lambda i: (0, 0)
    thin = pl.BlockSpec((block, units), moving)
    full = pl.BlockSpec((block, width), moving)
    return run(
        hidden_kernel,
        [*gb, one, two, down, gate, up],
        [shape_of((rows, 2 * units), BF), shape_of((rows, width), BF)],
        either_specs(block, width, rows // block) + [thin, thin] + [pl.BlockSpec(down.shape, fixed)] * 3,
        [pl.BlockSpec((block, 2 * units), moving), full],
        (rows // block,),
        vmem=56,
    )


def result_rows_kernel(h_ref, down_ref, out_ref):
    units, cols = h_ref.shape[1], down_ref.shape[1]
    for k in range(out_ref.shape[1] // cols):
        part = dot(h_ref[...], down_ref[k * units : (k + 1) * units])
        out_ref[:, k * cols : (k + 1) * cols] = part.astype(BF)


def result_rows(hidden, down, width, block):
    rows, units = hidden.shape
    moving = lambda i: (i, 0)
    return run(
        result_rows_kernel,
        [hidden, down],
        [shape_of((rows, width), BF)],
        [pl.BlockSpec((block, units), moving), pl.BlockSpec(down.shape, lambda i: (0, 0))],
        [pl.BlockSpec((block, width), moving)],
        (rows // block,),
    )[0]


def weight_grad_kernel(left_ref, first_ref, second_ref, out_ref):
    half = first_ref.shape[0]
    total = dot_tn(left_ref[:half], first_ref[...]) + dot_tn(left_ref[half:], second_ref[...])
    out_ref[...] = total.astype(BF)


def weight_grad(left, right, pieces):
    rows, units = left.shape
    cols = right[0].shape[1] // pieces
    return run(
        weight_grad_kernel,
        [left, *right],
        [shape_of((pieces * units, cols), BF)],
        [pl.BlockSpec((rows, units), lambda i: (0, 0)), *[pl.BlockSpec((rows // 2, cols), lambda i: (0, i))] * 2],
        [pl.BlockSpec((units, cols), lambda i: (i, 0))],
        (pieces,),
        vmem=48,
    )[0]


def gather_rows(value, bits, what):
    acc = value
    for bit in bits:
        acc = jnp.concatenate([acc, bit.swap(acc, what)], 0)
    return acc


def reduce_rows(acc, bits, what):
    steps = []
    for bit in reversed(bits):
        half = acc.shape[0] // 2
        steps.append((acc[:half], bit.swap(acc[half:], what)))
        acc = add_low(*steps[-1])
    return steps


def gather_team(value, bit_x, near, bit_core, what, marks):
    half = value.shape[0] // 2
    by_x, by_near = bit_x.swap(value, what), near.swap(value, what)
    diagonal = [bit_x.swap(by_near[:half], what), near.swap(by_x[half:], what)]
    four = after(jnp.concatenate([value, by_x, by_near] + diagonal, 0), *marks)
    return four, bit_core.swap(four, what)


def add_low(a, b):
    return (a.astype(F32) + b.astype(F32)).astype(BF)


def reduce_four(acc, got, bit_x, near, what):
    half = acc.shape[0]
    acc = add_low(acc, got)
    rows = half // 4
    own, by_x, by_near = acc[:rows], acc[rows : 2 * rows], acc[2 * rows : 3 * rows]
    first, second = acc[3 * rows : 3 * rows + rows // 2], acc[3 * rows + rows // 2 :]
    got_near = bit_x.swap(first, what)
    got_x = near.swap(second, what)
    by_near = jnp.concatenate([add_low(by_near[: rows // 2], got_near), by_near[rows // 2 :]], 0)
    by_x = jnp.concatenate([by_x[: rows // 2], add_low(by_x[rows // 2 :], got_x)], 0)
    return (add_low(own, bit_x.swap(by_x, what)), near.swap(by_near, what)), by_x


def absolute(blocks, index, bits):
    def one(j):
        other = index ^ j
        slot = sum(((other >> b.bit) & 1) << i for i, b in enumerate(bits))
        return lax.dynamic_index_in_dim(blocks, slot, 0, False)

    return jnp.stack([one(j) for j in range(blocks.shape[0])])


def relative(blocks, index, bits):
    def one(r):
        code = sum(((r >> i) & 1) << b.bit for i, b in enumerate(bits))
        return lax.dynamic_index_in_dim(blocks, index ^ code, 0, False)

    return jnp.stack([one(r) for r in range(blocks.shape[0])])


def shards(
    dp,
    ctx,
    tokens,
    cotangent,
    attn_gain,
    query_weight,
    key_weight,
    value_weight,
    output_weight,
    mlp_gain,
    gate_weight,
    up_weight,
    down_weight,
):
    seqs, seq_dev, width = tokens.shape
    rows = seqs * seq_dev
    depth = query_weight.shape[0]
    c_index = lax.axis_index("ctx")

    bit_x, bit_core = Bit("dp", 1, dp), Bit("dp", 0, dp)
    ctx_bits = [Bit("ctx", b, ctx) for b in reversed(range(ctx.bit_length() - 1))]
    near = ctx_bits[-1]
    far = [b for b in ctx_bits if b is not near]
    dp_bits = [bit_x, bit_core]
    names = dp_bits + ctx_bits
    attn_order = Order(names, list(reversed(ctx_bits)) + dp_bits, ctx_bits, depth)
    mlp_order = Order(names, far + dp_bits + [near], [], depth)
    x = tokens.reshape(rows, width)
    cot = cotangent.reshape(rows, width)
    gain_one = attn_gain.astype(F32)[:, None]
    gain_two = mlp_gain.astype(F32)[:, None]

    team_groups = []
    for c in range(ctx):
        if not (c >> near.bit) & 1:
            team_groups.append([d * ctx + (c | (n << near.bit)) for d in range(dp) for n in range(2)])
    team = 2 * dp

    def mlp_trade(parts):
        return lax.all_to_all(
            parts, ("dp", "ctx"), 0, 0, axis_index_groups=team_groups, tiled=True
        )

    def mlp_slices(weights, gain, *marks):
        kinds = len(weights)
        parts = after(mlp_trade(pack(weights, gain, team)), *marks)
        shape = (parts.shape[2], team * depth)
        return run(functools.partial(columns_kernel, kinds), [parts], [shape_of(shape, BF)] * kinds)

    def mlp_rows(sums):
        kinds = sum(t.shape[0] for t in sums) // units
        shape = (team, kinds * depth, units)
        return mlp_trade(run(functools.partial(rows_kernel, depth), sums, [shape_of(shape, BF)])[0])

    far_groups = []
    for n in range(2):
        far_groups.append([c for c in range(ctx) if (c >> near.bit) & 1 == n])
    pieces = ctx // 2

    def far_gather(own):
        return lax.all_gather(own, "ctx", axis=0, tiled=True, axis_index_groups=far_groups)

    def far_reduce(terms):
        return lax.psum_scatter(
            terms, "ctx", scatter_dimension=0, tiled=True, axis_index_groups=far_groups
        )

    qkv_cols = HEAD_COLS + 2 * HEAD_DIM
    me = lax.axis_index("dp").astype(jnp.int32).reshape(1)
    slices = run(
        functools.partial(pack_qkv_kernel, dp),
        [me, query_weight, key_weight, value_weight],
        [shape_of((dp, depth, qkv_cols), BF)],
        [SMEM] + [pl.BlockSpec(memory_space=pltpu.VMEM)] * 3,
    )[0]
    out_acc = [output_weight]
    for bit in ctx_bits[:-1]:
        out_acc.append(jnp.concatenate([out_acc[-1], bit.swap(out_acc[-1], "out")], 0))
    slices = [slices[0]] + [swap_difference(slices[r], "dp", dp, r, "slice") for r in range(1, dp)]
    own = run(
        functools.partial(place_kernel, dp),
        [me, after(slices[0], out_acc[1])] + slices[1:],
        [shape_of((dp, depth, qkv_cols), BF)],
        [SMEM] + [pl.BlockSpec(memory_space=pltpu.VMEM)] * dp,
    )[0].reshape(dp * depth, qkv_cols)
    halves = [own]
    for i, bit in enumerate(ctx_bits[:-1]):
        sent = halves[-1] if i == 0 else after(halves[-1], out_acc[i + 1])
        halves.append(jnp.concatenate([sent, bit.swap(sent, "qkv")], 0))
    qkv = [halves[-1], ctx_bits[-1].swap(halves[-1], "qkv")]
    out_rel = after(out_acc[-1], qkv[1])
    out_rel = jnp.concatenate([out_rel, ctx_bits[-1].swap(out_rel, "out")], 0)
    out_full = absolute(out_rel.reshape(ctx, depth, width), c_index, ctx_bits)
    out_full = out_full.reshape(ctx * depth, width)

    gate_own, up_own = mlp_slices([after(gate_weight, own), up_weight], gain_two, halves[-1])
    gain_all = jnp.broadcast_to(after(attn_gain, gate_own)[None], (dp * ctx, depth))
    gain_all = lax.all_to_all(gain_all, ("dp", "ctx"), 0, 0, tiled=True)
    gain_all = gain_all.reshape(1, width).astype(F32)
    a1_half = gather_rows(norm_to(attn_order, x, gain_all), dp_bits[:1], "a1")
    a1 = gather_rows(a1_half, dp_bits[1:], "a1")
    gate = far_gather(gate_own)
    (down_own,) = mlp_slices([after(down_weight.T, gain_all)], None)
    units = down_own.shape[0]

    places = jnp.arange(seq_dev, dtype=jnp.int32)
    half_dim = HEAD_DIM // 2
    freqs = rope_base ** (-(jnp.arange(half_dim, dtype=F32) * 2.0) / HEAD_DIM)
    angles = (c_index * seq_dev + places).astype(F32)[:, None] * freqs[None, :]
    cosine, sine = jnp.cos(angles), jnp.sin(angles)
    cosine = jnp.concatenate([cosine, cosine] * (GROUPS + 1) + [jnp.ones((seq_dev, HEAD_DIM), F32)], -1)
    sine = jnp.concatenate([-sine, sine] * (GROUPS + 1) + [jnp.zeros((seq_dev, HEAD_DIM), F32)], -1)
    rel = jnp.arange(ctx, dtype=jnp.int32)
    others = sum(((rel >> i) & 1) << b.bit for i, b in enumerate(ctx_bits)) ^ c_index
    key_places = (((others - c_index) * seq_dev)[:, None] + places[None, :]).reshape(1, -1)

    queries, kv_own = project(a1, cosine, sine, qkv)
    all_seqs = dp * seqs
    kv = kv_own
    for i, bit in enumerate(ctx_bits):
        if i == 1:
            kv = after(kv, down_own)
        if i == len(ctx_bits) - 2:
            up = far_gather(after(up_own, kv))
            down = far_gather(after(down_own, kv))
        kv = jnp.concatenate([kv, bit.swap(kv, "kv")], 0)
    kv = kv.reshape(ctx, all_seqs, seq_dev, 2 * HEAD_DIM)
    heads = attend(queries, kv, key_places, seq_dev)
    branch = dot(heads, out_full).astype(BF)
    branch = reduce_rows(branch, dp_bits, "branch")[-1]
    middle, a2 = middle_to(mlp_order, x, *branch)

    gb = gather_team(order_to(mlp_order, after(cot, middle)), bit_x, near, bit_core, "gb", [])
    a2 = gather_team(a2, bit_x, near, bit_core, "a2", [])
    block = min(256, a2[0].shape[0])
    hidden, one, two = gate_up(a2, gate, up, units, block)
    down_terms = weight_grad(hidden, gb, pieces)
    down_back = far_reduce(down_terms)
    dboth, da2 = hidden_back((after(gb[0], down_terms), gb[1]), one, two, down, gate, up, block)
    half = da2.shape[0] // 2
    da2_got = bit_core.swap(da2[half:], "da2")
    da2_two, da2_mark = reduce_four(da2[:half], da2_got, bit_x, near, "da2")
    down_out = result_rows(after(hidden, da2), down, width, block)
    result_got = bit_core.swap(after(down_out[half:], da2_mark), "result")
    both_terms = weight_grad(dboth, (after(a2[0], da2_mark), a2[1]), pieces)
    both_back = far_reduce(both_terms)
    grad_middle, db = norm_back(mlp_order, middle, after(cot, both_terms, result_got), *da2_two, low=True)
    grad_branch = gather_rows(db, dp_bits, "db")
    result_two, result_mark = reduce_four(
        down_out[:half], after(result_got, db), bit_x, near, "result"
    )
    result = result_of(mlp_order, middle, *result_two)

    grad_heads = dot_nt(grad_branch, out_full)
    dq, dkv = attend_back(
        queries, kv, after(key_places, *result_two), grad_heads, cosine, sine, seq_dev
    )

    class Sum:
        def __init__(self, terms, what):
            self.terms, self.what, self.bits = terms, what, list(reversed(ctx_bits))

        def step(self, *marks):
            half = self.terms.shape[0] // 2
            sent = after(self.terms[half:], *marks) if marks else self.terms[half:]
            self.pair = self.terms[:half], self.bits.pop(0).swap(sent, self.what)
            self.terms = add_low(*self.pair)
            return self.pair[1]

        def finish(self, *marks):
            while self.bits:
                self.step(*marks)
            return self.pair

    dkv_sum = Sum(dkv.reshape(-1, 2 * HEAD_DIM), "dkv")
    dkv_first = dkv_sum.step()
    dq_sum = Sum(dot_tn(a1, after(dq, dkv_first)).astype(BF), "dq_w")
    dq_first = dq_sum.step()
    dkv_sum.step(down_back)
    dkv_two = dkv_sum.finish()
    dkv_low = run(
        functools.partial(turn_back_kernel, all_seqs),
        [after(dkv_two[0], dq_first), dkv_two[1]] + [cosine, sine],
        [shape_of((dp * rows, 2 * HEAD_DIM), BF)],
    )[0]
    kv_sum = Sum(dot_tn(a1, dkv_low).astype(BF), "dkv_w")
    kv_first = kv_sum.step()
    da1 = wide(dot_nt, jnp.concatenate([dq, dkv_low], -1), qkv, width, min(256, dp * rows))
    da1_steps = reduce_rows(da1, dp_bits, "da1")
    da1_two = da1_steps[-1]
    (grad_tokens,) = norm_back(attn_order, x, grad_middle, *da1_two, gain_all)
    dq_second = dq_sum.step()
    kv_second = kv_sum.step(dq_second, da1_steps[0][1])
    out_total = dot_tn(heads, grad_branch).astype(BF).reshape(ctx, depth, width)
    out_total = relative(after(out_total, kv_first), c_index, ctx_bits).reshape(ctx * depth, width)
    out_sum = Sum(out_total, "dout_w")
    out_first = out_sum.step()
    all_back = mlp_rows([after(both_back, kv_first), down_back])
    dq_two = dq_sum.finish()
    kv_two = kv_sum.finish(dq_two[1], *da1_two)
    out_second = out_sum.step(kv_second)
    out_two = out_sum.finish()
    output_grad = out_two[0].astype(F32) + out_two[1].astype(F32)
    qkv_total = jnp.concatenate([add_low(*dq_two), add_low(*kv_two)], -1).reshape(dp, depth, qkv_cols)
    def place(blocks):
        return run(
            functools.partial(place_kernel, dp),
            [me] + blocks,
            [shape_of((dp, depth, qkv_cols), BF)],
            [SMEM] + [pl.BlockSpec(memory_space=pltpu.VMEM)] * dp,
        )[0]

    sent = place([qkv_total[r] for r in range(dp)])
    qkv_back = place(
        [sent[0]] + [swap_difference(sent[r], "dp", dp, r, "back") for r in range(1, dp)]
    )

    wide_shape = shape_of(gate_weight.shape, F32)
    gate_grad, up_grad, down_grad, mlp_sum = run(
        unpack_kernel,
        [all_back, gate_weight, up_weight, gain_two],
        [wide_shape, wide_shape, wide_shape, shape_of((depth, 1), F32)],
    )
    down_grad = down_grad.T
    query_grad, key_grad, value_grad, attn_sum = run(
        functools.partial(unpack_qkv_kernel, dp),
        [query_weight, key_weight, value_weight, gain_one, qkv_back],
        [shape_of(w.shape, F32) for w in (query_weight, key_weight, value_weight, gain_one)],
    )
    return (
        result.reshape(seqs, seq_dev, width),
        grad_tokens.reshape(seqs, seq_dev, width),
        attn_sum[:, 0],
        query_grad,
        key_grad,
        value_grad,
        output_grad,
        mlp_sum[:, 0],
        gate_grad,
        up_grad,
        down_grad,
    )


def solution(mesh):
    dp, ctx = mesh.shape["dp"], mesh.shape["ctx"]

    def local(*args):
        return shards(dp, ctx, *args)

    weight = P(("dp", "ctx"), None)
    flat = P(("dp", "ctx"))
    acts = P("dp", "ctx", None)
    down = P(None, ("dp", "ctx"))
    return jax.shard_map(
        local,
        mesh=mesh,
        in_specs=(acts, acts, flat, weight, weight, weight, weight, flat, weight, weight, down),
        out_specs=(acts, acts, flat, weight, weight, weight, weight, flat, weight, weight, down),
        check_vma=False,
    )
```

```python
import functools
import math

import jax
import jax.numpy as jnp
from jax import lax
from jax.experimental import pallas as pl
from jax.experimental.pallas import tpu as pltpu
from jax.sharding import PartitionSpec as P

HEADS = 32
KV_HEADS = 4
HEAD_DIM = 64
GROUPS = HEADS // KV_HEADS
HEAD_COLS = GROUPS * HEAD_DIM
FACTOR = 1.0 / math.sqrt(HEAD_DIM)

norm_eps = 1e-05
rope_base = 10000.0

BF = jnp.bfloat16
F32 = jnp.float32
MIB = 1 << 20


def dot(left, right):
    return jnp.dot(left, right, preferred_element_type=F32)


def dot_nt(left, right):
    return lax.dot_general(left, right, (((1,), (1,)), ((), ())), preferred_element_type=F32)


def dot_tn(left, right):
    return lax.dot_general(left, right, (((0,), (0,)), ((), ())), preferred_element_type=F32)


def shape_of(shape, kind):
    return jax.ShapeDtypeStruct(shape, kind)


def run(kernel, ins, outs, specs=None, out_specs=None, grid=None, vmem=32, scratch=(), flops=0):
    whole = pl.BlockSpec(memory_space=pltpu.VMEM)
    moved = sum(math.prod(a.shape) * a.dtype.itemsize for a in list(ins) + list(outs))
    extra = {} if grid is None else {"grid": grid}
    name = kernel.func.__name__ if isinstance(kernel, functools.partial) else kernel.__name__
    return pl.pallas_call(
        kernel,
        name=name,
        out_shape=list(outs),
        in_specs=specs or [whole] * len(ins),
        out_specs=out_specs or [whole] * len(outs),
        scratch_shapes=list(scratch),
        compiler_params=pltpu.CompilerParams(vmem_limit_bytes=vmem * MIB),
        cost_estimate=pl.CostEstimate(flops=0, bytes_accessed=0, transcendentals=0),
        **extra,
    )(*ins)


SMEM = pl.BlockSpec(memory_space=pltpu.SMEM)


class Bit:
    def __init__(self, axis, bit, size):
        self.axis, self.bit = axis, bit
        self.pairs = [(i, i ^ (1 << bit)) for i in range(size)]

    def mine(self):
        return (lax.axis_index(self.axis) >> self.bit) & 1

    def swap(self, value, what):
        with jax.named_scope(f"{what}_{self.axis}{self.bit}"):
            return lax.ppermute(value, self.axis, self.pairs)


def swap_difference(value, axis, size, difference, what):
    with jax.named_scope(f"{what}_{axis}"):
        return lax.ppermute(value, axis, [(i, i ^ difference) for i in range(size)])


def after(value, *others):
    return lax.optimization_barrier((value,) + others)[0]


class Order:
    def __init__(self, names, rel, gathered, depth):
        self.names, self.rel, self.gathered, self.depth = names, rel, gathered, depth
        self.whole_tiles = rel[-1] is names[-1] and not gathered
        self.fast = depth == 64 and len(names) == 5 and (
            self.whole_tiles or (rel[-1] is not names[-1] and rel[-1] not in gathered)
        )
        self.mine = jnp.stack(
            [b.mine() if b in gathered else jnp.zeros((), jnp.int32) for b in names]
        ).astype(jnp.int32)

    def to_tiles(self, read, write, mine):
        lanes = lax.broadcasted_iota(jnp.int32, (1, 128), 1)
        head = self.rel[:-1]
        last = self.rel[-1]
        for q in range(16):
            value = {b: (q >> (3 - i)) & 1 for i, b in enumerate(head)}
            if self.whole_tiles:
                write(q, read(sum(value[b] << (3 - i) for i, b in enumerate(self.names[:-1]))))
                continue

            def source(low):
                index = 0
                for i, b in enumerate(self.names[:-1]):
                    v = low if b is last else value[b]
                    if b in self.gathered:
                        v = v ^ mine[i]
                    index = index * 2 + v
                return read(index)

            a, b = source(0), source(1)
            side = value[self.names[-1]]
            low = lambda: jnp.where(lanes < 64, a, pltpu.roll(b, 64, 1))
            high = lambda: jnp.where(lanes < 64, pltpu.roll(a, 64, 1), b)
            if self.names[-1] in self.gathered:
                write(q, jnp.where((side ^ mine[4]) == 0, low(), high()))
            else:
                write(q, low() if side == 0 else high())

    def from_tiles(self, read, write, mine):
        lanes = lax.broadcasted_iota(jnp.int32, (1, 128), 1)
        for t in range(16):
            value = {b: (t >> (3 - i)) & 1 for i, b in enumerate(self.names[:-1])}
            if self.whole_tiles:
                write(t, read(sum(value[b] << (3 - i) for i, b in enumerate(self.rel[:-1]))))
                continue

            def source(y):
                index = 0
                for b in self.rel[:-1]:
                    v = y if b is self.names[-1] else value[b]
                    if b in self.gathered:
                        v = v ^ mine[self.names.index(b)]
                    index = index * 2 + v
                return read(index)

            low, high = source(0), source(1)
            if value[self.rel[-1]] == 0:
                write(t, jnp.where(lanes < 64, low, pltpu.roll(high, 64, 1)))
            else:
                write(t, jnp.where(lanes < 64, pltpu.roll(low, 64, 1), high))

    def to_rel(self, array):
        count, width = array.shape
        out = array.reshape((count,) + (2,) * len(self.names) + (self.depth,))
        for b in self.gathered:
            k = self.names.index(b) + 1
            out = jnp.where(b.mine() == 1, jnp.flip(out, k), out)
        axes = [self.names.index(b) + 1 for b in self.rel]
        return out.transpose([0] + axes + [len(self.names) + 1]).reshape(count, width)

    def from_rel(self, array):
        count, width = array.shape
        out = array.reshape((count,) + (2,) * len(self.names) + (self.depth,))
        axes = [self.rel.index(b) + 1 for b in self.names]
        out = out.transpose([0] + axes + [len(self.names) + 1])
        for b in self.gathered:
            k = self.names.index(b) + 1
            out = jnp.where(b.mine() == 1, jnp.flip(out, k), out)
        return out.reshape(count, width)


def tile(index):
    start = index * 128
    return pl.ds(start if isinstance(start, int) else pl.multiple_of(start, 128), 128)


def row_specs(count, rows, width, steps):
    return [pl.BlockSpec((rows // steps, width), lambda i: (i, 0))] * count


def inverse_of(x):
    return lax.rsqrt(jnp.mean(x * x, -1, keepdims=True) + norm_eps)


def norm_kernel(order, mine_ref, x_ref, gain_ref, out_ref):
    mine = [mine_ref[i] for i in range(5)]
    inverse = inverse_of(x_ref[...].astype(F32))

    def write(q, value):
        out_ref[:, tile(q)] = value.astype(BF)

    def read(i):
        return x_ref[:, tile(i)].astype(F32) * inverse * gain_ref[:, tile(i)]

    order.to_tiles(read, write, mine)


def norm_to(order, x, gain):
    if not order.fast:
        x = x.astype(F32)
        return order.to_rel((x * inverse_of(x) * gain).astype(BF))
    rows, width = x.shape
    specs = row_specs(2, rows, width, 2)
    return run(
        functools.partial(norm_kernel, order),
        [order.mine, x, gain],
        [shape_of((rows, width), BF)],
        [SMEM, specs[0], pl.BlockSpec((1, width), lambda i: (0, 0))],
        [specs[1]],
        (2,),
    )[0]


def order_kernel(order, mine_ref, x_ref, out_ref):
    mine = [mine_ref[i] for i in range(5)]

    def write(q, value):
        out_ref[:, tile(q)] = value.astype(out_ref.dtype)

    order.to_tiles(lambda i: x_ref[:, tile(i)].astype(F32), write, mine)


def order_to(order, x):
    if not order.fast:
        return order.to_rel(x)
    rows, width = x.shape
    specs = row_specs(2, rows, width, 2)
    return run(
        functools.partial(order_kernel, order),
        [order.mine, x],
        [shape_of((rows, width), x.dtype)],
        [SMEM, specs[0]],
        [specs[1]],
        (2,),
    )[0]


def middle_kernel(order, mine_ref, x_ref, a_ref, b_ref, mid_ref, out_ref):
    mine = [mine_ref[i] for i in range(5)]
    mid = x_ref[...].astype(F32) + a_ref[...].astype(F32) + b_ref[...].astype(F32)
    mid_ref[...] = mid
    inverse = inverse_of(mid)

    def write(q, value):
        out_ref[:, tile(q)] = value.astype(BF)

    order.to_tiles(lambda i: mid_ref[:, tile(i)] * inverse, write, mine)


def middle_to(order, x, a, b):
    rows, width = x.shape
    if not order.fast:
        mid = x.astype(F32) + a.astype(F32) + b.astype(F32)
        return mid, order.to_rel((mid * inverse_of(mid)).astype(BF))
    specs = row_specs(5, rows, width, 2)
    return run(
        functools.partial(middle_kernel, order),
        [order.mine, x, a, b],
        [shape_of((rows, width), F32), shape_of((rows, width), BF)],
        [SMEM] + specs[:3],
        specs[:2],
        (2,),
    )


def back_kernel(order, scaled, mine_ref, x_ref, g_ref, a_ref, b_ref, *outs):
    mine = [mine_ref[i] for i in range(5)]
    scratch = outs[-1]
    if scaled:
        gain_ref, outs = outs[0], outs[1:]
    inverse = inverse_of(x_ref[...].astype(F32))

    def write(t, value):
        scratch[:, tile(t)] = value * gain_ref[:, tile(t)] if scaled else value

    def read(i):
        return a_ref[:, tile(i)].astype(F32) + b_ref[:, tile(i)].astype(F32)

    order.from_tiles(read, write, mine)
    normed = x_ref[...].astype(F32) * inverse
    scaled = scratch[...]
    shared = jnp.mean(scaled * normed, -1, keepdims=True)
    total = g_ref[...].astype(F32) + inverse * (scaled - normed * shared)
    outs[0][...] = total
    if len(outs) == 3:
        outs[1][...] = total.astype(BF)


def norm_back(order, x, g, a, b, gain=None, low=False):
    rows, width = x.shape
    scaled = gain is not None
    if not order.fast:
        x = x.astype(F32)
        inverse = inverse_of(x)
        normed = x * inverse
        grad = a.astype(F32) + b.astype(F32)
        grad = order.from_rel(grad)
        grad = grad * gain if scaled else grad
        shared = jnp.mean(grad * normed, -1, keepdims=True)
        total = g.astype(F32) + inverse * (grad - normed * shared)
        return (total, total.astype(BF)) if low else (total,)
    specs = row_specs(6, rows, width, 2)
    outs = [shape_of((rows, width), F32)] + ([shape_of((rows, width), BF)] if low else [])
    return run(
        functools.partial(back_kernel, order, scaled),
        [order.mine, x, g, a, b] + ([gain] if scaled else []),
        outs,
        [SMEM] + specs[:4] + [pl.BlockSpec((1, width), lambda i: (0, 0))] * scaled,
        specs[: len(outs)],
        (2,),
        scratch=[pltpu.VMEM((rows // 2, width), F32)],
    )


def result_kernel(order, mine_ref, mid_ref, a_ref, b_ref, out_ref):
    mine = [mine_ref[i] for i in range(5)]

    def write(t, value):
        out_ref[:, tile(t)] = (mid_ref[:, tile(t)] + value).astype(BF)

    order.from_tiles(
        lambda i: a_ref[:, tile(i)].astype(F32) + b_ref[:, tile(i)].astype(F32), write, mine
    )


def result_of(order, mid, a, b):
    rows, width = mid.shape
    if not order.fast:
        return (mid + order.from_rel(a.astype(F32) + b.astype(F32))).astype(BF)
    specs = row_specs(4, rows, width, 2)
    return run(
        functools.partial(result_kernel, order),
        [order.mine, mid, a, b],
        [shape_of((rows, width), BF)],
        [SMEM] + specs[:3],
        specs[:1],
        (2,),
    )[0]


def pack_kernel(count, kinds, *refs):
    out_ref = refs[-1]
    cols = out_ref.shape[-1]
    depth = refs[0].shape[0]
    for m in range(kinds):
        value = refs[m][...].astype(F32)
        if len(refs) > kinds + 1:
            value = value * refs[kinds][...]
        for t in range(count):
            out_ref[t, m * depth : (m + 1) * depth] = value[:, t * cols : (t + 1) * cols].astype(BF)


def pack(weights, gain, count):
    depth, width = weights[0].shape
    return run(
        functools.partial(pack_kernel, count, len(weights)),
        weights + ([] if gain is None else [gain]),
        [shape_of((count, len(weights) * depth, width // count), BF)],
    )[0]


def unpack_kernel(p_ref, gate_ref, up_ref, gain_ref, gate_out, up_out, down_out, sum_ref):
    count, depth, cols = p_ref.shape
    depth = depth // 3
    total = jnp.zeros((depth, 1), F32)
    for t in range(count):
        lanes = slice(t * cols, (t + 1) * cols)
        for m, (w_ref, out_ref) in enumerate([(gate_ref, gate_out), (up_ref, up_out)]):
            part = p_ref[t, m * depth : (m + 1) * depth].astype(F32)
            total = total + jnp.sum(part * w_ref[:, lanes].astype(F32), -1, keepdims=True)
            out_ref[:, lanes] = part * gain_ref[...]
        down_out[:, lanes] = p_ref[t, 2 * depth :].astype(F32)
    sum_ref[...] = total


def pack_qkv_kernel(count, me_ref, q_ref, k_ref, v_ref, out_ref):
    for t in range(count):
        slot = me_ref[0] ^ t
        out_ref[slot, :, :HEAD_COLS] = q_ref[:, t * HEAD_COLS : (t + 1) * HEAD_COLS]
        lanes = slice(t * HEAD_DIM, (t + 1) * HEAD_DIM)
        both = jnp.concatenate([k_ref[:, lanes].astype(F32), v_ref[:, lanes].astype(F32)], -1)
        out_ref[slot, :, HEAD_COLS:] = both.astype(BF)


def place_kernel(count, me_ref, *refs):
    for r in range(count):
        refs[-1][me_ref[0] ^ r] = refs[r][...]


def columns_kernel(kinds, in_ref, *outs):
    count, depth, units = in_ref.shape
    depth = depth // kinds
    step = max(1, 128 // depth)
    for m in range(kinds):
        for t in range(0, count, step):
            rows = [in_ref[t + i, m * depth : (m + 1) * depth] for i in range(step)]
            both = jnp.concatenate(rows, 0).astype(F32)
            outs[m][:, t * depth : (t + step) * depth] = both.T.astype(BF)


def rows_kernel(depth, *refs):
    out_ref = refs[-1]
    count, _, units = out_ref.shape
    step = max(1, 128 // depth)
    m = 0
    for ref in refs[:-1]:
        for first in range(0, ref.shape[0], units):
            for t in range(0, count, step):
                lanes = slice(t * depth, (t + step) * depth)
                both = ref[first : first + units, lanes].astype(F32).T
                for i in range(step):
                    rows = both[i * depth : (i + 1) * depth]
                    out_ref[t + i, m * depth : (m + 1) * depth] = rows.astype(BF)
            m += 1


def unpack_qkv_kernel(count, q_ref, k_ref, v_ref, g_ref, p_ref, qo_ref, ko_ref, vo_ref, sum_ref):
    gain = g_ref[...]
    total = jnp.zeros_like(gain)
    for t in range(count):
        part = p_ref[t].astype(F32)
        lanes = slice(t * HEAD_COLS, (t + 1) * HEAD_COLS)
        thin = slice(t * HEAD_DIM, (t + 1) * HEAD_DIM)
        gq = part[:, :HEAD_COLS]
        gk = part[:, HEAD_COLS : HEAD_COLS + HEAD_DIM]
        gv = part[:, HEAD_COLS + HEAD_DIM :]
        total = total + jnp.sum(gq * q_ref[:, lanes].astype(F32), -1, keepdims=True)
        total = total + jnp.sum(gk * k_ref[:, thin].astype(F32), -1, keepdims=True)
        total = total + jnp.sum(gv * v_ref[:, thin].astype(F32), -1, keepdims=True)
        qo_ref[:, lanes] = gq
        ko_ref[:, thin] = gk
        vo_ref[:, thin] = gv
    sum_ref[...] = total / gain


def swap_halves(values):
    width = values.shape[-1]
    lanes = lax.broadcasted_iota(jnp.int32, (1, width), 1)
    return jnp.where(
        lanes % HEAD_DIM < HEAD_DIM // 2,
        pltpu.roll(values, width - HEAD_DIM // 2, 1),
        pltpu.roll(values, HEAD_DIM // 2, 1),
    )


def project_kernel(repeat, count, *refs):
    a_ref, cos_ref, sin_ref = refs[:3]
    w_refs, q_ref, kv_ref = refs[3 : 3 + count], refs[-2], refs[-1]
    piece = w_refs[0].shape[0]
    raw = None
    for k in range(count):
        term = dot(a_ref[:, k * piece : (k + 1) * piece], w_refs[k][...])
        raw = term if raw is None else raw + term
    cosine = jnp.concatenate([cos_ref[...]] * repeat, 0)
    sine = jnp.concatenate([sin_ref[...]] * repeat, 0)
    out = (raw * cosine + swap_halves(raw) * sine).astype(BF)
    q_ref[...] = out[:, :HEAD_COLS]
    kv_ref[...] = out[:, HEAD_COLS:]


def project(a1, cosine, sine, parts):
    rows, width = a1.shape
    seq_dev, cols = cosine.shape
    block = min(2 * seq_dev, rows)
    fixed = lambda i: (0, 0)
    moving = lambda i: (i, 0)
    return run(
        functools.partial(project_kernel, block // seq_dev, len(parts)),
        [a1, cosine, sine] + parts,
        [shape_of((rows, HEAD_COLS), BF), shape_of((rows, 2 * HEAD_DIM), BF)],
        [pl.BlockSpec((block, width), moving)]
        + [pl.BlockSpec((seq_dev, cols), fixed)] * 2
        + [pl.BlockSpec(p.shape, fixed) for p in parts],
        [pl.BlockSpec((block, HEAD_COLS), moving), pl.BlockSpec((block, 2 * HEAD_DIM), moving)],
        (rows // block,),
        flops=2 * rows * width * cols,
    )


def stack_heads(values):
    return jnp.concatenate(
        [values[:, j * HEAD_DIM : (j + 1) * HEAD_DIM] for j in range(GROUPS)], 0
    )


def soft_weights(queries, keys, key_ref, seq_dev):
    scores = dot_nt(queries, keys) * FACTOR
    place = lax.broadcasted_iota(jnp.int32, (queries.shape[0], 1), 0) % seq_dev
    return jnp.where(place >= key_ref[...], jnp.exp(scores), 0.0)


def attend_kernel(q_ref, kv_ref, key_ref, o_ref):
    seq_dev = q_ref.shape[0]
    both = kv_ref[...].reshape(-1, 2 * HEAD_DIM)
    keys, values = both[:, :HEAD_DIM], both[:, HEAD_DIM:]
    weights = soft_weights(stack_heads(q_ref[...]), keys, key_ref, seq_dev)
    totals = jnp.sum(weights, -1, keepdims=True)
    attended = dot(weights.astype(BF), values) / totals
    for j in range(GROUPS):
        rows = attended[j * seq_dev : (j + 1) * seq_dev]
        o_ref[:, j * HEAD_DIM : (j + 1) * HEAD_DIM] = rows.astype(BF)


def attend(queries, kv, key_places, seq_dev):
    rows = queries.shape[0]
    count, seqs = kv.shape[:2]
    return run(
        attend_kernel,
        [queries, kv, key_places],
        [shape_of((rows, HEAD_COLS), BF)],
        [
            pl.BlockSpec((seq_dev, HEAD_COLS), lambda s: (s, 0)),
            pl.BlockSpec((count, 1, seq_dev, 2 * HEAD_DIM), lambda s: (0, s, 0, 0)),
            pl.BlockSpec((1, count * seq_dev), lambda s: (0, 0)),
        ],
        [pl.BlockSpec((seq_dev, HEAD_COLS), lambda s: (s, 0))],
        (seqs,),
        flops=4 * rows * GROUPS * HEAD_DIM * count * seq_dev,
    )[0]


def attend_back_kernel(q_ref, kv_ref, key_ref, do_ref, cos_ref, sin_ref, dq_ref, dkv_ref, mid_ref):
    seq_dev = q_ref.shape[0]
    both = kv_ref[...].reshape(-1, 2 * HEAD_DIM)
    keys, values = both[:, :HEAD_DIM], both[:, HEAD_DIM:]
    queries = stack_heads(q_ref[...])
    weights = soft_weights(queries, keys, key_ref, seq_dev)
    totals = jnp.sum(weights, -1, keepdims=True)
    low = weights.astype(BF)
    attended = dot(low, values) / totals
    grads = stack_heads(do_ref[...])
    deltas = jnp.sum(grads * attended, -1, keepdims=True) / totals
    mixed = (grads / totals).astype(BF)
    scores = (weights * (dot_nt(mixed, values) - deltas)).astype(BF)
    turned = dot(scores, keys) * FACTOR
    for j in range(GROUPS):
        mid_ref[:, j * HEAD_DIM : (j + 1) * HEAD_DIM] = turned[j * seq_dev : (j + 1) * seq_dev]
    whole = mid_ref[...]
    cosine, sine = cos_ref[:, :HEAD_COLS], sin_ref[:, :HEAD_COLS]
    dq_ref[...] = (whole * cosine - swap_halves(whole) * sine).astype(BF)
    grad_keys = dot_tn(scores, queries) * FACTOR
    grad_values = dot_tn(low, mixed)
    joined = jnp.concatenate([grad_keys, grad_values], -1)
    dkv_ref[...] = joined.astype(BF).reshape(dkv_ref.shape)


def attend_back(queries, kv, key_places, grads, cosine, sine, seq_dev):
    rows = queries.shape[0]
    count, seqs = kv.shape[:2]
    own = pl.BlockSpec((seq_dev, HEAD_COLS), lambda s: (s, 0))
    table = pl.BlockSpec(cosine.shape, lambda s: (0, 0))
    blocks = pl.BlockSpec((count, 1, seq_dev, 2 * HEAD_DIM), lambda s: (0, s, 0, 0))
    return run(
        attend_back_kernel,
        [queries, kv, key_places, grads, cosine, sine],
        [shape_of((rows, HEAD_COLS), BF), shape_of(kv.shape, BF)],
        [own, blocks, pl.BlockSpec((1, count * seq_dev), lambda s: (0, 0)), own, table, table],
        [own, blocks],
        (seqs,),
        scratch=[pltpu.VMEM((seq_dev, HEAD_COLS), F32)],
        flops=14 * rows * GROUPS * HEAD_DIM * count * seq_dev,
    )


def turn_back_kernel(repeat, a_ref, b_ref, cos_ref, sin_ref, out_ref):
    total = a_ref[...].astype(F32) + b_ref[...].astype(F32)
    cosine = jnp.concatenate([cos_ref[:, HEAD_COLS:]] * repeat, 0)
    sine = jnp.concatenate([sin_ref[:, HEAD_COLS:]] * repeat, 0)
    out_ref[...] = (total * cosine - swap_halves(total) * sine).astype(BF)


def wide_kernel(product, left_ref, *refs):
    rights, out_ref = refs[:-1], refs[-1]
    cols = out_ref.shape[1] // len(rights)
    for k, right in enumerate(rights):
        out_ref[:, k * cols : (k + 1) * cols] = product(left_ref[...], right[...]).astype(BF)


def wide(product, left, rights, width, block):
    rows, depth = left.shape
    return run(
        functools.partial(wide_kernel, product),
        [left] + rights,
        [shape_of((rows, width), BF)],
        [pl.BlockSpec((block, depth), lambda i: (i, 0))]
        + [pl.BlockSpec(r.shape, lambda i: (0, 0)) for r in rights],
        [pl.BlockSpec((block, width), lambda i: (i, 0))],
        (rows // block,),
        vmem=48,
        flops=2 * rows * depth * width,
    )[0]


def either(first_ref, second_ref):
    steps = pl.num_programs(0)
    return jnp.where(pl.program_id(0) < steps // 2, first_ref[...], second_ref[...])


def either_specs(block, width, steps):
    return [
        pl.BlockSpec((block, width), lambda i: (jnp.minimum(i, steps // 2 - 1), 0)),
        pl.BlockSpec((block, width), lambda i: (jnp.maximum(i - steps // 2, 0), 0)),
    ]


def gate_kernel(first_ref, second_ref, gate_ref, up_ref, hid_ref, one_ref, two_ref):
    units, cols = hid_ref.shape[1], gate_ref.shape[1]
    rows = either(first_ref, second_ref)
    gate = up = None
    for k in range(rows.shape[1] // cols):
        part = rows[:, k * cols : (k + 1) * cols]
        g = dot_nt(part, gate_ref[k * units : (k + 1) * units])
        u = dot_nt(part, up_ref[k * units : (k + 1) * units])
        gate = g if gate is None else gate + g
        up = u if up is None else up + u
    sigmoid = jax.nn.sigmoid(gate)
    active = gate * sigmoid
    hid_ref[...] = (active * up).astype(BF)
    one_ref[...] = up * sigmoid * (1.0 + gate * (1.0 - sigmoid))
    two_ref[...] = active


def gate_up(a2, gate, up, units, block):
    rows, width = 2 * a2[0].shape[0], a2[0].shape[1]
    moving = lambda i: (i, 0)
    out = pl.BlockSpec((block, units), moving)
    return run(
        gate_kernel,
        [*a2, gate, up],
        [shape_of((rows, units), BF), shape_of((rows, units), F32), shape_of((rows, units), F32)],
        either_specs(block, width, rows // block) + [pl.BlockSpec(gate.shape, lambda i: (0, 0))] * 2,
        [out, out, out],
        (rows // block,),
        vmem=48,
    )


def hidden_kernel(first_ref, second_ref, one_ref, two_ref, down_ref, gate_ref, up_ref, dboth_ref, out_ref):
    units, cols = one_ref.shape[1], down_ref.shape[1]
    rows = either(first_ref, second_ref)
    pieces = rows.shape[1] // cols
    total = None
    for k in range(pieces):
        term = dot_nt(rows[:, k * cols : (k + 1) * cols], down_ref[k * units : (k + 1) * units])
        total = term if total is None else total + term
    dgate = (total * one_ref[...]).astype(BF)
    dup = (total * two_ref[...]).astype(BF)
    dboth_ref[:, :units] = dgate
    dboth_ref[:, units:] = dup
    for k in range(pieces):
        part = dot(dgate, gate_ref[k * units : (k + 1) * units])
        part = part + dot(dup, up_ref[k * units : (k + 1) * units])
        out_ref[:, k * cols : (k + 1) * cols] = part.astype(BF)


def hidden_back(gb, one, two, down, gate, up, block):
    rows, width = 2 * gb[0].shape[0], gb[0].shape[1]
    units = one.shape[1]
    moving = lambda i: (i, 0)
    fixed = lambda i: (0, 0)
    thin = pl.BlockSpec((block, units), moving)
    full = pl.BlockSpec((block, width), moving)
    return run(
        hidden_kernel,
        [*gb, one, two, down, gate, up],
        [shape_of((rows, 2 * units), BF), shape_of((rows, width), BF)],
        either_specs(block, width, rows // block) + [thin, thin] + [pl.BlockSpec(down.shape, fixed)] * 3,
        [pl.BlockSpec((block, 2 * units), moving), full],
        (rows // block,),
        vmem=56,
    )


def result_rows_kernel(h_ref, down_ref, out_ref):
    units, cols = h_ref.shape[1], down_ref.shape[1]
    for k in range(out_ref.shape[1] // cols):
        part = dot(h_ref[...], down_ref[k * units : (k + 1) * units])
        out_ref[:, k * cols : (k + 1) * cols] = part.astype(BF)


def result_rows(hidden, down, width, block):
    rows, units = hidden.shape
    moving = lambda i: (i, 0)
    return run(
        result_rows_kernel,
        [hidden, down],
        [shape_of((rows, width), BF)],
        [pl.BlockSpec((block, units), moving), pl.BlockSpec(down.shape, lambda i: (0, 0))],
        [pl.BlockSpec((block, width), moving)],
        (rows // block,),
    )[0]


def weight_grad_kernel(left_ref, first_ref, second_ref, out_ref):
    half = first_ref.shape[0]
    total = dot_tn(left_ref[:half], first_ref[...]) + dot_tn(left_ref[half:], second_ref[...])
    out_ref[...] = total.astype(BF)


def weight_grad(left, right, pieces):
    rows, units = left.shape
    cols = right[0].shape[1] // pieces
    return run(
        weight_grad_kernel,
        [left, *right],
        [shape_of((pieces * units, cols), BF)],
        [pl.BlockSpec((rows, units), lambda i: (0, 0)), *[pl.BlockSpec((rows // 2, cols), lambda i: (0, i))] * 2],
        [pl.BlockSpec((units, cols), lambda i: (i, 0))],
        (pieces,),
        vmem=48,
    )[0]


def gather_rows(value, bits, what):
    acc = value
    for bit in bits:
        acc = jnp.concatenate([acc, bit.swap(acc, what)], 0)
    return acc


def reduce_rows(acc, bits, what):
    steps = []
    for bit in reversed(bits):
        half = acc.shape[0] // 2
        steps.append((acc[:half], bit.swap(acc[half:], what)))
        acc = add_low(*steps[-1])
    return steps


def gather_team(value, bit_x, near, bit_core, what, marks):
    half = value.shape[0] // 2
    by_x, by_near = bit_x.swap(value, what), near.swap(value, what)
    diagonal = [bit_x.swap(by_near[:half], what), near.swap(by_x[half:], what)]
    four = after(jnp.concatenate([value, by_x, by_near] + diagonal, 0), *marks)
    return four, bit_core.swap(four, what)


def add_low(a, b):
    return (a.astype(F32) + b.astype(F32)).astype(BF)


def reduce_four(acc, got, bit_x, near, what):
    half = acc.shape[0]
    acc = add_low(acc, got)
    rows = half // 4
    own, by_x, by_near = acc[:rows], acc[rows : 2 * rows], acc[2 * rows : 3 * rows]
    first, second = acc[3 * rows : 3 * rows + rows // 2], acc[3 * rows + rows // 2 :]
    got_near = bit_x.swap(first, what)
    got_x = near.swap(second, what)
    by_near = jnp.concatenate([add_low(by_near[: rows // 2], got_near), by_near[rows // 2 :]], 0)
    by_x = jnp.concatenate([by_x[: rows // 2], add_low(by_x[rows // 2 :], got_x)], 0)
    return (add_low(own, bit_x.swap(by_x, what)), near.swap(by_near, what)), by_x


def absolute(blocks, index, bits):
    def one(j):
        other = index ^ j
        slot = sum(((other >> b.bit) & 1) << i for i, b in enumerate(bits))
        return lax.dynamic_index_in_dim(blocks, slot, 0, False)

    return jnp.stack([one(j) for j in range(blocks.shape[0])])


def relative(blocks, index, bits):
    def one(r):
        code = sum(((r >> i) & 1) << b.bit for i, b in enumerate(bits))
        return lax.dynamic_index_in_dim(blocks, index ^ code, 0, False)

    return jnp.stack([one(r) for r in range(blocks.shape[0])])


def shards(
    dp,
    ctx,
    tokens,
    cotangent,
    attn_gain,
    query_weight,
    key_weight,
    value_weight,
    output_weight,
    mlp_gain,
    gate_weight,
    up_weight,
    down_weight,
):
    seqs, seq_dev, width = tokens.shape
    rows = seqs * seq_dev
    depth = query_weight.shape[0]
    c_index = lax.axis_index("ctx")

    bit_x, bit_core = Bit("dp", 1, dp), Bit("dp", 0, dp)
    ctx_bits = [Bit("ctx", b, ctx) for b in reversed(range(ctx.bit_length() - 1))]
    near = ctx_bits[-1]
    far = [b for b in ctx_bits if b is not near]
    dp_bits = [bit_x, bit_core]
    names = dp_bits + ctx_bits
    attn_order = Order(names, list(reversed(ctx_bits)) + dp_bits, ctx_bits, depth)
    mlp_order = Order(names, far + dp_bits + [near], [], depth)
    x = tokens.reshape(rows, width)
    cot = cotangent.reshape(rows, width)
    gain_one = attn_gain.astype(F32)[:, None]
    gain_two = mlp_gain.astype(F32)[:, None]

    team_groups = []
    for c in range(ctx):
        if not (c >> near.bit) & 1:
            team_groups.append([d * ctx + (c | (n << near.bit)) for d in range(dp) for n in range(2)])
    team = 2 * dp

    def mlp_trade(parts):
        return lax.all_to_all(
            parts, ("dp", "ctx"), 0, 0, axis_index_groups=team_groups, tiled=True
        )

    def mlp_slices(weights, gain, *marks):
        kinds = len(weights)
        parts = after(mlp_trade(pack(weights, gain, team)), *marks)
        shape = (parts.shape[2], team * depth)
        return run(functools.partial(columns_kernel, kinds), [parts], [shape_of(shape, BF)] * kinds)

    def mlp_rows(sums):
        kinds = sum(t.shape[0] for t in sums) // units
        shape = (team, kinds * depth, units)
        return mlp_trade(run(functools.partial(rows_kernel, depth), sums, [shape_of(shape, BF)])[0])

    far_groups = []
    for n in range(2):
        far_groups.append([c for c in range(ctx) if (c >> near.bit) & 1 == n])
    pieces = ctx // 2

    def far_gather(own):
        return lax.all_gather(own, "ctx", axis=0, tiled=True, axis_index_groups=far_groups)

    def far_reduce(terms):
        return lax.psum_scatter(
            terms, "ctx", scatter_dimension=0, tiled=True, axis_index_groups=far_groups
        )

    qkv_cols = HEAD_COLS + 2 * HEAD_DIM
    me = lax.axis_index("dp").astype(jnp.int32).reshape(1)
    slices = run(
        functools.partial(pack_qkv_kernel, dp),
        [me, query_weight, key_weight, value_weight],
        [shape_of((dp, depth, qkv_cols), BF)],
        [SMEM] + [pl.BlockSpec(memory_space=pltpu.VMEM)] * 3,
    )[0]
    out_acc = [output_weight]
    for bit in ctx_bits[:-1]:
        out_acc.append(jnp.concatenate([out_acc[-1], bit.swap(out_acc[-1], "out")], 0))
    slices = [slices[0]] + [swap_difference(slices[r], "dp", dp, r, "slice") for r in range(1, dp)]
    own = run(
        functools.partial(place_kernel, dp),
        [me, after(slices[0], out_acc[1])] + slices[1:],
        [shape_of((dp, depth, qkv_cols), BF)],
        [SMEM] + [pl.BlockSpec(memory_space=pltpu.VMEM)] * dp,
    )[0].reshape(dp * depth, qkv_cols)
    halves = [own]
    for i, bit in enumerate(ctx_bits[:-1]):
        sent = halves[-1] if i == 0 else after(halves[-1], out_acc[i + 1])
        halves.append(jnp.concatenate([sent, bit.swap(sent, "qkv")], 0))
    qkv = [halves[-1], ctx_bits[-1].swap(halves[-1], "qkv")]
    out_rel = after(out_acc[-1], qkv[1])
    out_rel = jnp.concatenate([out_rel, ctx_bits[-1].swap(out_rel, "out")], 0)
    out_full = absolute(out_rel.reshape(ctx, depth, width), c_index, ctx_bits)
    out_full = out_full.reshape(ctx * depth, width)

    gate_own, up_own = mlp_slices([after(gate_weight, own), up_weight], gain_two, halves[-1])
    gain_all = jnp.broadcast_to(after(attn_gain, gate_own)[None], (dp * ctx, depth))
    gain_all = lax.all_to_all(gain_all, ("dp", "ctx"), 0, 0, tiled=True)
    gain_all = gain_all.reshape(1, width).astype(F32)
    a1_half = gather_rows(norm_to(attn_order, x, gain_all), dp_bits[:1], "a1")
    a1 = gather_rows(a1_half, dp_bits[1:], "a1")
    gate = far_gather(gate_own)
    (down_own,) = mlp_slices([after(down_weight.T, gain_all)], None)
    units = down_own.shape[0]

    places = jnp.arange(seq_dev, dtype=jnp.int32)
    half_dim = HEAD_DIM // 2
    freqs = rope_base ** (-(jnp.arange(half_dim, dtype=F32) * 2.0) / HEAD_DIM)
    angles = (c_index * seq_dev + places).astype(F32)[:, None] * freqs[None, :]
    cosine, sine = jnp.cos(angles), jnp.sin(angles)
    cosine = jnp.concatenate([cosine, cosine] * (GROUPS + 1) + [jnp.ones((seq_dev, HEAD_DIM), F32)], -1)
    sine = jnp.concatenate([-sine, sine] * (GROUPS + 1) + [jnp.zeros((seq_dev, HEAD_DIM), F32)], -1)
    rel = jnp.arange(ctx, dtype=jnp.int32)
    others = sum(((rel >> i) & 1) << b.bit for i, b in enumerate(ctx_bits)) ^ c_index
    key_places = (((others - c_index) * seq_dev)[:, None] + places[None, :]).reshape(1, -1)

    queries, kv_own = project(a1, cosine, sine, qkv)
    all_seqs = dp * seqs
    kv = kv_own
    for i, bit in enumerate(ctx_bits):
        if i == 1:
            kv = after(kv, down_own)
        if i == len(ctx_bits) - 2:
            up = far_gather(after(up_own, kv))
            down = far_gather(after(down_own, kv))
        kv = jnp.concatenate([kv, bit.swap(kv, "kv")], 0)
    kv = kv.reshape(ctx, all_seqs, seq_dev, 2 * HEAD_DIM)
    heads = attend(queries, kv, key_places, seq_dev)
    branch = dot(heads, out_full).astype(BF)
    branch = reduce_rows(branch, dp_bits, "branch")[-1]
    middle, a2 = middle_to(mlp_order, x, *branch)

    gb = gather_team(order_to(mlp_order, after(cot, middle)), bit_x, near, bit_core, "gb", [])
    a2 = gather_team(a2, bit_x, near, bit_core, "a2", [])
    block = min(256, a2[0].shape[0])
    hidden, one, two = gate_up(a2, gate, up, units, block)
    down_terms = weight_grad(hidden, gb, pieces)
    down_back = far_reduce(down_terms)
    dboth, da2 = hidden_back((after(gb[0], down_terms), gb[1]), one, two, down, gate, up, block)
    half = da2.shape[0] // 2
    da2_got = bit_core.swap(da2[half:], "da2")
    da2_two, da2_mark = reduce_four(da2[:half], da2_got, bit_x, near, "da2")
    down_out = result_rows(after(hidden, da2), down, width, block)
    result_got = bit_core.swap(after(down_out[half:], da2_mark), "result")
    both_terms = weight_grad(dboth, (after(a2[0], da2_mark), a2[1]), pieces)
    both_back = far_reduce(both_terms)
    grad_middle, db = norm_back(mlp_order, middle, after(cot, both_terms, result_got), *da2_two, low=True)
    grad_branch = gather_rows(db, dp_bits, "db")
    result_two, result_mark = reduce_four(
        down_out[:half], after(result_got, db), bit_x, near, "result"
    )
    result = result_of(mlp_order, middle, *result_two)

    grad_heads = dot_nt(grad_branch, out_full)
    dq, dkv = attend_back(
        queries, kv, after(key_places, result_mark), grad_heads, cosine, sine, seq_dev
    )

    class Sum:
        def __init__(self, terms, what):
            self.terms, self.what, self.bits = terms, what, list(reversed(ctx_bits))

        def step(self, *marks):
            half = self.terms.shape[0] // 2
            sent = after(self.terms[half:], *marks) if marks else self.terms[half:]
            self.pair = self.terms[:half], self.bits.pop(0).swap(sent, self.what)
            self.terms = add_low(*self.pair)
            return self.pair[1]

        def finish(self, *marks):
            while self.bits:
                self.step(*marks)
            return self.pair

    dkv_sum = Sum(dkv.reshape(-1, 2 * HEAD_DIM), "dkv")
    dkv_first = dkv_sum.step()
    dq_sum = Sum(dot_tn(a1, after(dq, dkv_first)).astype(BF), "dq_w")
    dq_first = dq_sum.step()
    dkv_sum.step(down_back, *result_two)
    dkv_two = dkv_sum.finish()
    dkv_low = run(
        functools.partial(turn_back_kernel, all_seqs),
        [after(dkv_two[0], dq_first), dkv_two[1]] + [cosine, sine],
        [shape_of((dp * rows, 2 * HEAD_DIM), BF)],
    )[0]
    kv_sum = Sum(dot_tn(a1, dkv_low).astype(BF), "dkv_w")
    kv_first = kv_sum.step()
    da1 = wide(dot_nt, jnp.concatenate([dq, dkv_low], -1), qkv, width, min(256, dp * rows))
    da1_steps = reduce_rows(da1, dp_bits, "da1")
    da1_two = da1_steps[-1]
    (grad_tokens,) = norm_back(attn_order, x, grad_middle, *da1_two, gain_all)
    dq_second = dq_sum.step()
    kv_second = kv_sum.step(dq_second, da1_steps[0][1])
    out_total = dot_tn(heads, grad_branch).astype(BF).reshape(ctx, depth, width)
    out_total = relative(after(out_total, kv_first), c_index, ctx_bits).reshape(ctx * depth, width)
    out_sum = Sum(out_total, "dout_w")
    out_first = out_sum.step()
    all_back = mlp_rows([after(both_back, kv_first), down_back])
    dq_two = dq_sum.finish()
    kv_two = kv_sum.finish(dq_two[1], *da1_two)
    out_second = out_sum.step(kv_second)
    out_two = out_sum.finish()
    output_grad = out_two[0].astype(F32) + out_two[1].astype(F32)
    qkv_total = jnp.concatenate([add_low(*dq_two), add_low(*kv_two)], -1).reshape(dp, depth, qkv_cols)
    qkv_back = lax.all_to_all(after(qkv_total, all_back), "dp", 0, 0, tiled=True)

    wide_shape = shape_of(gate_weight.shape, F32)
    gate_grad, up_grad, down_grad, mlp_sum = run(
        unpack_kernel,
        [all_back, gate_weight, up_weight, gain_two],
        [wide_shape, wide_shape, wide_shape, shape_of((depth, 1), F32)],
    )
    down_grad = down_grad.T
    query_grad, key_grad, value_grad, attn_sum = run(
        functools.partial(unpack_qkv_kernel, dp),
        [query_weight, key_weight, value_weight, gain_one, qkv_back],
        [shape_of(w.shape, F32) for w in (query_weight, key_weight, value_weight, gain_one)],
    )
    return (
        result.reshape(seqs, seq_dev, width),
        grad_tokens.reshape(seqs, seq_dev, width),
        attn_sum[:, 0],
        query_grad,
        key_grad,
        value_grad,
        output_grad,
        mlp_sum[:, 0],
        gate_grad,
        up_grad,
        down_grad,
    )


def solution(mesh):
    dp, ctx = mesh.shape["dp"], mesh.shape["ctx"]

    def local(*args):
        return shards(dp, ctx, *args)

    weight = P(("dp", "ctx"), None)
    flat = P(("dp", "ctx"))
    acts = P("dp", "ctx", None)
    down = P(None, ("dp", "ctx"))
    return jax.shard_map(
        local,
        mesh=mesh,
        in_specs=(acts, acts, flat, weight, weight, weight, weight, flat, weight, weight, down),
        out_specs=(acts, acts, flat, weight, weight, weight, weight, flat, weight, weight, down),
        check_vma=False,
    )
```
